1024 devices in a mesh: dp: 256 (over y, x_lo, z), tower: 4 (over x_hi, core).
Axes of the slice: x: 4 (x_hi: 2, x_lo: 2; x = x_hi * 2 + x_lo), y: 4, z: 32, core: 2. Of those that a mesh axis runs over, the one named last changes fastest.
Arguments:
- image_feats: bfloat16 [32768, 1152], P('dp'), may hold values from -6 to 6
- text_feats: bfloat16 [32768, 1152], P('dp'), may hold values from -6 to 6
- image_proj: bfloat16 [1152, 1152], P(None, 'tower'), may hold values from -0.1875 to 0.1875
- text_proj: bfloat16 [1152, 1152], P(None, 'tower'), may hold values from -0.1875 to 0.1875
- logit_scale: float32 [1], replicated, may hold values from 2 to 5
- logit_bias: float32 [1], replicated, may hold values from -3 to -1
Outputs:
- pair_loss: float32 [32768], P('dp')
- image_grad: float32 [4, 331776], P('tower', 'dp')
- text_grad: float32 [4, 331776], P('tower', 'dp')
The draws below stay inside these ranges and needn't reach their ends.
All inputs are finite; a program needn't handle non-finite values.
Results may differ from the reference program's by a relative error of at most 0.0043.
Values may be sent and summed in bfloat16 or wider, within the bound.
No kernel may reach another device: no remote copies, remote signals or barrier semaphores. Data moves between devices by JAX's collectives and lax.ppermute only.
A program may use at most 32 MiB of HBM per device.

```python
import jax
import jax.numpy as jnp
from jax import lax

D = 1152
B_DEV = 128
CYCLE = 4
PAIRS = 32768
N_DP = 256
N_TOWER = 4


def level_of(stream_key, shape, split, low, largest):
    loudness, own = 1.0, jax.random.fold_in(stream_key, 6)
    for position, shards_of in split:
        draws = jnp.exp(jax.random.uniform(jax.random.fold_in(own, position), (shards_of,), jnp.float32, low / len(split), largest / len(split)))
        loudness = loudness * jnp.repeat(draws, shape[position] // shards_of).reshape([-1 if axis == position else 1 for axis in range(len(shape))])
    return loudness


def bell_draw(own_key, shape, scale, reach, shards=(), held_as=jnp.bfloat16):
    loudness = level_of(own_key, shape, shards, -0.22, 0.18) if shards else 1.0
    array = jax.random.normal(own_key, shape, jnp.float32) * scale * loudness
    return jnp.minimum(jnp.maximum(array, -reach), reach).astype(held_as)


def setup_inputs(seed: int = 0) -> dict:
    key_of = jax.random.split(jax.random.key(seed), 7)
    return {
        "image_feats": bell_draw(key_of[0], (PAIRS, D), 1.0, 6.0, ((0, 256),)),
        "text_feats": bell_draw(key_of[1], (PAIRS, D), 1.0, 6.0, ((0, 256),)),
        "image_proj": bell_draw(key_of[2], (D, D), D ** -0.5, 0.1875, ((1, 4),)),
        "text_proj": bell_draw(key_of[3], (D, D), D ** -0.5, 0.1875, ((1, 4),)),
        "logit_scale": jnp.clip(jax.random.uniform(key_of[4], (1,), jnp.float32, 2.0, 5.0), 2.0, 5.0),
        "logit_bias": jnp.clip(jax.random.uniform(key_of[5], (1,), jnp.float32, -3.0, -1.0), -3.0, -1.0),
    }


def unit_rows(z):
    norm = jnp.sqrt(lax.optimization_barrier(jnp.sum(z * z, axis=-1, keepdims=True)) + 1e-06)
    return (z / norm, norm)

def reference(image_feats, text_feats, image_proj, text_proj, logit_scale, logit_bias):
    zi = jnp.dot(image_feats, image_proj, preferred_element_type=jnp.float32)
    zt = jnp.dot(text_feats, text_proj, preferred_element_type=jnp.float32)
    ui, ni = unit_rows(zi)
    ut, nt = unit_rows(zt)
    ub = ui.astype(jnp.bfloat16).reshape(N_DP, B_DEV, D).astype(jnp.float32)
    vb = ut.astype(jnp.bfloat16).reshape(N_DP, B_DEV, D).astype(jnp.float32)
    scale = logit_scale[0]
    bias = logit_bias[0]
    eye = jnp.eye(B_DEV, dtype=jnp.float32)
    loss = jnp.zeros((N_DP, B_DEV), jnp.float32)
    du = jnp.zeros((N_DP, B_DEV, D), jnp.float32)
    dv = jnp.zeros((N_DP, B_DEV, D), jnp.float32)
    for k in range(CYCLE + 1):
        block = jnp.roll(vb, k, axis=0)
        label = eye if k == 0 else jnp.zeros_like(eye)
        s = scale * jnp.einsum('dbe,dce->dbc', ub, block) + bias
        loss = loss + lax.optimization_barrier(jnp.sum(jax.nn.softplus((1.0 - 2.0 * label) * s), axis=-1))
        g = (jax.nn.sigmoid(s) - label).astype(jnp.bfloat16).astype(jnp.float32)
        du = du + jnp.einsum('dbc,dce->dbe', g, block)
        part = jnp.einsum('dbc,dbe->dce', g, ub)
        dv = dv + jnp.roll(part, -k, axis=0)
    du = scale * du.reshape(N_DP * B_DEV, D)
    dv = scale * dv.reshape(N_DP * B_DEV, D)
    dzi = ((du - ui * lax.optimization_barrier(jnp.sum(ui * du, axis=-1, keepdims=True))) / ni).astype(jnp.bfloat16)
    dzt = ((dv - ut * lax.optimization_barrier(jnp.sum(ut * dv, axis=-1, keepdims=True))) / nt).astype(jnp.bfloat16)
    grad_i = jnp.dot(image_feats.T, dzi, preferred_element_type=jnp.float32)
    grad_t = jnp.dot(text_feats.T, dzt, preferred_element_type=jnp.float32)
    width = D // N_TOWER
    image_grad = grad_i.reshape(D, N_TOWER, width).transpose(1, 0, 2).reshape(N_TOWER, D * width)
    text_grad = grad_t.reshape(D, N_TOWER, width).transpose(1, 0, 2).reshape(N_TOWER, D * width)
    return (loss.reshape(N_DP * B_DEV), image_grad, text_grad)
```

```python
import jax
import jax.numpy as jnp
from jax import lax
from jax.sharding import PartitionSpec as P

RING = 32


def across(left, right):
    return lax.dot_general(
        left, right, (((1,), (1,)), ((), ())), preferred_element_type=jnp.float32
    )


def down(left, right):
    return lax.dot_general(
        left, right, (((0,), (0,)), ((), ())), preferred_element_type=jnp.float32
    )


def times(left, right):
    return jnp.dot(left, right, preferred_element_type=jnp.float32)


def rounded(x):
    return lax.reduce_precision(x, 8, 7)


def shifted(block, distances):
    dp, tower = lax.axis_size("dp"), lax.axis_size("tower")
    route = [
        (i * tower + t, ((i + distances[t % 2]) % dp) * tower + t)
        for i in range(dp)
        for t in range(tower)
    ]
    return lax.ppermute(block, ("dp", "tower"), route)


def shards(image_feats, text_feats, image_proj, text_proj, logit_scale, logit_bias):
    bf16, f32 = jnp.bfloat16, jnp.float32
    rows = image_feats.shape[0]
    width = image_proj.shape[1]
    dp, tower = lax.axis_size("dp"), lax.axis_size("tower")
    planes = dp // RING
    scale, bias = logit_scale[0], logit_bias[0]
    to_core = [(t, t ^ 1) for t in range(tower)]
    to_chip = [(t, t ^ 2) for t in range(tower)]
    core0 = (lax.axis_index("tower") % 2 == 0).astype(f32)

    zi = times(image_feats, image_proj)
    zt = times(text_feats, text_proj)
    mine = jnp.concatenate((zi, zt), axis=0).astype(bf16)
    other = lax.ppermute(mine, "tower", to_core)
    half = jnp.concatenate((mine, other), axis=1)
    i0, t0 = half[:rows], half[rows:]
    t1 = shifted(t0, (1, 2))
    i1 = shifted(i0, (-1, -2))
    t2 = shifted(t1, (2, 2))
    i2 = shifted(i1, (-2, -2))

    parts = [across(i0, t0), across(i0, t1), across(i0, t2), across(t0, i1), across(t0, i2)]
    squares = [
        jnp.sum(jnp.square(b.astype(f32)), axis=-1)[None] for b in (i0, t0, i1, i2, t1, t2)
    ]
    squares = jnp.concatenate(squares, axis=0)
    coarse = rounded(squares)
    payload = jnp.concatenate(
        [rounded(p) for p in parts]
        + [coarse, rounded(squares - coarse), jnp.zeros((4, rows), f32)],
        axis=0,
    ).astype(bf16)
    peer = lax.ppermute(payload, "tower", to_chip).astype(f32)
    total = payload.astype(f32) + peer
    s0, s1, s2, r1, r2 = (total[j * rows : (j + 1) * rows] for j in range(5))
    sq = total[5 * rows : 5 * rows + 6] + total[5 * rows + 6 : 5 * rows + 12]
    inv = lax.rsqrt(sq + 1e-06)
    ni, nt = inv[0], inv[1]

    def pair(raw, row_inv, col_inv):
        return scale * (raw * row_inv[:, None] * col_inv[None, :])

    eye = jnp.eye(rows, dtype=f32)
    c0, c1, c2 = pair(s0, ni, nt), pair(s1, ni, inv[4]), pair(s2, ni, inv[5])
    e1, e2 = pair(r1, nt, inv[2]), pair(r2, nt, inv[3])
    loss0 = jnp.sum(jax.nn.softplus((1.0 - 2.0 * eye) * (c0 + bias)), axis=-1)
    loss = (
        core0 * loss0
        + jnp.sum(jax.nn.softplus(c1 + bias), axis=-1)
        + jnp.sum(jax.nn.softplus(c2 + bias), axis=-1)
    )
    g0 = jax.nn.sigmoid(c0 + bias) - eye
    g1, g2 = jax.nn.sigmoid(c1 + bias), jax.nn.sigmoid(c2 + bias)
    h1, h2 = jax.nn.sigmoid(e1 + bias), jax.nn.sigmoid(e2 + bias)
    along_i = jnp.sum(g1 * c1 + g2 * c2, axis=-1)
    along_t = jnp.sum(h1 * e1 + h2 * e2, axis=-1)
    du = times((g1 * inv[4]).astype(bf16), t1) + times((g2 * inv[5]).astype(bf16), t2)
    dv = times((h1 * inv[2]).astype(bf16), i1) + times((h2 * inv[3]).astype(bf16), i2)
    du0 = times((g0 * nt[None, :]).astype(bf16), t0[:, :width])
    dv0 = down((g0 * ni[:, None]).astype(bf16), i0[:, :width])
    lines = jnp.stack((along_i, along_t, loss), axis=0)
    lines = jnp.pad(lines, ((0, 5), (0, width - rows)))
    sums = jnp.concatenate((du[:, width:], dv[:, width:], lines), axis=0)
    got = lax.ppermute(sums, "tower", to_core)
    lines = lines[:3, :rows] + got[2 * rows : 2 * rows + 3, :rows]
    along_i = lines[0] + jnp.sum(g0 * c0, axis=1)
    along_t = lines[1] + jnp.sum(g0 * c0, axis=0)
    loss = lines[2]
    du = scale * (du[:, :width] + got[:rows] + du0)
    dv = scale * (dv[:, :width] + got[rows : 2 * rows] + dv0)
    dzi = ((du - zi * (ni * along_i)[:, None]) * ni[:, None]).astype(bf16)
    dzt = ((dv - zt * (nt * along_t)[:, None]) * nt[:, None]).astype(bf16)

    depth = image_feats.shape[1]
    grads = jnp.concatenate((down(image_feats, dzi), down(text_feats, dzt)), axis=1)
    grads = grads.astype(bf16).reshape(planes, depth // planes, 2 * width)
    groups = [[g * RING + z for g in range(planes)] for z in range(RING)]
    grads = lax.all_to_all(grads, "dp", 0, 0, axis_index_groups=groups, tiled=True)
    grads = jnp.sum(grads.astype(f32), axis=0).astype(bf16)
    gi = grads[:, :width].reshape(RING, -1)
    gt = grads[:, width:].reshape(RING, -1)
    share = gi.shape[1]
    lanes = 128
    filled = -(-2 * share // lanes)
    flat = jnp.concatenate((gi, gt), axis=1)
    flat = jnp.pad(flat, ((0, 0), (0, filled * lanes - 2 * share)))
    flat = flat.reshape(RING, filled, lanes)
    groups = [[g * RING + z for z in range(RING)] for g in range(planes)]
    flat = lax.all_to_all(flat, "dp", 0, 0, axis_index_groups=groups, tiled=True)
    flat = jnp.sum(flat.astype(f32), axis=0).reshape(1, -1)
    return (loss, flat[:, :share], flat[:, share : 2 * share])


def solution(mesh):
    in_specs = (P("dp", None), P("dp", None), P(None, "tower"), P(None, "tower"), P(), P())
    out_specs = (P("dp"), P("tower", "dp"), P("tower", "dp"))
    return jax.shard_map(shards, mesh=mesh, in_specs=in_specs, out_specs=out_specs, check_vma=False)
```

```python
import jax
import jax.numpy as jnp
from jax import lax
from jax.sharding import PartitionSpec as P

RING = 32
LANES = 128


def across(left, right):
    return lax.dot_general(
        left, right, (((1,), (1,)), ((), ())), preferred_element_type=jnp.float32
    )


def down(left, right):
    return lax.dot_general(
        left, right, (((0,), (0,)), ((), ())), preferred_element_type=jnp.float32
    )


def times(left, right):
    return jnp.dot(left, right, preferred_element_type=jnp.float32)


def two_terms(x):
    high = rounded(x)
    return high.astype(jnp.bfloat16), (x - high).astype(jnp.bfloat16)


def fine(weights, block):
    return times(jnp.concatenate(two_terms(weights), axis=1), jnp.concatenate((block, block), axis=0))


def fine_down(feats, grad):
    return down(jnp.concatenate((feats, feats), axis=0), jnp.concatenate(two_terms(grad), axis=0))


def laned(x):
    rows, cols = x.shape[1:]
    whole = cols // LANES * LANES
    blocks = [x[:, :, j : j + LANES] for j in range(0, whole, LANES)]
    rest = x[:, :, whole:]
    blocks.append(jnp.concatenate((rest[:, : rows // 2], rest[:, rows // 2 :]), axis=2))
    return jnp.concatenate(blocks, axis=1)


def unlaned(x, rows, cols):
    whole = cols // LANES
    blocks = [x[j * rows : (j + 1) * rows] for j in range(whole)]
    rest = x[whole * rows :]
    blocks.append(jnp.concatenate((rest[:, : LANES // 2], rest[:, LANES // 2 :]), axis=0))
    return jnp.concatenate(blocks, axis=1)


def swapped(x, groups, spare):
    f16, f32 = jnp.float16, jnp.float32
    top = jnp.max(jnp.abs(x))
    power = jnp.floor(jnp.log2(jnp.where(top > 0, top, 1.0))) - 13.0
    power = jnp.maximum(power, -120.0)
    x = x * jnp.exp2(-power)
    if spare:
        last = lax.broadcasted_iota(jnp.int32, x.shape, 1) == x.shape[1] - 1
        last &= lax.broadcasted_iota(jnp.int32, x.shape, 2) == LANES - 1
        x = jnp.where(last, power, x)
    else:
        x = jnp.concatenate((x, jnp.full((x.shape[0], 8, LANES), power)), axis=1)
    sent = x.astype(f16)
    got = lax.all_to_all(sent, "dp", 0, 0, axis_index_groups=groups, tiled=True).astype(f32)
    summed = jnp.sum(got * jnp.exp2(got[:, -1:, -1:]), axis=0)
    return summed if spare else summed[:-8]


def rounded(x):
    return lax.reduce_precision(x, 8, 7)


def shifted(block, distances):
    dp, tower = lax.axis_size("dp"), lax.axis_size("tower")
    route = [
        (i * tower + t, ((i + distances[t % 2]) % dp) * tower + t)
        for i in range(dp)
        for t in range(tower)
    ]
    return lax.ppermute(block, ("dp", "tower"), route)


def shards(image_feats, text_feats, image_proj, text_proj, logit_scale, logit_bias):
    bf16, f32 = jnp.bfloat16, jnp.float32
    rows = image_feats.shape[0]
    width = image_proj.shape[1]
    dp, tower = lax.axis_size("dp"), lax.axis_size("tower")
    planes = dp // RING
    scale, bias = logit_scale[0], logit_bias[0]
    to_core = [(t, t ^ 1) for t in range(tower)]
    to_chip = [(t, t ^ 2) for t in range(tower)]
    core0 = (lax.axis_index("tower") % 2 == 0).astype(f32)

    zi = times(image_feats, image_proj)
    zt = times(text_feats, text_proj)
    mine = jnp.concatenate((zi, zt), axis=0).astype(bf16)
    other = lax.ppermute(mine, "tower", to_core)
    half = jnp.concatenate((mine, other), axis=1)
    i0, t0 = half[:rows], half[rows:]
    t1 = shifted(t0, (1, 2))
    i1 = shifted(i0, (-1, -2))
    t2 = shifted(t1, (2, 2))
    i2 = shifted(i1, (-2, -2))

    parts = [across(i0, t0), across(i0, t1), across(i0, t2), across(t0, i1), across(t0, i2)]
    squares = [
        jnp.sum(jnp.square(b.astype(f32)), axis=-1)[None] for b in (i0, t0, i1, i2, t1, t2)
    ]
    squares = jnp.concatenate(squares, axis=0)
    coarse = rounded(squares)
    payload = jnp.concatenate(
        [rounded(p) for p in parts]
        + [coarse, rounded(squares - coarse), jnp.zeros((4, rows), f32)],
        axis=0,
    ).astype(bf16)
    peer = lax.ppermute(payload, "tower", to_chip).astype(f32)
    total = payload.astype(f32) + peer
    s0, s1, s2, r1, r2 = (total[j * rows : (j + 1) * rows] for j in range(5))
    sq = total[5 * rows : 5 * rows + 6] + total[5 * rows + 6 : 5 * rows + 12]
    inv = lax.rsqrt(sq + 1e-06)
    ni, nt = inv[0], inv[1]

    def pair(raw, row_inv, col_inv):
        return scale * (raw * row_inv[:, None] * col_inv[None, :])

    eye = jnp.eye(rows, dtype=f32)
    c0, c1, c2 = pair(s0, ni, nt), pair(s1, ni, inv[4]), pair(s2, ni, inv[5])
    e1, e2 = pair(r1, nt, inv[2]), pair(r2, nt, inv[3])
    loss0 = jnp.sum(jax.nn.softplus((1.0 - 2.0 * eye) * (c0 + bias)), axis=-1)
    loss = (
        core0 * loss0
        + jnp.sum(jax.nn.softplus(c1 + bias), axis=-1)
        + jnp.sum(jax.nn.softplus(c2 + bias), axis=-1)
    )
    g0 = jax.nn.sigmoid(c0 + bias) - eye
    g1, g2 = jax.nn.sigmoid(c1 + bias), jax.nn.sigmoid(c2 + bias)
    h1, h2 = jax.nn.sigmoid(e1 + bias), jax.nn.sigmoid(e2 + bias)
    along_i = jnp.sum(g1 * c1 + g2 * c2, axis=-1)
    along_t = jnp.sum(h1 * e1 + h2 * e2, axis=-1)
    du = fine(g1 * inv[4], t1) + fine(g2 * inv[5], t2)
    dv = fine(h1 * inv[2], i1) + fine(h2 * inv[3], i2)
    du0 = fine(g0 * nt[None, :], t0[:, :width])
    dv0 = fine((g0 * ni[:, None]).T, i0[:, :width])
    lines = jnp.stack((along_i, along_t, loss), axis=0)
    lines = jnp.pad(lines, ((0, 5), (0, width - rows)))
    sums = jnp.concatenate((du[:, width:], dv[:, width:], lines), axis=0)
    got = lax.ppermute(sums, "tower", to_core)
    lines = lines[:3, :rows] + got[2 * rows : 2 * rows + 3, :rows]
    along_i = lines[0] + jnp.sum(g0 * c0, axis=1)
    along_t = lines[1] + jnp.sum(g0 * c0, axis=0)
    loss = lines[2]
    du = scale * (du[:, :width] + got[:rows] + du0)
    dv = scale * (dv[:, :width] + got[rows : 2 * rows] + dv0)
    dzi = (du - zi * (ni * along_i)[:, None]) * ni[:, None]
    dzt = (dv - zt * (nt * along_t)[:, None]) * nt[:, None]

    depth = image_feats.shape[1]
    share = depth * width // dp
    grads = jnp.concatenate((fine_down(image_feats, dzi), fine_down(text_feats, dzt)), axis=1)
    grads = grads.reshape(planes, depth // planes, 2 * width)
    groups = [[g * RING + z for g in range(planes)] for z in range(RING)]
    grads = unlaned(swapped(laned(grads), groups, False), depth // planes, 2 * width)
    flat = jnp.concatenate(
        (grads[:, :width].reshape(RING, share), grads[:, width:].reshape(RING, share)), axis=1
    )
    filled = -(-2 * share // LANES)
    flat = jnp.pad(flat, ((0, 0), (0, filled * LANES - 2 * share)))
    groups = [[g * RING + z for z in range(RING)] for g in range(planes)]
    flat = swapped(flat.reshape(RING, filled, LANES), groups, True).reshape(1, -1)
    return (loss, flat[:, :share], flat[:, share : 2 * share])


def solution(mesh):
    in_specs = (P("dp", None), P("dp", None), P(None, "tower"), P(None, "tower"), P(), P())
    out_specs = (P("dp"), P("tower", "dp"), P("tower", "dp"))
    return jax.shard_map(shards, mesh=mesh, in_specs=in_specs, out_specs=out_specs, check_vma=False)
```

```python
import functools

import jax
import jax.numpy as jnp
from jax import lax
from jax.experimental import pallas as pl
from jax.experimental.pallas import tpu as pltpu
from jax.sharding import PartitionSpec as P

RING = 32
LANES = 128
BF16, F32 = jnp.bfloat16, jnp.float32
VMEM = pltpu.CompilerParams(vmem_limit_bytes=32 * 1024 * 1024)


def dot(left, right, over_left, over_right):
    return lax.dot_general(
        left, right, (((over_left,), (over_right,)), ((), ())), preferred_element_type=F32
    )


def two_terms(x):
    high = x.astype(BF16)
    return jnp.concatenate((high, (x - high.astype(F32)).astype(BF16)), axis=1)


def fine(block, weights):
    both = dot(block, two_terms(weights), 1, 0)
    return both[:, :LANES] + both[:, LANES:]


def shifted(block, distances):
    dp, tower = lax.axis_size("dp"), lax.axis_size("tower")
    route = [
        (i * tower + t, ((i + distances[t % 2]) % dp) * tower + t)
        for i in range(dp)
        for t in range(tower)
    ]
    return lax.ppermute(block, ("dp", "tower"), route)


def score_kernel(i0, t0, t1, t2, i1, i2, out):
    pairs = ((t0, i0), (t1, i0), (t2, i0), (i1, t0), (i2, t0))
    for j, (other, own) in enumerate(pairs):
        out[j * LANES : (j + 1) * LANES] = dot(other[...], own[...], 0, 0).astype(BF16)
    squares = [
        jnp.sum(jnp.square(b[...].astype(F32)), axis=0, keepdims=True)
        for b in (i0, t0, t1, t2, i1, i2)
    ]
    squares = jnp.concatenate(squares + [jnp.zeros((2, LANES), F32)], axis=0)
    high = squares.astype(BF16).astype(F32)
    low = (squares - high).astype(BF16).astype(F32)
    out[5 * LANES :] = jnp.concatenate((high, low), axis=0).astype(BF16)


def weight_kernel(numbers, mine, peer, own, t1, t2, i1, i2, send, keep):
    scale, bias, core0 = numbers[0], numbers[1], numbers[2]
    width = own.shape[0] // 2
    rows = 5 * LANES

    def total(start, size):
        a = mine[start : start + size].astype(F32)
        return a + peer[start : start + size].astype(F32)

    squares = total(rows, 16)
    inv = lax.rsqrt(squares[:8] + squares[8:] + 1e-06)
    down = inv.T

    def weigh(j, across, along):
        c = scale * (total(j * LANES, LANES) * across * along)
        s = c + bias
        e = jnp.exp(-jnp.abs(s))
        return c, s, jnp.log1p(e), jnp.where(s >= 0, 1.0, e) / (1.0 + e)

    ni, nt = inv[0:1], inv[1:2]
    eye = (
        lax.broadcasted_iota(jnp.int32, (LANES, LANES), 0)
        == lax.broadcasted_iota(jnp.int32, (LANES, LANES), 1)
    ).astype(F32)
    c, s, tail, g = weigh(0, ni, down[:, 1:2])
    loss = core0 * jnp.sum(jnp.maximum((1.0 - 2.0 * eye) * s, 0.0) + tail, axis=0, keepdims=True)
    g = g - eye
    gc = g * c
    along_i0 = jnp.sum(gc, axis=0, keepdims=True)
    along_t0 = jnp.sum(gc.T, axis=0, keepdims=True)
    du0 = fine(own[width:], g * down[:, 1:2])
    dv0 = fine(own[:width], (g * ni).T)

    along_i, along_t = jnp.zeros_like(ni), jnp.zeros_like(ni)
    du = dv = None
    for j, block in ((1, t1), (2, t2)):
        col = down[:, j + 1 : j + 2]
        c, s, tail, g = weigh(j, ni, col)
        loss += jnp.sum(jnp.maximum(s, 0.0) + tail, axis=0, keepdims=True)
        along_i += jnp.sum(g * c, axis=0, keepdims=True)
        term = fine(block[...], g * col)
        du = term if du is None else du + term
    for j, block in ((3, i1), (4, i2)):
        col = down[:, j + 1 : j + 2]
        c, s, tail, g = weigh(j, nt, col)
        along_t += jnp.sum(g * c, axis=0, keepdims=True)
        term = fine(block[...], g * col)
        dv = term if dv is None else dv + term
    zero = jnp.zeros_like(ni)
    send[:width] = du[width:]
    send[width : 2 * width] = dv[width:]
    send[2 * width :] = jnp.concatenate((along_i, along_t, loss) + (zero,) * 5, axis=0)
    keep[:width] = du[:width] + du0
    keep[width : 2 * width] = dv[:width] + dv0
    keep[2 * width :] = jnp.concatenate(
        (along_i + along_i0, along_t + along_t0, loss, ni, nt) + (zero,) * 3, axis=0
    )


def gradient_kernel(planes, numbers, keep, got, z, xi, xt, out, loss):
    scale = numbers[0]
    width = z.shape[0] // 2
    lines, more = keep[2 * width :], got[2 * width :]
    loss[...] = jnp.broadcast_to(lines[2:3] + more[2:3], loss.shape)
    grads = []
    for side in range(2):
        part = slice(side * width, (side + 1) * width)
        d = scale * (keep[part] + got[part])
        along = lines[side : side + 1] + more[side : side + 1]
        n = lines[3 + side : 4 + side]
        grads.append(two_terms((d - z[part] * (n * along)) * n))
    block = xi.shape[0] // planes
    whole = width // LANES * LANES
    rest = width - whole
    depth = grads[0].shape[1]
    fold = -(-block // 32) * 16
    folded = []
    for place in range(4):
        pieces = []
        if place:
            pieces.append(jnp.zeros((place * rest, depth), BF16))
        pieces.append(grads[place % 2][whole:])
        if place < 3:
            pieces.append(jnp.zeros(((3 - place) * rest, depth), BF16))
        folded.append(jnp.concatenate(pieces, axis=0))
    for p in range(planes):
        last = None
        for side, x in enumerate((xi, xt)):
            feats = x[p * block : (p + 1) * block]
            feats = jnp.concatenate((feats, feats), axis=1)
            main = dot(feats, grads[side][:whole], 1, 1).astype(BF16)
            for j in range(whole // LANES):
                at = (side * (whole // LANES) + j) * block
                out[p, at : at + block] = main[:, j * LANES : (j + 1) * LANES]
            for half in range(2):
                rows = feats[:fold] if half == 0 else feats[block - fold :]
                term = dot(rows, folded[2 * half + side], 1, 1)
                last = term if last is None else last + term
        out[p, 2 * whole // LANES * block :] = last.astype(BF16)


def unfolded(x, block, width):
    count = width // LANES
    rest = width - count * LANES
    last = x[2 * count * block :]
    fold = last.shape[0]
    sides = []
    for side in range(2):
        pieces = [x[(side * count + j) * block : (side * count + j + 1) * block] for j in range(count)]
        top = last[:, side * rest : (side + 1) * rest]
        low = last[2 * fold - block :, (2 + side) * rest : (3 + side) * rest]
        pieces.append(jnp.concatenate((top, low), axis=0))
        sides.append(jnp.concatenate(pieces, axis=1))
    return sides


def summed_over_ring(x):
    dp = lax.axis_size("dp")
    groups = [[g * RING + z for z in range(RING)] for g in range(dp // RING)]
    top = jnp.max(jnp.abs(x))
    power = jnp.floor(jnp.log2(jnp.where(top > 0, top, 1.0))) - 13.0
    power = jnp.maximum(power, -120.0)
    last = lax.broadcasted_iota(jnp.int32, x.shape, 1) == x.shape[1] - 1
    last &= lax.broadcasted_iota(jnp.int32, x.shape, 2) == LANES - 1
    sent = jnp.where(last, power, x * jnp.exp2(-power)).astype(jnp.float16)
    got = lax.all_to_all(sent, "dp", 0, 0, axis_index_groups=groups, tiled=True).astype(F32)
    return jnp.sum(got * jnp.exp2(got[:, -1:, -1:]), axis=0)


def shards(image_feats, text_feats, image_proj, text_proj, logit_scale, logit_bias):
    rows, depth = image_feats.shape
    width = image_proj.shape[1]
    dp, tower = lax.axis_size("dp"), lax.axis_size("tower")
    planes = dp // RING
    to_core = [(t, t ^ 1) for t in range(tower)]
    to_chip = [(t, t ^ 2) for t in range(tower)]
    core0 = (lax.axis_index("tower") % 2 == 0).astype(F32)
    numbers = jnp.concatenate((logit_scale, logit_bias, core0[None]))
    scalars = pl.BlockSpec(memory_space=pltpu.SMEM)
    array = pl.BlockSpec(memory_space=pltpu.VMEM)

    zi = jnp.dot(image_feats, image_proj, preferred_element_type=F32)
    zt = jnp.dot(text_feats, text_proj, preferred_element_type=F32)
    z = jnp.concatenate((zi.T, zt.T), axis=0)
    own = z.astype(BF16)
    other = lax.ppermute(own, "tower", to_core)
    i0 = jnp.concatenate((own[:width], other[:width]), axis=0)
    t0 = jnp.concatenate((own[width:], other[width:]), axis=0)
    t1 = shifted(t0, (1, 2))
    i1 = shifted(i0, (-1, -2))
    t2 = shifted(t1, (2, 2))
    i2 = shifted(i1, (-2, -2))
    scores = pl.pallas_call(
        score_kernel,
        out_shape=jax.ShapeDtypeStruct((5 * rows + 16, rows), BF16),
        in_specs=[array] * 6,
        out_specs=array,
        compiler_params=VMEM,
        name="scores",
    )(i0, t0, t1, t2, i1, i2)
    peer = lax.ppermute(scores, "tower", to_chip)
    sums = jax.ShapeDtypeStruct((2 * width + 8, rows), F32)
    send, keep = pl.pallas_call(
        weight_kernel,
        out_shape=(sums, sums),
        in_specs=[scalars] + [array] * 7,
        out_specs=(array, array),
        compiler_params=VMEM,
        name="weights",
    )(numbers, scores, peer, own, t1, t2, i1, i2)
    got = lax.ppermute(send, "tower", to_core)
    block = depth // planes
    payload = 2 * (width // LANES) * block + -(-block // 32) * 16
    grads, loss = pl.pallas_call(
        functools.partial(gradient_kernel, planes),
        out_shape=(
            jax.ShapeDtypeStruct((planes, payload, LANES), BF16),
            jax.ShapeDtypeStruct((8, rows), F32),
        ),
        in_specs=[scalars] + [array] * 5,
        out_specs=(array, array),
        compiler_params=VMEM,
        name="gradients",
    )(numbers, keep, got, z, image_feats.T, text_feats.T)

    groups = [[g * RING + z for g in range(planes)] for z in range(RING)]
    grads = lax.all_to_all(grads, "dp", 0, 0, axis_index_groups=groups, tiled=True)
    gi, gt = unfolded(jnp.sum(grads.astype(F32), axis=0), block, width)
    share = depth * width // dp
    flat = jnp.concatenate((gi.reshape(RING, share), gt.reshape(RING, share)), axis=1)
    filled = -(-2 * share // LANES)
    flat = jnp.pad(flat, ((0, 0), (0, filled * LANES - 2 * share)))
    flat = summed_over_ring(flat.reshape(RING, filled, LANES)).reshape(1, -1)
    return (loss[0], flat[:, :share], flat[:, share : 2 * share])


def solution(mesh):
    in_specs = (P("dp", None), P("dp", None), P(None, "tower"), P(None, "tower"), P(), P())
    out_specs = (P("dp"), P("tower", "dp"), P("tower", "dp"))
    return jax.shard_map(shards, mesh=mesh, in_specs=in_specs, out_specs=out_specs, check_vma=False)
```

```python
import functools

import jax
import jax.numpy as jnp
from jax import lax
from jax.experimental import pallas as pl
from jax.experimental.pallas import tpu as pltpu
from jax.sharding import PartitionSpec as P

RING = 32
LANES = 128
BF16, F32 = jnp.bfloat16, jnp.float32
VMEM = pltpu.CompilerParams(vmem_limit_bytes=32 * 1024 * 1024)


def dot(left, right, over_left, over_right):
    return lax.dot_general(
        left, right, (((over_left,), (over_right,)), ((), ())), preferred_element_type=F32
    )


def two_terms(x):
    high = x.astype(BF16)
    return jnp.concatenate((high, (x - high.astype(F32)).astype(BF16)), axis=1)


def fine(block, weights):
    both = dot(block, two_terms(weights), 1, 0)
    return both[:, :LANES] + both[:, LANES:]


def shifted(block, distances):
    dp, tower = lax.axis_size("dp"), lax.axis_size("tower")
    route = [
        (i * tower + t, ((i + distances[t % 2]) % dp) * tower + t)
        for i in range(dp)
        for t in range(tower)
    ]
    return lax.ppermute(block, ("dp", "tower"), route)


def score_kernel(i0, t0, t1, t2, i1, i2, out):
    pairs = ((t0, i0), (t1, i0), (t2, i0), (i1, t0), (i2, t0))
    for j, (other, own) in enumerate(pairs):
        out[j * LANES : (j + 1) * LANES] = dot(other[...], own[...], 0, 0).astype(BF16)
    squares = [
        jnp.sum(jnp.square(b[...].astype(F32)), axis=0, keepdims=True)
        for b in (i0, t0, t1, t2, i1, i2)
    ]
    squares = jnp.concatenate(squares + [jnp.zeros((2, LANES), F32)], axis=0)
    high = squares.astype(BF16).astype(F32)
    low = (squares - high).astype(BF16).astype(F32)
    out[5 * LANES :] = jnp.concatenate((high, low), axis=0).astype(BF16)


def weight_kernel(numbers, mine, peer, own, t1, t2, i1, i2, send, keep):
    scale, bias, core0 = numbers[0], numbers[1], numbers[2]
    width = own.shape[0] // 2
    rows = 5 * LANES

    def total(start, size):
        a = mine[start : start + size].astype(F32)
        return a + peer[start : start + size].astype(F32)

    squares = total(rows, 16)
    inv = lax.rsqrt(squares[:8] + squares[8:] + 1e-06)
    down = inv.T

    def weigh(j, across, along):
        c = scale * (total(j * LANES, LANES) * across * along)
        s = c + bias
        e = jnp.exp(-jnp.abs(s))
        return c, s, jnp.log1p(e), jnp.where(s >= 0, 1.0, e) / (1.0 + e)

    ni, nt = inv[0:1], inv[1:2]
    eye = (
        lax.broadcasted_iota(jnp.int32, (LANES, LANES), 0)
        == lax.broadcasted_iota(jnp.int32, (LANES, LANES), 1)
    ).astype(F32)
    c, s, tail, g = weigh(0, ni, down[:, 1:2])
    loss = core0 * jnp.sum(jnp.maximum((1.0 - 2.0 * eye) * s, 0.0) + tail, axis=0, keepdims=True)
    g = g - eye
    gc = g * c
    along_i0 = jnp.sum(gc, axis=0, keepdims=True)
    along_t0 = jnp.sum(gc.T, axis=0, keepdims=True)
    du0 = fine(own[width:], g * down[:, 1:2])
    dv0 = fine(own[:width], (g * ni).T)

    along_i, along_t = jnp.zeros_like(ni), jnp.zeros_like(ni)
    du = dv = None
    for j, block in ((1, t1), (2, t2)):
        col = down[:, j + 1 : j + 2]
        c, s, tail, g = weigh(j, ni, col)
        loss += jnp.sum(jnp.maximum(s, 0.0) + tail, axis=0, keepdims=True)
        along_i += jnp.sum(g * c, axis=0, keepdims=True)
        term = fine(block[...], g * col)
        du = term if du is None else du + term
    for j, block in ((3, i1), (4, i2)):
        col = down[:, j + 1 : j + 2]
        c, s, tail, g = weigh(j, nt, col)
        along_t += jnp.sum(g * c, axis=0, keepdims=True)
        term = fine(block[...], g * col)
        dv = term if dv is None else dv + term
    zero = jnp.zeros_like(ni)
    send[:width] = du[width:]
    send[width : 2 * width] = dv[width:]
    send[2 * width :] = jnp.concatenate((along_i, along_t, loss) + (zero,) * 5, axis=0)
    keep[:width] = du[:width] + du0
    keep[width : 2 * width] = dv[:width] + dv0
    keep[2 * width :] = jnp.concatenate(
        (along_i + along_i0, along_t + along_t0, loss, ni, nt) + (zero,) * 3, axis=0
    )


def gradient_kernel(parts, numbers, keep, got, z, xi, xt, out, loss):
    scale = numbers[0]
    width = z.shape[0] // 2
    lines, more = keep[2 * width :], got[2 * width :]
    loss[...] = jnp.broadcast_to(lines[2:3] + more[2:3], loss.shape)
    grads = []
    for side in range(2):
        part = slice(side * width, (side + 1) * width)
        d = scale * (keep[part] + got[part])
        along = lines[side : side + 1] + more[side : side + 1]
        n = lines[3 + side : 4 + side]
        grads.append(two_terms((d - z[part] * (n * along)) * n))
    block = xi.shape[0] // parts
    whole = width // LANES * LANES
    rest = width - whole
    depth = grads[0].shape[1]
    fold = -(-block // 32) * 16
    folded = []
    for place in range(4):
        pieces = []
        if place:
            pieces.append(jnp.zeros((place * rest, depth), BF16))
        pieces.append(grads[place % 2][whole:])
        if place < 3:
            pieces.append(jnp.zeros(((3 - place) * rest, depth), BF16))
        folded.append(jnp.concatenate(pieces, axis=0))
    for p in range(parts):
        last = None
        for side, x in enumerate((xi, xt)):
            feats = x[p * block : (p + 1) * block]
            feats = jnp.concatenate((feats, feats), axis=1)
            main = dot(feats, grads[side][:whole], 1, 1).astype(BF16)
            for j in range(whole // LANES):
                at = (side * (whole // LANES) + j) * block
                out[p, at : at + block] = main[:, j * LANES : (j + 1) * LANES]
            for half in range(2):
                rows = feats[:fold] if half == 0 else feats[block - fold :]
                term = dot(rows, folded[2 * half + side], 1, 1)
                last = term if last is None else last + term
        out[p, 2 * whole // LANES * block :] = last.astype(BF16)


def ring_kernel(got, out):
    total = jnp.sum(got[...].astype(F32), axis=0)
    top = jnp.max(jnp.max(jnp.abs(total), axis=0, keepdims=True), axis=1, keepdims=True)
    power = jnp.floor(jnp.log2(jnp.where(top > 0, top, 1.0))) - 13.0
    power = jnp.broadcast_to(jnp.maximum(power, -120.0), (1, LANES))
    total = total * jnp.exp2(-power)
    places = out.shape[0]
    count = total.shape[0] // places
    for j in range(count):
        out[:, j] = total[j * places : (j + 1) * places]
    out[:, count] = jnp.broadcast_to(power, (places, LANES))


def row_sets(feats, planes):
    x = feats.T.reshape(planes, RING // 2, -1, feats.shape[0])
    nine = x.shape[2]
    five = nine // 2 + 1
    halves = [x[:, :, nine - five :] if q else x[:, :, :five] for q in range(2)]
    x = jnp.stack(halves, axis=1).transpose(0, 1, 3, 2, 4)
    return x.reshape(-1, feats.shape[0])


def shares(total, width, share):
    count = width // LANES
    rest = width - count * LANES
    five = 5
    fold = total[2 * count * five : 2 * count * five + five // 2 + 1]
    half = lax.axis_index("dp") % 2
    out = []
    for side in range(2):
        pieces = [total[(side * count + j) * five : (side * count + j + 1) * five] for j in range(count)]
        top = fold[:, side * rest : (side + 1) * rest]
        low = fold[1:, (2 + side) * rest : (3 + side) * rest]
        pieces.append(jnp.concatenate((top, low), axis=0))
        flat = jnp.concatenate(pieces, axis=1).reshape(1, -1)
        out.append(jnp.where(half == 0, flat[:, :share], flat[:, flat.shape[1] - share :]))
    return out


def shards(image_feats, text_feats, image_proj, text_proj, logit_scale, logit_bias):
    rows, depth = image_feats.shape
    width = image_proj.shape[1]
    dp, tower = lax.axis_size("dp"), lax.axis_size("tower")
    planes = dp // RING
    to_core = [(t, t ^ 1) for t in range(tower)]
    to_chip = [(t, t ^ 2) for t in range(tower)]
    core0 = (lax.axis_index("tower") % 2 == 0).astype(F32)
    numbers = jnp.concatenate((logit_scale, logit_bias, core0[None]))
    scalars = pl.BlockSpec(memory_space=pltpu.SMEM)
    array = pl.BlockSpec(memory_space=pltpu.VMEM)

    zi = jnp.dot(image_feats, image_proj, preferred_element_type=F32)
    zt = jnp.dot(text_feats, text_proj, preferred_element_type=F32)
    z = jnp.concatenate((zi.T, zt.T), axis=0)
    own = z.astype(BF16)
    other = lax.ppermute(own, "tower", to_core)
    i0 = jnp.concatenate((own[:width], other[:width]), axis=0)
    t0 = jnp.concatenate((own[width:], other[width:]), axis=0)
    t1 = shifted(t0, (1, 2))
    i1 = shifted(i0, (-1, -2))
    t2 = shifted(t1, (2, 2))
    i2 = shifted(i1, (-2, -2))
    xi, xt = row_sets(image_feats, planes), row_sets(text_feats, planes)
    i1, xi, xt = lax.optimization_barrier((i1, xi, xt))
    scores = pl.pallas_call(
        score_kernel,
        out_shape=jax.ShapeDtypeStruct((5 * rows + 16, rows), BF16),
        in_specs=[array] * 6,
        out_specs=array,
        compiler_params=VMEM,
        name="scores",
    )(i0, t0, t1, t2, i1, i2)
    peer = lax.ppermute(scores, "tower", to_chip)
    sums = jax.ShapeDtypeStruct((2 * width + 8, rows), F32)
    send, keep = pl.pallas_call(
        weight_kernel,
        out_shape=(sums, sums),
        in_specs=[scalars] + [array] * 7,
        out_specs=(array, array),
        compiler_params=VMEM,
        name="weights",
    )(numbers, scores, peer, own, t1, t2, i1, i2)
    got = lax.ppermute(send, "tower", to_core)
    parts = 2 * planes
    block = xi.shape[0] // parts
    payload = 2 * (width // LANES) * block + -(-block // 32) * 16
    grads, loss = pl.pallas_call(
        functools.partial(gradient_kernel, parts),
        out_shape=(
            jax.ShapeDtypeStruct((parts, payload, LANES), BF16),
            jax.ShapeDtypeStruct((8, rows), F32),
        ),
        in_specs=[scalars] + [array] * 5,
        out_specs=(array, array),
        compiler_params=VMEM,
        name="gradients",
    )(numbers, keep, got, z, xi, xt)

    places = RING // 2
    groups = [
        [g * RING + 2 * m + q for g in range(planes) for q in range(2)] for m in range(places)
    ]
    grads = lax.all_to_all(grads, "dp", 0, 0, axis_index_groups=groups, tiled=True)
    sent = pl.pallas_call(
        ring_kernel,
        out_shape=jax.ShapeDtypeStruct((places, payload // places + 1, LANES), F32),
        in_specs=[array],
        out_specs=array,
        compiler_params=VMEM,
        name="ring",
    )(grads)
    groups = [
        [g * RING + 2 * m + q for m in range(places)] for g in range(planes) for q in range(2)
    ]
    sent = sent.astype(jnp.float16)
    back = lax.all_to_all(sent, "dp", 0, 0, axis_index_groups=groups, tiled=True).astype(F32)
    total = jnp.sum(back * jnp.exp2(back[:, -1:]), axis=0)
    image_grad, text_grad = shares(total, width, depth * width // dp)
    return (loss[0], image_grad, text_grad)


def solution(mesh):
    in_specs = (P("dp", None), P("dp", None), P(None, "tower"), P(None, "tower"), P(), P())
    out_specs = (P("dp"), P("tower", "dp"), P("tower", "dp"))
    return jax.shard_map(shards, mesh=mesh, in_specs=in_specs, out_specs=out_specs, check_vma=False)
```

```python
import functools

import jax
import jax.numpy as jnp
from jax import lax
from jax.experimental import pallas as pl
from jax.experimental.pallas import tpu as pltpu
from jax.sharding import PartitionSpec as P

RING = 32
LANES = 128
BF16, F32 = jnp.bfloat16, jnp.float32
VMEM = pltpu.CompilerParams(vmem_limit_bytes=32 * 1024 * 1024)


def dot(left, right, over_left, over_right):
    return lax.dot_general(
        left, right, (((over_left,), (over_right,)), ((), ())), preferred_element_type=F32
    )


def two_terms(x):
    high = x.astype(BF16)
    return jnp.concatenate((high, (x - high.astype(F32)).astype(BF16)), axis=1)


def fine(block, weights):
    both = dot(block, two_terms(weights), 1, 0)
    return both[:, :LANES] + both[:, LANES:]


def shifted(block, distances):
    dp, tower = lax.axis_size("dp"), lax.axis_size("tower")
    route = [
        (i * tower + t, ((i + distances[t % 2]) % dp) * tower + t)
        for i in range(dp)
        for t in range(tower)
    ]
    return lax.ppermute(block, ("dp", "tower"), route)


def project_kernel(xi, wi, xt, wt, z, own, xi_here, wi_here, xt_here, wt_here, arrived):
    moves = [
        pltpu.make_async_copy(there, here, arrived.at[j])
        for j, (there, here) in enumerate(
            ((xi, xi_here), (wi, wi_here), (xt, xt_here), (wt, wt_here))
        )
    ]
    for move in moves:
        move.start()
    width = wi_here.shape[0]
    for side, (x, w) in enumerate(((xi_here, wi_here), (xt_here, wt_here))):
        moves[2 * side].wait()
        moves[2 * side + 1].wait()
        part = dot(w[...], x[...], 1, 1)
        z[side * width : (side + 1) * width] = part
        own[side * width : (side + 1) * width] = part.astype(BF16)


def score_kernel(i0, t0, t1, t2, i1, i2, out):
    pairs = ((t0, i0), (t1, i0), (t2, i0), (i1, t0), (i2, t0))
    for j, (other, own) in enumerate(pairs):
        out[j * LANES : (j + 1) * LANES] = dot(other[...], own[...], 0, 0).astype(BF16)
    squares = [
        jnp.sum(jnp.square(b[...].astype(F32)), axis=0, keepdims=True)
        for b in (i0, t0, t1, t2, i1, i2)
    ]
    squares = jnp.concatenate(squares + [jnp.zeros((2, LANES), F32)], axis=0)
    high = squares.astype(BF16).astype(F32)
    low = (squares - high).astype(BF16).astype(F32)
    out[5 * LANES :] = jnp.concatenate((high, low), axis=0).astype(BF16)


def weight_kernel(numbers, mine, peer, own, t1, t2, i1, i2, send, keep):
    scale, bias, core0 = numbers[0], numbers[1], numbers[2]
    width = own.shape[0] // 2
    rows = 5 * LANES

    def total(start, size):
        a = mine[start : start + size].astype(F32)
        return a + peer[start : start + size].astype(F32)

    squares = total(rows, 16)
    inv = lax.rsqrt(squares[:8] + squares[8:] + 1e-06)
    down = inv.T

    def weigh(j, across, along):
        c = scale * (total(j * LANES, LANES) * across * along)
        s = c + bias
        e = jnp.exp(-jnp.abs(s))
        return c, s, jnp.log1p(e), jnp.where(s >= 0, 1.0, e) / (1.0 + e)

    ni, nt = inv[0:1], inv[1:2]
    eye = (
        lax.broadcasted_iota(jnp.int32, (LANES, LANES), 0)
        == lax.broadcasted_iota(jnp.int32, (LANES, LANES), 1)
    ).astype(F32)
    c, s, tail, g = weigh(0, ni, down[:, 1:2])
    loss = core0 * jnp.sum(jnp.maximum((1.0 - 2.0 * eye) * s, 0.0) + tail, axis=0, keepdims=True)
    g = g - eye
    gc = g * c
    along_i0 = jnp.sum(gc, axis=0, keepdims=True)
    along_t0 = jnp.sum(gc.T, axis=0, keepdims=True)
    du0 = fine(own[width:], g * down[:, 1:2])
    dv0 = fine(own[:width], (g * ni).T)

    along_i, along_t = jnp.zeros_like(ni), jnp.zeros_like(ni)
    du = dv = None
    for j, block in ((1, t1), (2, t2)):
        col = down[:, j + 1 : j + 2]
        c, s, tail, g = weigh(j, ni, col)
        loss += jnp.sum(jnp.maximum(s, 0.0) + tail, axis=0, keepdims=True)
        along_i += jnp.sum(g * c, axis=0, keepdims=True)
        term = fine(block[...], g * col)
        du = term if du is None else du + term
    for j, block in ((3, i1), (4, i2)):
        col = down[:, j + 1 : j + 2]
        c, s, tail, g = weigh(j, nt, col)
        along_t += jnp.sum(g * c, axis=0, keepdims=True)
        term = fine(block[...], g * col)
        dv = term if dv is None else dv + term
    zero = jnp.zeros_like(ni)
    send[:width] = du[width:]
    send[width : 2 * width] = dv[width:]
    send[2 * width :] = jnp.concatenate((along_i, along_t, loss) + (zero,) * 5, axis=0)
    keep[:width] = du[:width] + du0
    keep[width : 2 * width] = dv[:width] + dv0
    keep[2 * width :] = jnp.concatenate(
        (along_i + along_i0, along_t + along_t0, loss, ni, nt) + (zero,) * 3, axis=0
    )


def gradient_kernel(parts, numbers, keep, got, z, xi, xt, out, loss):
    scale = numbers[0]
    width = z.shape[0] // 2
    lines, more = keep[2 * width :], got[2 * width :]
    loss[...] = jnp.broadcast_to(lines[2:3] + more[2:3], loss.shape)
    grads = []
    for side in range(2):
        part = slice(side * width, (side + 1) * width)
        d = scale * (keep[part] + got[part])
        along = lines[side : side + 1] + more[side : side + 1]
        n = lines[3 + side : 4 + side]
        grads.append(two_terms((d - z[part] * (n * along)) * n))
    block = xi.shape[0] // parts
    whole = width // LANES * LANES
    rest = width - whole
    fold = -(-block // 32) * 16
    tail = None
    for side, x in enumerate((xi, xt)):
        feats = jnp.concatenate((x[...], x[...]), axis=1)
        main = dot(feats, grads[side][:whole], 1, 1).astype(BF16)
        for j in range(whole // LANES):
            at = (side * (whole // LANES) + j) * block
            for p in range(parts):
                out[p, at : at + block] = main[p * block : (p + 1) * block, j * LANES : (j + 1) * LANES]
        piece = grads[side][whole:]
        gap = jnp.zeros_like(piece)
        pieces = [gap] * (2 * LANES // rest)
        pieces[side] = pieces[LANES // rest + LANES // rest // 2 + side] = piece
        term = dot(feats, jnp.concatenate(pieces, axis=0), 1, 1)
        tail = term if tail is None else tail + term
    for p in range(parts):
        upper = tail[p * block : p * block + fold, :LANES]
        lower = tail[(p + 1) * block - fold : (p + 1) * block, LANES:]
        out[p, 2 * whole // LANES * block :] = (upper + lower).astype(BF16)


def ring_kernel(got, out):
    total = jnp.sum(got[...].astype(F32), axis=0)
    top = jnp.max(jnp.max(jnp.abs(total), axis=0, keepdims=True), axis=1, keepdims=True)
    power = jnp.floor(jnp.log2(jnp.where(top > 0, top, 1.0))) - 13.0
    power = jnp.broadcast_to(jnp.maximum(power, -120.0), (1, LANES))
    total = total * jnp.exp2(-power)
    places = out.shape[0]
    count = total.shape[0] // places
    for j in range(count):
        out[:, j] = total[j * places : (j + 1) * places]
    out[:, count] = jnp.broadcast_to(power, (places, LANES))


def row_sets(feats, planes):
    x = feats.T.reshape(planes, RING // 2, -1, feats.shape[0])
    nine = x.shape[2]
    five = nine // 2 + 1
    halves = [x[:, :, nine - five :] if q else x[:, :, :five] for q in range(2)]
    x = jnp.stack(halves, axis=1).transpose(0, 1, 3, 2, 4)
    return x.reshape(-1, feats.shape[0])


def shares(total, width, share):
    count = width // LANES
    rest = width - count * LANES
    five = 5
    fold = total[2 * count * five : 2 * count * five + five // 2 + 1]
    half = lax.axis_index("dp") % 2
    out = []
    for side in range(2):
        pieces = [total[(side * count + j) * five : (side * count + j + 1) * five] for j in range(count)]
        top = fold[:, side * rest : (side + 1) * rest]
        low = fold[1:, (2 + side) * rest : (3 + side) * rest]
        pieces.append(jnp.concatenate((top, low), axis=0))
        flat = jnp.concatenate(pieces, axis=1).reshape(1, -1)
        out.append(jnp.where(half == 0, flat[:, :share], flat[:, flat.shape[1] - share :]))
    return out


def shards(image_feats, text_feats, image_proj, text_proj, logit_scale, logit_bias):
    rows, depth = image_feats.shape
    width = image_proj.shape[1]
    dp, tower = lax.axis_size("dp"), lax.axis_size("tower")
    planes = dp // RING
    to_core = [(t, t ^ 1) for t in range(tower)]
    to_chip = [(t, t ^ 2) for t in range(tower)]
    core0 = (lax.axis_index("tower") % 2 == 0).astype(F32)
    numbers = jnp.concatenate((logit_scale, logit_bias, core0[None]))
    scalars = pl.BlockSpec(memory_space=pltpu.SMEM)
    array = pl.BlockSpec(memory_space=pltpu.VMEM)

    here = [pltpu.VMEM((rows, depth), BF16), pltpu.VMEM((width, depth), BF16)] * 2
    z, own = pl.pallas_call(
        project_kernel,
        out_shape=(
            jax.ShapeDtypeStruct((2 * width, rows), F32),
            jax.ShapeDtypeStruct((2 * width, rows), BF16),
        ),
        in_specs=[pl.BlockSpec(memory_space=pl.ANY)] * 4,
        out_specs=(array, array),
        scratch_shapes=here + [pltpu.SemaphoreType.DMA((4,))],
        compiler_params=pltpu.CompilerParams(vmem_limit_bytes=60 * 1024 * 1024),
        name="project",
    )(image_feats, image_proj.T, text_feats, text_proj.T)
    other = lax.ppermute(own, "tower", to_core)
    i0 = jnp.concatenate((own[:width], other[:width]), axis=0)
    t0 = jnp.concatenate((own[width:], other[width:]), axis=0)
    t2 = shifted(t0, (4, 3))
    i2 = shifted(i0, (-4, -3))
    t1 = shifted(t0, (1, 2))
    i1 = shifted(i0, (-1, -2))
    xi, xt = row_sets(image_feats, planes), row_sets(text_feats, planes)
    i1, xi, xt = lax.optimization_barrier((i1, xi, xt))
    scores = pl.pallas_call(
        score_kernel,
        out_shape=jax.ShapeDtypeStruct((5 * rows + 16, rows), BF16),
        in_specs=[array] * 6,
        out_specs=array,
        compiler_params=VMEM,
        name="scores",
    )(i0, t0, t1, t2, i1, i2)
    peer = lax.ppermute(scores, "tower", to_chip)
    sums = jax.ShapeDtypeStruct((2 * width + 8, rows), F32)
    send, keep = pl.pallas_call(
        weight_kernel,
        out_shape=(sums, sums),
        in_specs=[scalars] + [array] * 7,
        out_specs=(array, array),
        compiler_params=VMEM,
        name="weights",
    )(numbers, scores, peer, own, t1, t2, i1, i2)
    got = lax.ppermute(send, "tower", to_core)
    parts = 2 * planes
    block = xi.shape[0] // parts
    payload = 2 * (width // LANES) * block + -(-block // 32) * 16
    grads, loss = pl.pallas_call(
        functools.partial(gradient_kernel, parts),
        out_shape=(
            jax.ShapeDtypeStruct((parts, payload, LANES), BF16),
            jax.ShapeDtypeStruct((8, rows), F32),
        ),
        in_specs=[scalars] + [array] * 5,
        out_specs=(array, array),
        compiler_params=VMEM,
        name="gradients",
    )(numbers, keep, got, z, xi, xt)

    places = RING // 2
    groups = [
        [g * RING + 2 * m + q for g in range(planes) for q in range(2)] for m in range(places)
    ]
    grads = lax.all_to_all(grads, "dp", 0, 0, axis_index_groups=groups, tiled=True)
    sent = pl.pallas_call(
        ring_kernel,
        out_shape=jax.ShapeDtypeStruct((places, payload // places + 1, LANES), F32),
        in_specs=[array],
        out_specs=array,
        compiler_params=VMEM,
        name="ring",
    )(grads)
    groups = [
        [g * RING + 2 * m + q for m in range(places)] for g in range(planes) for q in range(2)
    ]
    sent = sent.astype(jnp.float16)
    back = lax.all_to_all(sent, "dp", 0, 0, axis_index_groups=groups, tiled=True).astype(F32)
    total = jnp.sum(back * jnp.exp2(back[:, -1:]), axis=0)
    image_grad, text_grad = shares(total, width, depth * width // dp)
    return (loss[0], image_grad, text_grad)


def solution(mesh):
    in_specs = (P("dp", None), P("dp", None), P(None, "tower"), P(None, "tower"), P(), P())
    out_specs = (P("dp"), P("tower", "dp"), P("tower", "dp"))
    return jax.shard_map(shards, mesh=mesh, in_specs=in_specs, out_specs=out_specs, check_vma=False)
```

```python
import functools

import jax
import jax.numpy as jnp
from jax import lax
from jax.experimental import pallas as pl
from jax.experimental.pallas import tpu as pltpu
from jax.sharding import PartitionSpec as P

RING = 32
LANES = 128
BF16, F32 = jnp.bfloat16, jnp.float32
VMEM = pltpu.CompilerParams(vmem_limit_bytes=32 * 1024 * 1024)


def dot(left, right, over_left, over_right):
    return lax.dot_general(
        left, right, (((over_left,), (over_right,)), ((), ())), preferred_element_type=F32
    )


def two_terms(x):
    high = x.astype(BF16)
    return jnp.concatenate((high, (x - high.astype(F32)).astype(BF16)), axis=1)


def fine(block, weights):
    both = dot(block, two_terms(weights), 1, 0)
    return both[:, :LANES] + both[:, LANES:]


def shifted(block, distances):
    dp, tower = lax.axis_size("dp"), lax.axis_size("tower")
    route = [
        (i * tower + t, ((i + distances[t % 2]) % dp) * tower + t)
        for i in range(dp)
        for t in range(tower)
    ]
    return lax.ppermute(block, ("dp", "tower"), route)


def project_kernel(xi, wi, xt, wt, z, own, xi_here, wi_here, xt_here, wt_here, arrived):
    moves = [
        pltpu.make_async_copy(there, here, arrived.at[j])
        for j, (there, here) in enumerate(
            ((xi, xi_here), (wi, wi_here), (xt, xt_here), (wt, wt_here))
        )
    ]
    for move in moves:
        move.start()
    width = wi_here.shape[0]
    for side, (x, w) in enumerate(((xi_here, wi_here), (xt_here, wt_here))):
        moves[2 * side].wait()
        moves[2 * side + 1].wait()
        part = dot(w[...], x[...], 1, 1)
        z[side * width : (side + 1) * width] = part
        own[side * width : (side + 1) * width] = part.astype(BF16)


def score_kernel(own, o0, o1, o2, far, out):
    size = own.shape[0]
    blocks = [own[...], o0[...], o1[...], o2[...], far[:size], far[size:]]
    for j, other in enumerate(blocks[1:]):
        out[j * LANES : (j + 1) * LANES] = dot(other, blocks[0], 0, 0).astype(BF16)
    squares = [jnp.sum(jnp.square(b.astype(F32)), axis=0, keepdims=True) for b in blocks]
    squares = jnp.concatenate(squares + [jnp.zeros((2, LANES), F32)], axis=0)
    high = squares.astype(BF16).astype(F32)
    low = (squares - high).astype(BF16).astype(F32)
    out[5 * LANES :] = jnp.concatenate((high, low), axis=0).astype(BF16)


def weight_kernel(numbers, mine, peer, o0, o1, o2, far, send, keep):
    scale, bias = numbers[0], numbers[1]
    size = o0.shape[0]
    width = size // 2

    def total(start, rows):
        a = mine[start : start + rows].astype(F32)
        return a + peer[start : start + rows].astype(F32)

    squares = total(5 * LANES, 16)
    inv = lax.rsqrt(squares[:8] + squares[8:] + 1e-06)
    down = inv.T
    eye = (
        lax.broadcasted_iota(jnp.int32, (LANES, LANES), 0)
        == lax.broadcasted_iota(jnp.int32, (LANES, LANES), 1)
    ).astype(F32)
    n = inv[0:1]
    loss = along = jnp.zeros_like(n)
    d = None
    for j, other in enumerate((o0[...], o1[...], o2[...], far[:size], far[size:])):
        col = down[:, j + 1 : j + 2]
        c = scale * (total(j * LANES, LANES) * n * col)
        s = c + bias
        e = jnp.exp(-jnp.abs(s))
        g = jnp.where(s >= 0, 1.0, e) / (1.0 + e)
        signed = s
        if j == 0:
            signed, g = (1.0 - 2.0 * eye) * s, g - eye
        loss += jnp.sum(jnp.maximum(signed, 0.0) + jnp.log1p(e), axis=0, keepdims=True)
        along += jnp.sum(g * c, axis=0, keepdims=True)
        term = fine(other, g * col)
        d = term if d is None else d + term
    lines = jnp.concatenate((along, loss, n, jnp.zeros((5, LANES), F32)), axis=0)
    keep[:width], send[:width] = d[:width], d[width:]
    keep[width:], send[width:] = lines, lines


def gradient_kernel(parts, numbers, keep, got, z, xi, xt, out, loss):
    scale, first = numbers[0], numbers[2] > 0
    width = z.shape[0] // 2
    grads = []
    for side in range(2):
        own, other = (keep, got) if side == 0 else (got, keep)
        lines = jnp.where(first, own[width:], other[width:])
        along, n = lines[0:1], lines[2:3]
        if side == 0:
            loss[...] = jnp.broadcast_to(lines[1:2], loss.shape)
        d = scale * jnp.where(first, own[:width], other[:width])
        part = z[side * width : (side + 1) * width]
        grads.append(two_terms((d - part * (n * along)) * n))
    block = xi.shape[0] // parts
    whole = width // LANES * LANES
    rest = width - whole
    fold = -(-block // 32) * 16
    tail = None
    for side, x in enumerate((xi, xt)):
        feats = jnp.concatenate((x[...], x[...]), axis=1)
        main = dot(feats, grads[side][:whole], 1, 1).astype(BF16)
        for j in range(whole // LANES):
            at = (side * (whole // LANES) + j) * block
            for p in range(parts):
                out[p, at : at + block] = main[p * block : (p + 1) * block, j * LANES : (j + 1) * LANES]
        piece = grads[side][whole:]
        gap = jnp.zeros_like(piece)
        pieces = [gap] * (2 * LANES // rest)
        pieces[side] = pieces[LANES // rest + LANES // rest // 2 + side] = piece
        term = dot(feats, jnp.concatenate(pieces, axis=0), 1, 1)
        tail = term if tail is None else tail + term
    for p in range(parts):
        upper = tail[p * block : p * block + fold, :LANES]
        lower = tail[(p + 1) * block - fold : (p + 1) * block, LANES:]
        out[p, 2 * whole // LANES * block :] = (upper + lower).astype(BF16)


def ring_kernel(got, out):
    total = jnp.sum(got[...].astype(F32), axis=0)
    top = jnp.max(jnp.max(jnp.abs(total), axis=0, keepdims=True), axis=1, keepdims=True)
    power = jnp.floor(jnp.log2(jnp.where(top > 0, top, 1.0))) - 13.0
    power = jnp.broadcast_to(jnp.maximum(power, -120.0), (1, LANES))
    total = total * jnp.exp2(-power)
    places = out.shape[0]
    count = total.shape[0] // places
    for j in range(count):
        out[:, j] = total[j * places : (j + 1) * places]
    out[:, count] = jnp.broadcast_to(power, (places, LANES))


def row_sets(feats, planes):
    x = feats.T.reshape(planes, RING // 2, -1, feats.shape[0])
    nine = x.shape[2]
    five = nine // 2 + 1
    halves = [x[:, :, nine - five :] if q else x[:, :, :five] for q in range(2)]
    x = jnp.stack(halves, axis=1).transpose(0, 1, 3, 2, 4)
    return x.reshape(-1, feats.shape[0])


def shares(total, width, share):
    count = width // LANES
    rest = width - count * LANES
    five = 5
    fold = total[2 * count * five : 2 * count * five + five // 2 + 1]
    half = lax.axis_index("dp") % 2
    out = []
    for side in range(2):
        pieces = [total[(side * count + j) * five : (side * count + j + 1) * five] for j in range(count)]
        top = fold[:, side * rest : (side + 1) * rest]
        low = fold[1:, (2 + side) * rest : (3 + side) * rest]
        pieces.append(jnp.concatenate((top, low), axis=0))
        flat = jnp.concatenate(pieces, axis=1).reshape(1, -1)
        out.append(jnp.where(half == 0, flat[:, :share], flat[:, flat.shape[1] - share :]))
    return out


def shards(image_feats, text_feats, image_proj, text_proj, logit_scale, logit_bias):
    rows, depth = image_feats.shape
    width = image_proj.shape[1]
    dp, tower = lax.axis_size("dp"), lax.axis_size("tower")
    planes = dp // RING
    to_core = [(t, t ^ 1) for t in range(tower)]
    to_chip = [(t, t ^ 2) for t in range(tower)]
    first = lax.axis_index("tower") % 2 == 0
    core0 = first.astype(F32)
    numbers = jnp.concatenate((logit_scale, logit_bias, core0[None]))
    scalars = pl.BlockSpec(memory_space=pltpu.SMEM)
    array = pl.BlockSpec(memory_space=pltpu.VMEM)

    here = [pltpu.VMEM((rows, depth), BF16), pltpu.VMEM((width, depth), BF16)] * 2
    z, own = pl.pallas_call(
        project_kernel,
        out_shape=(
            jax.ShapeDtypeStruct((2 * width, rows), F32),
            jax.ShapeDtypeStruct((2 * width, rows), BF16),
        ),
        in_specs=[pl.BlockSpec(memory_space=pl.ANY)] * 4,
        out_specs=(array, array),
        scratch_shapes=here + [pltpu.SemaphoreType.DMA((4,))],
        compiler_params=pltpu.CompilerParams(vmem_limit_bytes=60 * 1024 * 1024),
        name="project",
    )(image_feats, image_proj.T, text_feats, text_proj.T)
    other = lax.ppermute(own, "tower", to_core)
    i0 = jnp.concatenate((own[:width], other[:width]), axis=0)
    t0 = jnp.concatenate((own[width:], other[width:]), axis=0)
    mine, o0 = jnp.where(first, i0, t0), jnp.where(first, t0, i0)
    o1 = shifted(o0, (1, -1))
    o2 = shifted(o0, (2, -2))
    far = shifted(jnp.concatenate((o1, o2), axis=0), (2, -2))
    xi, xt = row_sets(image_feats, planes), row_sets(text_feats, planes)
    mine, xi, xt = lax.optimization_barrier((mine, xi, xt))
    scores = pl.pallas_call(
        score_kernel,
        out_shape=jax.ShapeDtypeStruct((5 * rows + 16, rows), BF16),
        in_specs=[array] * 5,
        out_specs=array,
        compiler_params=VMEM,
        name="scores",
    )(mine, o0, o1, o2, far)
    peer = lax.ppermute(scores, "tower", to_chip)
    sums = jax.ShapeDtypeStruct((width + 8, rows), F32)
    send, keep = pl.pallas_call(
        weight_kernel,
        out_shape=(sums, sums),
        in_specs=[scalars] + [array] * 6,
        out_specs=(array, array),
        compiler_params=VMEM,
        name="weights",
    )(numbers, scores, peer, o0, o1, o2, far)
    got = lax.ppermute(send, "tower", to_core)
    parts = 2 * planes
    block = xi.shape[0] // parts
    payload = 2 * (width // LANES) * block + -(-block // 32) * 16
    grads, loss = pl.pallas_call(
        functools.partial(gradient_kernel, parts),
        out_shape=(
            jax.ShapeDtypeStruct((parts, payload, LANES), BF16),
            jax.ShapeDtypeStruct((8, rows), F32),
        ),
        in_specs=[scalars] + [array] * 5,
        out_specs=(array, array),
        compiler_params=VMEM,
        name="gradients",
    )(numbers, keep, got, z, xi, xt)

    places = RING // 2
    groups = [
        [g * RING + 2 * m + q for g in range(planes) for q in range(2)] for m in range(places)
    ]
    grads = lax.all_to_all(grads, "dp", 0, 0, axis_index_groups=groups, tiled=True)
    sent = pl.pallas_call(
        ring_kernel,
        out_shape=jax.ShapeDtypeStruct((places, payload // places + 1, LANES), F32),
        in_specs=[array],
        out_specs=array,
        compiler_params=VMEM,
        name="ring",
    )(grads)
    groups = [
        [g * RING + 2 * m + q for m in range(places)] for g in range(planes) for q in range(2)
    ]
    sent = sent.astype(jnp.float16)
    back = lax.all_to_all(sent, "dp", 0, 0, axis_index_groups=groups, tiled=True).astype(F32)
    total = jnp.sum(back * jnp.exp2(back[:, -1:]), axis=0)
    image_grad, text_grad = shares(total, width, depth * width // dp)
    return (loss[0], image_grad, text_grad)


def solution(mesh):
    in_specs = (P("dp", None), P("dp", None), P(None, "tower"), P(None, "tower"), P(), P())
    out_specs = (P("dp"), P("tower", "dp"), P("tower", "dp"))
    return jax.shard_map(shards, mesh=mesh, in_specs=in_specs, out_specs=out_specs, check_vma=False)
```

```python
import functools

import jax
import jax.numpy as jnp
from jax import lax
from jax.experimental import pallas as pl
from jax.experimental.pallas import tpu as pltpu
from jax.sharding import PartitionSpec as P

RING = 32
LANES = 128
BF16, F32 = jnp.bfloat16, jnp.float32
VMEM = pltpu.CompilerParams(vmem_limit_bytes=32 * 1024 * 1024)


def dot(left, right, over_left, over_right):
    return lax.dot_general(
        left, right, (((over_left,), (over_right,)), ((), ())), preferred_element_type=F32
    )


def two_terms(x):
    high = x.astype(BF16)
    return jnp.concatenate((high, (x - high.astype(F32)).astype(BF16)), axis=1)


def fine(block, weights):
    both = dot(block, two_terms(weights), 1, 0)
    return both[:, :LANES] + both[:, LANES:]


def shifted(block, distances):
    dp, tower = lax.axis_size("dp"), lax.axis_size("tower")
    route = [
        (i * tower + t, ((i + distances[t % 2]) % dp) * tower + t)
        for i in range(dp)
        for t in range(tower)
    ]
    return lax.ppermute(block, ("dp", "tower"), route)


def project_kernel(xi, wi, xt, wt, z, own, xi_here, wi_here, xt_here, wt_here, arrived):
    moves = [
        pltpu.make_async_copy(there, here, arrived.at[j])
        for j, (there, here) in enumerate(
            ((xi, xi_here), (wi, wi_here), (xt, xt_here), (wt, wt_here))
        )
    ]
    for move in moves:
        move.start()
    width = wi_here.shape[0]
    for side, (x, w) in enumerate(((xi_here, wi_here), (xt_here, wt_here))):
        moves[2 * side].wait()
        moves[2 * side + 1].wait()
        part = dot(w[...], x[...], 1, 1)
        z[side * width : (side + 1) * width] = part
        own[side * width : (side + 1) * width] = part.astype(BF16)


def score_kernel(own, o0, o1, o2, far, out):
    size = own.shape[0]
    blocks = [own[...], o0[...], o1[...], o2[...], far[:size], far[size:]]
    for j, other in enumerate(blocks[1:]):
        out[j * LANES : (j + 1) * LANES] = dot(other, blocks[0], 0, 0).astype(BF16)
    squares = [jnp.sum(jnp.square(b.astype(F32)), axis=0, keepdims=True) for b in blocks]
    squares = jnp.concatenate(squares + [jnp.zeros((2, LANES), F32)], axis=0)
    high = squares.astype(BF16).astype(F32)
    low = (squares - high).astype(BF16).astype(F32)
    out[5 * LANES :] = jnp.concatenate((high, low), axis=0).astype(BF16)


def weight_kernel(numbers, mine, peer, o0, o1, o2, far, send, keep):
    scale, bias = numbers[0], numbers[1]
    size = o0.shape[0]
    width = size // 2

    def total(start, rows):
        a = mine[start : start + rows].astype(F32)
        return a + peer[start : start + rows].astype(F32)

    squares = total(5 * LANES, 16)
    inv = lax.rsqrt(squares[:8] + squares[8:] + 1e-06)
    down = inv.T
    eye = (
        lax.broadcasted_iota(jnp.int32, (LANES, LANES), 0)
        == lax.broadcasted_iota(jnp.int32, (LANES, LANES), 1)
    ).astype(F32)
    n = inv[0:1]
    loss = along = jnp.zeros_like(n)
    d = None
    for j, other in enumerate((o0[...], o1[...], o2[...], far[:size], far[size:])):
        col = down[:, j + 1 : j + 2]
        c = scale * (total(j * LANES, LANES) * n * col)
        s = c + bias
        e = jnp.exp(-jnp.abs(s))
        g = jnp.where(s >= 0, 1.0, e) / (1.0 + e)
        signed = s
        if j == 0:
            signed, g = (1.0 - 2.0 * eye) * s, g - eye
        loss += jnp.sum(jnp.maximum(signed, 0.0) + jnp.log1p(e), axis=0, keepdims=True)
        along += jnp.sum(g * c, axis=0, keepdims=True)
        term = fine(other, g * col)
        d = term if d is None else d + term
    lines = jnp.concatenate((along, loss, n, jnp.zeros((5, LANES), F32)), axis=0)
    keep[:width], send[:width] = d[:width], d[width:]
    keep[width:], send[width:] = lines, lines


def slope_kernel(numbers, keep, got, z, slopes, send, loss):
    scale, first = numbers[0], numbers[2] > 0
    width = z.shape[0] // 2
    for side in range(2):
        own, other = (keep, got) if side == 0 else (got, keep)
        lines = jnp.where(first, own[width:], other[width:])
        along, n = lines[0:1], lines[2:3]
        if side == 0:
            loss[...] = jnp.broadcast_to(lines[1:2], loss.shape)
        d = scale * jnp.where(first, own[:width], other[:width])
        part = slice(side * width, (side + 1) * width)
        terms = two_terms((d - z[part] * (n * along)) * n)
        slopes[part] = terms
        send[part] = terms[:, :LANES]


def gradient_kernel(parts, slopes, theirs, xi, xt, beside, out):
    width, count = slopes.shape[0] // 2, xi.shape[0]
    block = xi.shape[0] // parts
    whole = width // LANES * LANES
    rest = width - whole
    fold = -(-block // 32) * 16
    tail = None
    for side, x in enumerate((xi, xt)):
        there = slice(side * count, (side + 1) * count)
        feats = jnp.concatenate((x[...], x[...], beside[there]), axis=1)
        part = slice(side * width, (side + 1) * width)
        grads = jnp.concatenate((slopes[part], theirs[part]), axis=1)
        main = dot(feats, grads[:whole], 1, 1).astype(BF16)
        for j in range(whole // LANES):
            at = (side * (whole // LANES) + j) * block
            for p in range(parts):
                out[p, at : at + block] = main[p * block : (p + 1) * block, j * LANES : (j + 1) * LANES]
        piece = grads[whole:]
        gap = jnp.zeros_like(piece)
        pieces = [gap] * (2 * LANES // rest)
        pieces[side] = pieces[LANES // rest + LANES // rest // 2 + side] = piece
        term = dot(feats, jnp.concatenate(pieces, axis=0), 1, 1)
        tail = term if tail is None else tail + term
    for p in range(parts):
        upper = tail[p * block : p * block + fold, :LANES]
        lower = tail[(p + 1) * block - fold : (p + 1) * block, LANES:]
        out[p, 2 * whole // LANES * block :] = (upper + lower).astype(BF16)


def ring_kernel(got, out):
    total = jnp.sum(got[...].astype(F32), axis=0)
    top = jnp.max(jnp.max(jnp.abs(total), axis=0, keepdims=True), axis=1, keepdims=True)
    power = jnp.floor(jnp.log2(jnp.where(top > 0, top, 1.0))) - 13.0
    power = jnp.broadcast_to(jnp.maximum(power, -120.0), (1, LANES))
    total = total * jnp.exp2(-power)
    places = out.shape[0]
    count = total.shape[0] // places
    for j in range(count):
        out[:, j] = total[j * places : (j + 1) * places]
    out[:, count] = jnp.broadcast_to(power, (places, LANES))


def order_kernel(column, xi, xt, own_i, own_t, away, turned):
    places = RING // 2
    depth, size = turned.shape[0], own_i.shape[0]
    five = 5
    nine = 2 * five - 1
    planes = size // (2 * five * places)
    block = depth // (2 * planes)
    for side, x in enumerate((xi, xt)):
        turned[...] = x[...].astype(F32).T
        for beside in range(2):
            first = (column[0] + beside) % 2 * block
            for p in range(planes):
                for q in range(2):
                    for r in range(five):
                        start = first + 2 * p * block + (five - 1) * q + r
                        rows = turned[pl.ds(start, places, stride=nine)].astype(BF16)
                        at = ((2 * p + q) * five + r) * places
                        if beside:
                            away[side * size + at : side * size + at + places] = rows
                        else:
                            (own_t if side else own_i)[at : at + places] = rows


def shares(total, width, share):
    count = width // LANES
    rest = width - count * LANES
    five = 5
    fold = total[2 * count * five : 2 * count * five + five // 2 + 1]
    half = lax.axis_index("dp") % 2
    out = []
    for side in range(2):
        pieces = [total[(side * count + j) * five : (side * count + j + 1) * five] for j in range(count)]
        top = fold[:, side * rest : (side + 1) * rest]
        low = fold[1:, (2 + side) * rest : (3 + side) * rest]
        pieces.append(jnp.concatenate((top, low), axis=0))
        flat = jnp.concatenate(pieces, axis=1).reshape(1, -1)
        out.append(jnp.where(half == 0, flat[:, :share], flat[:, flat.shape[1] - share :]))
    return out


def shards(image_feats, text_feats, image_proj, text_proj, logit_scale, logit_bias):
    rows, depth = image_feats.shape
    width = image_proj.shape[1]
    dp, tower = lax.axis_size("dp"), lax.axis_size("tower")
    planes = dp // RING
    to_core = [(t, t ^ 1) for t in range(tower)]
    to_chip = [(t, t ^ 2) for t in range(tower)]
    first = lax.axis_index("tower") % 2 == 0
    core0 = first.astype(F32)
    numbers = jnp.concatenate((logit_scale, logit_bias, core0[None]))
    scalars = pl.BlockSpec(memory_space=pltpu.SMEM)
    array = pl.BlockSpec(memory_space=pltpu.VMEM)

    here = [pltpu.VMEM((rows, depth), BF16), pltpu.VMEM((width, depth), BF16)] * 2
    z, own = pl.pallas_call(
        project_kernel,
        out_shape=(
            jax.ShapeDtypeStruct((2 * width, rows), F32),
            jax.ShapeDtypeStruct((2 * width, rows), BF16),
        ),
        in_specs=[pl.BlockSpec(memory_space=pl.ANY)] * 4,
        out_specs=(array, array),
        scratch_shapes=here + [pltpu.SemaphoreType.DMA((4,))],
        compiler_params=pltpu.CompilerParams(vmem_limit_bytes=60 * 1024 * 1024),
        name="project",
    )(image_feats, image_proj.T, text_feats, text_proj.T)
    other = lax.ppermute(own, "tower", to_core)
    i0 = jnp.concatenate((own[:width], other[:width]), axis=0)
    t0 = jnp.concatenate((own[width:], other[width:]), axis=0)
    mine, o0 = jnp.where(first, i0, t0), jnp.where(first, t0, i0)
    o1 = shifted(o0, (1, -1))
    o2 = shifted(o0, (2, -2))
    far = shifted(jnp.concatenate((o1, o2), axis=0), (2, -2))
    column = (lax.axis_index("dp") // RING % 2).astype(jnp.int32)[None]
    beside = [(i, i ^ RING) for i in range(dp)]
    image_feats, text_feats, column, _ = lax.optimization_barrier((image_feats, text_feats, column, o0))
    size = planes * 5 * (RING // 2)
    xi, xt, away = pl.pallas_call(
        order_kernel,
        out_shape=tuple(jax.ShapeDtypeStruct((n, rows), BF16) for n in (size, size, 2 * size)),
        in_specs=[scalars, array, array],
        out_specs=(array,) * 3,
        scratch_shapes=[pltpu.VMEM((depth, rows), F32)],
        compiler_params=VMEM,
        name="order",
    )(column, image_feats, text_feats)
    x_beside = lax.ppermute(away, "dp", beside)
    mine, xi, xt, x_beside = lax.optimization_barrier((mine, xi, xt, x_beside))
    scores = pl.pallas_call(
        score_kernel,
        out_shape=jax.ShapeDtypeStruct((5 * rows + 16, rows), BF16),
        in_specs=[array] * 5,
        out_specs=array,
        compiler_params=VMEM,
        name="scores",
    )(mine, o0, o1, o2, far)
    peer = lax.ppermute(scores, "tower", to_chip)
    sums = jax.ShapeDtypeStruct((width + 8, rows), F32)
    send, keep = pl.pallas_call(
        weight_kernel,
        out_shape=(sums, sums),
        in_specs=[scalars] + [array] * 6,
        out_specs=(array, array),
        compiler_params=VMEM,
        name="weights",
    )(numbers, scores, peer, o0, o1, o2, far)
    got = lax.ppermute(send, "tower", to_core)
    slopes, send, loss = pl.pallas_call(
        slope_kernel,
        out_shape=(
            jax.ShapeDtypeStruct((2 * width, 2 * rows), BF16),
            jax.ShapeDtypeStruct((2 * width, rows), BF16),
            jax.ShapeDtypeStruct((8, rows), F32),
        ),
        in_specs=[scalars] + [array] * 3,
        out_specs=(array,) * 3,
        compiler_params=VMEM,
        name="slopes",
    )(numbers, keep, got, z)
    theirs = lax.ppermute(send, "dp", beside)
    parts = planes
    block = xi.shape[0] // parts
    payload = 2 * (width // LANES) * block + -(-block // 32) * 16
    grads = pl.pallas_call(
        functools.partial(gradient_kernel, parts),
        out_shape=jax.ShapeDtypeStruct((parts, payload, LANES), BF16),
        in_specs=[array] * 5,
        out_specs=array,
        compiler_params=VMEM,
        name="gradients",
    )(slopes, theirs, xi, xt, x_beside)

    places = RING // 2
    groups = [
        [(2 * y + x) * RING + 2 * m + q for y in range(planes // 2) for q in range(2)]
        for x in range(2)
        for m in range(places)
    ]
    grads = lax.all_to_all(grads, "dp", 0, 0, axis_index_groups=groups, tiled=True)
    sent = pl.pallas_call(
        ring_kernel,
        out_shape=jax.ShapeDtypeStruct((places, payload // places + 1, LANES), F32),
        in_specs=[array],
        out_specs=array,
        compiler_params=VMEM,
        name="ring",
    )(grads)
    groups = [
        [g * RING + 2 * m + q for m in range(places)] for g in range(planes) for q in range(2)
    ]
    sent = sent.astype(jnp.float16)
    back = lax.all_to_all(sent, "dp", 0, 0, axis_index_groups=groups, tiled=True).astype(F32)
    total = jnp.sum(back * jnp.exp2(back[:, -1:]), axis=0)
    image_grad, text_grad = shares(total, width, depth * width // dp)
    return (loss[0], image_grad, text_grad)


def solution(mesh):
    in_specs = (P("dp", None), P("dp", None), P(None, "tower"), P(None, "tower"), P(), P())
    out_specs = (P("dp"), P("tower", "dp"), P("tower", "dp"))
    return jax.shard_map(shards, mesh=mesh, in_specs=in_specs, out_specs=out_specs, check_vma=False)
```

```python
import functools

import jax
import jax.numpy as jnp
from jax import lax
from jax.experimental import pallas as pl
from jax.experimental.pallas import tpu as pltpu
from jax.sharding import PartitionSpec as P

RING = 32
LANES = 128
BF16, F32 = jnp.bfloat16, jnp.float32
VMEM = pltpu.CompilerParams(vmem_limit_bytes=32 * 1024 * 1024)


def dot(left, right, over_left, over_right):
    return lax.dot_general(
        left, right, (((over_left,), (over_right,)), ((), ())), preferred_element_type=F32
    )


def two_terms(x):
    high = x.astype(BF16)
    return jnp.concatenate((high, (x - high.astype(F32)).astype(BF16)), axis=1)


def fine(block, weights):
    both = dot(block, two_terms(weights), 1, 0)
    return both[:, :LANES] + both[:, LANES:]


def shifted(block, distances):
    dp, tower = lax.axis_size("dp"), lax.axis_size("tower")
    route = [
        (i * tower + t, ((i + distances[t % 2]) % dp) * tower + t)
        for i in range(dp)
        for t in range(tower)
    ]
    return lax.ppermute(block, ("dp", "tower"), route)


def project_kernel(xi, wi, xt, wt, z, own, xi_here, wi_here, xt_here, wt_here, arrived):
    moves = [
        pltpu.make_async_copy(there, here, arrived.at[j])
        for j, (there, here) in enumerate(
            ((xi, xi_here), (wi, wi_here), (xt, xt_here), (wt, wt_here))
        )
    ]
    for move in moves:
        move.start()
    width = wi_here.shape[0]
    for side, (x, w) in enumerate(((xi_here, wi_here), (xt_here, wt_here))):
        moves[2 * side].wait()
        moves[2 * side + 1].wait()
        part = dot(w[...], x[...], 1, 1)
        z[side * width : (side + 1) * width] = part
        own[side * width : (side + 1) * width] = part.astype(BF16)


def score_kernel(own, o0, o1, o2, o3, o4, out):
    blocks = [b[...] for b in (own, o0, o1, o2, o3, o4)]
    for j, other in enumerate(blocks[1:]):
        out[j * LANES : (j + 1) * LANES] = dot(other, blocks[0], 0, 0).astype(BF16)
    squares = [jnp.sum(jnp.square(b.astype(F32)), axis=0, keepdims=True) for b in blocks]
    squares = jnp.concatenate(squares + [jnp.zeros((2, LANES), F32)], axis=0)
    high = squares.astype(BF16).astype(F32)
    low = (squares - high).astype(BF16).astype(F32)
    out[5 * LANES :] = jnp.concatenate((high, low), axis=0).astype(BF16)


def weight_kernel(numbers, mine, peer, o0, o1, o2, o3, o4, send, keep):
    scale, bias = numbers[0], numbers[1]
    width = o0.shape[0] // 2

    def total(start, rows):
        a = mine[start : start + rows].astype(F32)
        return a + peer[start : start + rows].astype(F32)

    squares = total(5 * LANES, 16)
    inv = lax.rsqrt(squares[:8] + squares[8:] + 1e-06)
    down = inv.T
    eye = (
        lax.broadcasted_iota(jnp.int32, (LANES, LANES), 0)
        == lax.broadcasted_iota(jnp.int32, (LANES, LANES), 1)
    ).astype(F32)
    n = inv[0:1]
    loss = along = jnp.zeros_like(n)
    d = None
    for j, other in enumerate((o0, o1, o2, o3, o4)):
        col = down[:, j + 1 : j + 2]
        c = scale * (total(j * LANES, LANES) * n * col)
        s = c + bias
        e = jnp.exp(-jnp.abs(s))
        g = jnp.where(s >= 0, 1.0, e) / (1.0 + e)
        signed = s
        if j == 0:
            signed, g = (1.0 - 2.0 * eye) * s, g - eye
        loss += jnp.sum(jnp.maximum(signed, 0.0) + jnp.log1p(e), axis=0, keepdims=True)
        along += jnp.sum(g * c, axis=0, keepdims=True)
        term = fine(other[...], g * col)
        d = term if d is None else d + term
    lines = jnp.concatenate((along, loss, n, jnp.zeros((5, LANES), F32)), axis=0)
    keep[:width], send[:width] = d[:width], d[width:]
    keep[width:], send[width:] = lines, lines


def slope_kernel(numbers, keep, got, z, slopes, send, loss):
    scale, first = numbers[0], numbers[2] > 0
    width = z.shape[0] // 2
    for side in range(2):
        own, other = (keep, got) if side == 0 else (got, keep)
        lines = jnp.where(first, own[width:], other[width:])
        along, n = lines[0:1], lines[2:3]
        if side == 0:
            loss[...] = jnp.broadcast_to(lines[1:2], loss.shape)
        d = scale * jnp.where(first, own[:width], other[:width])
        part = slice(side * width, (side + 1) * width)
        terms = two_terms((d - z[part] * (n * along)) * n)
        slopes[part] = terms
        send[part] = terms[:, :LANES]


def gradient_kernel(parts, slopes, theirs, xi, xt, beside, out):
    width, count = slopes.shape[0] // 2, xi.shape[0]
    block = xi.shape[0] // parts
    whole = width // LANES * LANES
    rest = width - whole
    fold = -(-block // 32) * 16
    tail = None
    for side, x in enumerate((xi, xt)):
        there = slice(side * count, (side + 1) * count)
        feats = jnp.concatenate((x[...], x[...], beside[there]), axis=1)
        part = slice(side * width, (side + 1) * width)
        grads = jnp.concatenate((slopes[part], theirs[part]), axis=1)
        main = dot(feats, grads[:whole], 1, 1).astype(BF16)
        for j in range(whole // LANES):
            at = (side * (whole // LANES) + j) * block
            for p in range(parts):
                out[p, at : at + block] = main[p * block : (p + 1) * block, j * LANES : (j + 1) * LANES]
        piece = grads[whole:]
        gap = jnp.zeros_like(piece)
        pieces = [gap] * (2 * LANES // rest)
        pieces[side] = pieces[LANES // rest + LANES // rest // 2 + side] = piece
        term = dot(feats, jnp.concatenate(pieces, axis=0), 1, 1)
        tail = term if tail is None else tail + term
    for p in range(parts):
        upper = tail[p * block : p * block + fold, :LANES]
        lower = tail[(p + 1) * block - fold : (p + 1) * block, LANES:]
        out[p, 2 * whole // LANES * block :] = (upper + lower).astype(BF16)


def ring_kernel(got, out):
    total = jnp.sum(got[...].astype(F32), axis=0)
    top = jnp.max(jnp.max(jnp.abs(total), axis=0, keepdims=True), axis=1, keepdims=True)
    power = jnp.floor(jnp.log2(jnp.where(top > 0, top, 1.0))) - 13.0
    power = jnp.broadcast_to(jnp.maximum(power, -120.0), (1, LANES))
    total = total * jnp.exp2(-power)
    places = out.shape[0]
    count = total.shape[0] // places
    for j in range(count):
        out[:, j] = total[j * places : (j + 1) * places]
    out[:, count] = jnp.broadcast_to(power, (places, LANES))


def order_kernel(column, xi, xt, own_i, own_t, away, turned):
    places = RING // 2
    depth, size = turned.shape[0], own_i.shape[0]
    five = 5
    nine = 2 * five - 1
    planes = size // (2 * five * places)
    block = depth // (2 * planes)
    for side, x in enumerate((xi, xt)):
        turned[...] = x[...].astype(F32).T
        for beside in range(2):
            first = (column[0] + beside) % 2 * block
            for p in range(planes):
                for q in range(2):
                    for r in range(five):
                        start = first + 2 * p * block + (five - 1) * q + r
                        rows = turned[pl.ds(start, places, stride=nine)].astype(BF16)
                        at = ((2 * p + q) * five + r) * places
                        if beside:
                            away[side * size + at : side * size + at + places] = rows
                        else:
                            (own_t if side else own_i)[at : at + places] = rows


def shares(total, width, share):
    count = width // LANES
    rest = width - count * LANES
    five = 5
    fold = total[2 * count * five : 2 * count * five + five // 2 + 1]
    half = lax.axis_index("dp") % 2
    out = []
    for side in range(2):
        pieces = [total[(side * count + j) * five : (side * count + j + 1) * five] for j in range(count)]
        top = fold[:, side * rest : (side + 1) * rest]
        low = fold[1:, (2 + side) * rest : (3 + side) * rest]
        pieces.append(jnp.concatenate((top, low), axis=0))
        flat = jnp.concatenate(pieces, axis=1).reshape(1, -1)
        out.append(jnp.where(half == 0, flat[:, :share], flat[:, flat.shape[1] - share :]))
    return out


def shards(image_feats, text_feats, image_proj, text_proj, logit_scale, logit_bias):
    rows, depth = image_feats.shape
    width = image_proj.shape[1]
    dp, tower = lax.axis_size("dp"), lax.axis_size("tower")
    planes = dp // RING
    to_core = [(t, t ^ 1) for t in range(tower)]
    to_chip = [(t, t ^ 2) for t in range(tower)]
    first = lax.axis_index("tower") % 2 == 0
    core0 = first.astype(F32)
    numbers = jnp.concatenate((logit_scale, logit_bias, core0[None]))
    scalars = pl.BlockSpec(memory_space=pltpu.SMEM)
    array = pl.BlockSpec(memory_space=pltpu.VMEM)

    here = [pltpu.VMEM((rows, depth), BF16), pltpu.VMEM((width, depth), BF16)] * 2
    z, own = pl.pallas_call(
        project_kernel,
        out_shape=(
            jax.ShapeDtypeStruct((2 * width, rows), F32),
            jax.ShapeDtypeStruct((2 * width, rows), BF16),
        ),
        in_specs=[pl.BlockSpec(memory_space=pl.ANY)] * 4,
        out_specs=(array, array),
        scratch_shapes=here + [pltpu.SemaphoreType.DMA((4,))],
        compiler_params=pltpu.CompilerParams(vmem_limit_bytes=60 * 1024 * 1024),
        name="project",
    )(image_feats, image_proj.T, text_feats, text_proj.T)
    other = lax.ppermute(own, "tower", to_core)
    i0 = jnp.concatenate((own[:width], other[:width]), axis=0)
    t0 = jnp.concatenate((own[width:], other[width:]), axis=0)
    mine, o0 = jnp.where(first, i0, t0), jnp.where(first, t0, i0)
    o2 = shifted(o0, (2, -2))
    o1 = shifted(o0, (1, -1))
    o4 = shifted(o2, (2, -2))
    o3 = shifted(o1, (2, -2))
    column = (lax.axis_index("dp") // RING % 2).astype(jnp.int32)[None]
    beside = [(i, i ^ RING) for i in range(dp)]
    image_feats, text_feats, column = lax.optimization_barrier((image_feats, text_feats, column, o0))[:3]
    size = planes * 5 * (RING // 2)
    xi, xt, away = pl.pallas_call(
        order_kernel,
        out_shape=tuple(jax.ShapeDtypeStruct((n, rows), BF16) for n in (size, size, 2 * size)),
        in_specs=[scalars, array, array],
        out_specs=(array,) * 3,
        scratch_shapes=[pltpu.VMEM((depth, rows), F32)],
        compiler_params=VMEM,
        name="order",
    )(column, image_feats, text_feats)
    x_beside = lax.ppermute(away, "dp", beside)

    scores = pl.pallas_call(
        score_kernel,
        out_shape=jax.ShapeDtypeStruct((5 * rows + 16, rows), BF16),
        in_specs=[array] * 6,
        out_specs=array,
        compiler_params=VMEM,
        name="scores",
    )(mine, o0, o1, o2, o3, o4)
    peer = lax.ppermute(scores, "tower", to_chip)
    sums = jax.ShapeDtypeStruct((width + 8, rows), F32)
    send, keep = pl.pallas_call(
        weight_kernel,
        out_shape=(sums, sums),
        in_specs=[scalars] + [array] * 7,
        out_specs=(array, array),
        compiler_params=VMEM,
        name="weights",
    )(numbers, scores, lax.optimization_barrier((peer, x_beside))[0], o0, o1, o2, o3, o4)
    got = lax.ppermute(send, "tower", to_core)
    slopes, send, loss = pl.pallas_call(
        slope_kernel,
        out_shape=(
            jax.ShapeDtypeStruct((2 * width, 2 * rows), BF16),
            jax.ShapeDtypeStruct((2 * width, rows), BF16),
            jax.ShapeDtypeStruct((8, rows), F32),
        ),
        in_specs=[scalars] + [array] * 3,
        out_specs=(array,) * 3,
        compiler_params=VMEM,
        name="slopes",
    )(numbers, keep, got, z)
    theirs = lax.ppermute(send, "dp", beside)
    parts = planes
    block = xi.shape[0] // parts
    payload = 2 * (width // LANES) * block + -(-block // 32) * 16
    grads = pl.pallas_call(
        functools.partial(gradient_kernel, parts),
        out_shape=jax.ShapeDtypeStruct((parts, payload, LANES), BF16),
        in_specs=[array] * 5,
        out_specs=array,
        compiler_params=VMEM,
        name="gradients",
    )(slopes, theirs, xi, xt, x_beside)

    places = RING // 2
    groups = [
        [(2 * y + x) * RING + 2 * m + q for y in range(planes // 2) for q in range(2)]
        for x in range(2)
        for m in range(places)
    ]
    grads = lax.all_to_all(grads, "dp", 0, 0, axis_index_groups=groups, tiled=True)
    sent = pl.pallas_call(
        ring_kernel,
        out_shape=jax.ShapeDtypeStruct((places, payload // places + 1, LANES), F32),
        in_specs=[array],
        out_specs=array,
        compiler_params=VMEM,
        name="ring",
    )(grads)
    groups = [
        [g * RING + 2 * m + q for m in range(places)] for g in range(planes) for q in range(2)
    ]
    sent = sent.astype(jnp.float16)
    back = lax.all_to_all(sent, "dp", 0, 0, axis_index_groups=groups, tiled=True).astype(F32)
    total = jnp.sum(back * jnp.exp2(back[:, -1:]), axis=0)
    image_grad, text_grad = shares(total, width, depth * width // dp)
    return (loss[0], image_grad, text_grad)


def solution(mesh):
    in_specs = (P("dp", None), P("dp", None), P(None, "tower"), P(None, "tower"), P(), P())
    out_specs = (P("dp"), P("tower", "dp"), P("tower", "dp"))
    return jax.shard_map(shards, mesh=mesh, in_specs=in_specs, out_specs=out_specs, check_vma=False)
```

```python
import functools

import jax
import jax.numpy as jnp
from jax import lax
from jax.experimental import pallas as pl
from jax.experimental.pallas import tpu as pltpu
from jax.sharding import PartitionSpec as P

RING = 32
LANES = 128
BF16, F32 = jnp.bfloat16, jnp.float32
VMEM = pltpu.CompilerParams(vmem_limit_bytes=32 * 1024 * 1024)


def dot(left, right, over_left, over_right):
    return lax.dot_general(
        left, right, (((over_left,), (over_right,)), ((), ())), preferred_element_type=F32
    )


def two_terms(x):
    high = x.astype(BF16)
    return jnp.concatenate((high, (x - high.astype(F32)).astype(BF16)), axis=1)


def fine(block, weights):
    both = dot(block, two_terms(weights), 1, 0)
    return both[:, :LANES] + both[:, LANES:]


def shifted(block, distances):
    dp, tower = lax.axis_size("dp"), lax.axis_size("tower")
    route = [
        (i * tower + t, ((i + distances[t % 2]) % dp) * tower + t)
        for i in range(dp)
        for t in range(tower)
    ]
    return lax.ppermute(block, ("dp", "tower"), route)


def project_kernel(xi, wi, xt, wt, z, own, xi_here, wi_here, xt_here, wt_here, arrived):
    moves = [
        pltpu.make_async_copy(there, here, arrived.at[j])
        for j, (there, here) in enumerate(
            ((xi, xi_here), (wi, wi_here), (xt, xt_here), (wt, wt_here))
        )
    ]
    for move in moves:
        move.start()
    width = wi_here.shape[0]
    for side, (x, w) in enumerate(((xi_here, wi_here), (xt_here, wt_here))):
        moves[2 * side].wait()
        moves[2 * side + 1].wait()
        part = dot(w[...], x[...], 1, 1)
        z[side * width : (side + 1) * width] = part
        own[side * width : (side + 1) * width] = part.astype(BF16)


def score_kernel(own, o0, o1, o2, o3, o4, out):
    blocks = [b[...] for b in (own, o0, o1, o2, o3, o4)]
    for j, other in enumerate(blocks[1:]):
        out[j * LANES : (j + 1) * LANES] = dot(other, blocks[0], 0, 0).astype(BF16)
    squares = [jnp.sum(jnp.square(b.astype(F32)), axis=0, keepdims=True) for b in blocks]
    squares = jnp.concatenate(squares + [jnp.zeros((2, LANES), F32)], axis=0)
    high = squares.astype(BF16).astype(F32)
    low = (squares - high).astype(BF16).astype(F32)
    out[5 * LANES :] = jnp.concatenate((high, low), axis=0).astype(BF16)


def weight_kernel(numbers, mine, peer, o0, o1, o2, o3, o4, send, keep):
    scale, bias = numbers[0], numbers[1]
    width = o0.shape[0] // 2

    def total(start, rows):
        a = mine[start : start + rows].astype(F32)
        return a + peer[start : start + rows].astype(F32)

    squares = total(5 * LANES, 16)
    inv = lax.rsqrt(squares[:8] + squares[8:] + 1e-06)
    down = inv.T
    eye = (
        lax.broadcasted_iota(jnp.int32, (LANES, LANES), 0)
        == lax.broadcasted_iota(jnp.int32, (LANES, LANES), 1)
    ).astype(F32)
    n = inv[0:1]
    loss = along = jnp.zeros_like(n)
    d = None
    for j, other in enumerate((o0, o1, o2, o3, o4)):
        col = down[:, j + 1 : j + 2]
        c = scale * (total(j * LANES, LANES) * n * col)
        s = c + bias
        e = jnp.exp(-jnp.abs(s))
        g = jnp.where(s >= 0, 1.0, e) / (1.0 + e)
        signed = s
        if j == 0:
            signed, g = (1.0 - 2.0 * eye) * s, g - eye
        loss += jnp.sum(jnp.maximum(signed, 0.0) + jnp.log1p(e), axis=0, keepdims=True)
        along += jnp.sum(g * c, axis=0, keepdims=True)
        term = fine(other[...], g * col)
        d = term if d is None else d + term
    lines = jnp.concatenate((along, loss, n, jnp.zeros((5, LANES), F32)), axis=0)
    keep[:width], send[:width] = d[:width], d[width:]
    keep[width:], send[width:] = lines, lines


def slope_kernel(numbers, keep, got, z, slopes, send, loss):
    scale, first = numbers[0], numbers[2] > 0
    width = z.shape[0] // 2
    for side in range(2):
        own, other = (keep, got) if side == 0 else (got, keep)
        lines = jnp.where(first, own[width:], other[width:])
        along, n = lines[0:1], lines[2:3]
        if side == 0:
            loss[...] = jnp.broadcast_to(lines[1:2], loss.shape)
        d = scale * jnp.where(first, own[:width], other[:width])
        part = slice(side * width, (side + 1) * width)
        terms = two_terms((d - z[part] * (n * along)) * n)
        slopes[part] = terms
        send[part] = terms[:, :LANES]


def gradient_kernel(parts, slopes, theirs, xi, xt, beside, out):
    width, count = slopes.shape[0] // 2, xi.shape[0]
    block = xi.shape[0] // parts
    whole = width // LANES * LANES
    rest = width - whole
    fold = -(-block // 32) * 16
    tail = None
    for side, x in enumerate((xi, xt)):
        there = slice(side * count, (side + 1) * count)
        feats = jnp.concatenate((x[...], x[...], beside[there]), axis=1)
        part = slice(side * width, (side + 1) * width)
        grads = jnp.concatenate((slopes[part], theirs[part]), axis=1)
        main = dot(feats, grads[:whole], 1, 1).astype(BF16)
        for j in range(whole // LANES):
            at = (side * (whole // LANES) + j) * block
            for p in range(parts):
                out[p, at : at + block] = main[p * block : (p + 1) * block, j * LANES : (j + 1) * LANES]
        piece = grads[whole:]
        gap = jnp.zeros_like(piece)
        pieces = [gap] * (2 * LANES // rest)
        pieces[side] = pieces[LANES // rest + LANES // rest // 2 + side] = piece
        term = dot(feats, jnp.concatenate(pieces, axis=0), 1, 1)
        tail = term if tail is None else tail + term
    for p in range(parts):
        upper = tail[p * block : p * block + fold, :LANES]
        lower = tail[(p + 1) * block - fold : (p + 1) * block, LANES:]
        out[p, 2 * whole // LANES * block :] = (upper + lower).astype(BF16)


def ring_kernel(got, out):
    total = jnp.sum(got[...].astype(F32), axis=0)
    top = jnp.max(jnp.max(jnp.abs(total), axis=0, keepdims=True), axis=1, keepdims=True)
    power = jnp.floor(jnp.log2(jnp.where(top > 0, top, 1.0))) - 13.0
    power = jnp.broadcast_to(jnp.maximum(power, -120.0), (1, LANES))
    total = total * jnp.exp2(-power)
    places = out.shape[0]
    count = total.shape[0] // places
    for j in range(count):
        out[:, j] = total[j * places : (j + 1) * places]
    out[:, count] = jnp.broadcast_to(power, (places, LANES))


def order_kernel(column, xi, xt, own_i, own_t, away, turned):
    places = RING // 2
    depth, size = turned.shape[0], own_i.shape[0]
    five = 5
    nine = 2 * five - 1
    planes = size // (2 * five * places)
    block = depth // (2 * planes)
    for side, x in enumerate((xi, xt)):
        turned[...] = x[...].astype(F32).T
        for beside in range(2):
            first = (column[0] + beside) % 2 * block
            for p in range(planes):
                for q in range(2):
                    for r in range(five):
                        start = first + 2 * p * block + (five - 1) * q + r
                        rows = turned[pl.ds(start, places, stride=nine)].astype(BF16)
                        at = ((2 * p + q) * five + r) * places
                        if beside:
                            away[side * size + at : side * size + at + places] = rows
                        else:
                            (own_t if side else own_i)[at : at + places] = rows


def shares(total, width, share):
    count = width // LANES
    rest = width - count * LANES
    five = 5
    fold = total[2 * count * five : 2 * count * five + five // 2 + 1]
    half = lax.axis_index("dp") % 2
    out = []
    for side in range(2):
        pieces = [total[(side * count + j) * five : (side * count + j + 1) * five] for j in range(count)]
        top = fold[:, side * rest : (side + 1) * rest]
        low = fold[1:, (2 + side) * rest : (3 + side) * rest]
        pieces.append(jnp.concatenate((top, low), axis=0))
        flat = jnp.concatenate(pieces, axis=1).reshape(1, -1)
        out.append(jnp.where(half == 0, flat[:, :share], flat[:, flat.shape[1] - share :]))
    return out


def shards(image_feats, text_feats, image_proj, text_proj, logit_scale, logit_bias):
    rows, depth = image_feats.shape
    width = image_proj.shape[1]
    dp, tower = lax.axis_size("dp"), lax.axis_size("tower")
    planes = dp // RING
    to_core = [(t, t ^ 1) for t in range(tower)]
    to_chip = [(t, t ^ 2) for t in range(tower)]
    first = lax.axis_index("tower") % 2 == 0
    core0 = first.astype(F32)
    numbers = jnp.concatenate((logit_scale, logit_bias, core0[None]))
    scalars = pl.BlockSpec(memory_space=pltpu.SMEM)
    array = pl.BlockSpec(memory_space=pltpu.VMEM)

    here = [pltpu.VMEM((rows, depth), BF16), pltpu.VMEM((width, depth), BF16)] * 2
    z, own = pl.pallas_call(
        project_kernel,
        out_shape=(
            jax.ShapeDtypeStruct((2 * width, rows), F32),
            jax.ShapeDtypeStruct((2 * width, rows), BF16),
        ),
        in_specs=[pl.BlockSpec(memory_space=pl.ANY)] * 4,
        out_specs=(array, array),
        scratch_shapes=here + [pltpu.SemaphoreType.DMA((4,))],
        compiler_params=pltpu.CompilerParams(vmem_limit_bytes=60 * 1024 * 1024),
        name="project",
    )(image_feats, image_proj.T, text_feats, text_proj.T)
    other = lax.ppermute(own, "tower", to_core)
    i0 = jnp.concatenate((own[:width], other[:width]), axis=0)
    t0 = jnp.concatenate((own[width:], other[width:]), axis=0)
    mine, o0 = jnp.where(first, i0, t0), jnp.where(first, t0, i0)
    o2 = shifted(o0, (2, -2))
    o1 = shifted(o0, (1, -1))
    o4 = shifted(o2, (2, -2))
    o3 = shifted(o1, (2, -2))
    column = (lax.axis_index("dp") // RING % 2).astype(jnp.int32)[None]
    beside = [(i, i ^ RING) for i in range(dp)]
    image_feats, text_feats, column = lax.optimization_barrier((image_feats, text_feats, column, o1))[:3]
    size = planes * 5 * (RING // 2)
    xi, xt, away = pl.pallas_call(
        order_kernel,
        out_shape=tuple(jax.ShapeDtypeStruct((n, rows), BF16) for n in (size, size, 2 * size)),
        in_specs=[scalars, array, array],
        out_specs=(array,) * 3,
        scratch_shapes=[pltpu.VMEM((depth, rows), F32)],
        compiler_params=VMEM,
        name="order",
    )(column, image_feats, text_feats)
    x_beside = lax.ppermute(away, "dp", beside)
    scores = pl.pallas_call(
        score_kernel,
        out_shape=jax.ShapeDtypeStruct((5 * rows + 16, rows), BF16),
        in_specs=[array] * 6,
        out_specs=array,
        compiler_params=VMEM,
        name="scores",
    )(mine, o0, o1, o2, o3, o4)
    peer = lax.ppermute(scores, "tower", to_chip)
    sums = jax.ShapeDtypeStruct((width + 8, rows), F32)
    send, keep = pl.pallas_call(
        weight_kernel,
        out_shape=(sums, sums),
        in_specs=[scalars] + [array] * 7,
        out_specs=(array, array),
        compiler_params=VMEM,
        name="weights",
    )(numbers, scores, peer, o0, o1, o2, o3, o4)
    got = lax.ppermute(send, "tower", to_core)
    got, x_beside = lax.optimization_barrier((got, x_beside))
    slopes, send, loss = pl.pallas_call(
        slope_kernel,
        out_shape=(
            jax.ShapeDtypeStruct((2 * width, 2 * rows), BF16),
            jax.ShapeDtypeStruct((2 * width, rows), BF16),
            jax.ShapeDtypeStruct((8, rows), F32),
        ),
        in_specs=[scalars] + [array] * 3,
        out_specs=(array,) * 3,
        compiler_params=VMEM,
        name="slopes",
    )(numbers, keep, got, z)
    theirs = lax.ppermute(send, "dp", beside)
    parts = planes
    block = xi.shape[0] // parts
    payload = 2 * (width // LANES) * block + -(-block // 32) * 16
    grads = pl.pallas_call(
        functools.partial(gradient_kernel, parts),
        out_shape=jax.ShapeDtypeStruct((parts, payload, LANES), BF16),
        in_specs=[array] * 5,
        out_specs=array,
        compiler_params=VMEM,
        name="gradients",
    )(slopes, theirs, xi, xt, x_beside)

    places = RING // 2
    groups = [
        [(2 * y + x) * RING + 2 * m + q for y in range(planes // 2) for q in range(2)]
        for x in range(2)
        for m in range(places)
    ]
    grads = lax.all_to_all(grads, "dp", 0, 0, axis_index_groups=groups, tiled=True)
    sent = pl.pallas_call(
        ring_kernel,
        out_shape=jax.ShapeDtypeStruct((places, payload // places + 1, LANES), F32),
        in_specs=[array],
        out_specs=array,
        compiler_params=VMEM,
        name="ring",
    )(grads)
    groups = [
        [g * RING + 2 * m + q for m in range(places)] for g in range(planes) for q in range(2)
    ]
    sent = sent.astype(jnp.float16)
    back = lax.all_to_all(sent, "dp", 0, 0, axis_index_groups=groups, tiled=True).astype(F32)
    total = jnp.sum(back * jnp.exp2(back[:, -1:]), axis=0)
    image_grad, text_grad = shares(total, width, depth * width // dp)
    return (loss[0], image_grad, text_grad)


def solution(mesh):
    in_specs = (P("dp", None), P("dp", None), P(None, "tower"), P(None, "tower"), P(), P())
    out_specs = (P("dp"), P("tower", "dp"), P("tower", "dp"))
    return jax.shard_map(shards, mesh=mesh, in_specs=in_specs, out_specs=out_specs, check_vma=False)
```

```python
import functools

import jax
import jax.numpy as jnp
from jax import lax
from jax.experimental import pallas as pl
from jax.experimental.pallas import tpu as pltpu
from jax.sharding import PartitionSpec as P

RING = 32
LANES = 128
BF16, F32 = jnp.bfloat16, jnp.float32
VMEM = pltpu.CompilerParams(vmem_limit_bytes=32 * 1024 * 1024)


def dot(left, right, over_left, over_right):
    return lax.dot_general(
        left, right, (((over_left,), (over_right,)), ((), ())), preferred_element_type=F32
    )


def two_terms(x):
    high = x.astype(BF16)
    return jnp.concatenate((high, (x - high.astype(F32)).astype(BF16)), axis=1)


def fine(block, weights):
    both = dot(block, two_terms(weights), 1, 0)
    return both[:, :LANES] + both[:, LANES:]


def shifted(block, distances):
    dp, tower = lax.axis_size("dp"), lax.axis_size("tower")
    route = [
        (i * tower + t, ((i + distances[t % 2]) % dp) * tower + t)
        for i in range(dp)
        for t in range(tower)
    ]
    return lax.ppermute(block, ("dp", "tower"), route)


def project_kernel(xi, wi, xt, wt, z, own, xi_here, wi_here, xt_here, wt_here, arrived):
    moves = [
        pltpu.make_async_copy(there, here, arrived.at[j])
        for j, (there, here) in enumerate(
            ((xi, xi_here), (wi, wi_here), (xt, xt_here), (wt, wt_here))
        )
    ]
    for move in moves:
        move.start()
    width = wi_here.shape[0]
    for side, (x, w) in enumerate(((xi_here, wi_here), (xt_here, wt_here))):
        moves[2 * side].wait()
        moves[2 * side + 1].wait()
        part = dot(w[...], x[...], 1, 1)
        z[side * width : (side + 1) * width] = part
        own[side * width : (side + 1) * width] = part.astype(BF16)


def score_kernel(own, o0, o1, o2, o3, o4, out):
    blocks = [b[...] for b in (own, o0, o1, o2, o3, o4)]
    for j, other in enumerate(blocks[1:]):
        out[j * LANES : (j + 1) * LANES] = dot(other, blocks[0], 0, 0).astype(BF16)
    squares = [jnp.sum(jnp.square(b.astype(F32)), axis=0, keepdims=True) for b in blocks]
    squares = jnp.concatenate(squares + [jnp.zeros((2, LANES), F32)], axis=0)
    high = squares.astype(BF16).astype(F32)
    low = (squares - high).astype(BF16).astype(F32)
    out[5 * LANES :] = jnp.concatenate((high, low), axis=0).astype(BF16)


def weight_kernel(numbers, mine, peer, o0, o1, o2, o3, o4, send, keep):
    scale, bias = numbers[0], numbers[1]
    width = o0.shape[0] // 2

    def total(start, rows):
        a = mine[start : start + rows].astype(F32)
        return a + peer[start : start + rows].astype(F32)

    squares = total(5 * LANES, 16)
    inv = lax.rsqrt(squares[:8] + squares[8:] + 1e-06)
    down = inv.T
    eye = (
        lax.broadcasted_iota(jnp.int32, (LANES, LANES), 0)
        == lax.broadcasted_iota(jnp.int32, (LANES, LANES), 1)
    ).astype(F32)
    n = inv[0:1]
    loss = along = jnp.zeros_like(n)
    d = None
    for j, other in enumerate((o0, o1, o2, o3, o4)):
        col = down[:, j + 1 : j + 2]
        c = scale * (total(j * LANES, LANES) * n * col)
        s = c + bias
        e = jnp.exp(-jnp.abs(s))
        g = jnp.where(s >= 0, 1.0, e) / (1.0 + e)
        signed = s
        if j == 0:
            signed, g = (1.0 - 2.0 * eye) * s, g - eye
        loss += jnp.sum(jnp.maximum(signed, 0.0) + jnp.log1p(e), axis=0, keepdims=True)
        along += jnp.sum(g * c, axis=0, keepdims=True)
        term = fine(other[...], g * col)
        d = term if d is None else d + term
    lines = jnp.concatenate((along, loss, n, jnp.zeros((5, LANES), F32)), axis=0)
    keep[:width], send[:width] = d[:width], d[width:]
    keep[width:], send[width:] = lines, lines


def slope_kernel(numbers, keep, got, z, slopes, send, loss):
    scale, first = numbers[0], numbers[2] > 0
    width = z.shape[0] // 2
    for side in range(2):
        own, other = (keep, got) if side == 0 else (got, keep)
        lines = jnp.where(first, own[width:], other[width:])
        along, n = lines[0:1], lines[2:3]
        if side == 0:
            loss[...] = jnp.broadcast_to(lines[1:2], loss.shape)
        d = scale * jnp.where(first, own[:width], other[:width])
        part = slice(side * width, (side + 1) * width)
        terms = two_terms((d - z[part] * (n * along)) * n)
        slopes[part] = terms
        send[part] = terms[:, :LANES]


def gradient_kernel(parts, slopes, theirs, xi, xt, beside, out):
    width, count = slopes.shape[0] // 2, xi.shape[0]
    block = xi.shape[0] // parts
    whole = width // LANES * LANES
    rest = width - whole
    fold = -(-block // 32) * 16
    tail = None
    for side, x in enumerate((xi, xt)):
        there = slice(side * count, (side + 1) * count)
        feats = jnp.concatenate((x[...], x[...], beside[there]), axis=1)
        part = slice(side * width, (side + 1) * width)
        grads = jnp.concatenate((slopes[part], theirs[part]), axis=1)
        main = dot(feats, grads[:whole], 1, 1).astype(BF16)
        for j in range(whole // LANES):
            at = (side * (whole // LANES) + j) * block
            for p in range(parts):
                out[p, at : at + block] = main[p * block : (p + 1) * block, j * LANES : (j + 1) * LANES]
        piece = grads[whole:]
        gap = jnp.zeros_like(piece)
        pieces = [gap] * (2 * LANES // rest)
        pieces[side] = pieces[LANES // rest + LANES // rest // 2 + side] = piece
        term = dot(feats, jnp.concatenate(pieces, axis=0), 1, 1)
        tail = term if tail is None else tail + term
    for p in range(parts):
        upper = tail[p * block : p * block + fold, :LANES]
        lower = tail[(p + 1) * block - fold : (p + 1) * block, LANES:]
        out[p, 2 * whole // LANES * block :] = (upper + lower).astype(BF16)


def ring_kernel(got, out):
    total = jnp.sum(got[...].astype(F32), axis=0)
    top = jnp.max(jnp.max(jnp.abs(total), axis=0, keepdims=True), axis=1, keepdims=True)
    power = jnp.floor(jnp.log2(jnp.where(top > 0, top, 1.0))) - 13.0
    power = jnp.broadcast_to(jnp.maximum(power, -120.0), (1, LANES))
    total = total * jnp.exp2(-power)
    places = out.shape[0]
    count = total.shape[0] // places
    for j in range(count):
        middle = j * places + places // 2
        out[: places // 2, j] = total[middle : (j + 1) * places]
        out[places // 2 :, j] = total[j * places : middle]
    out[:, count] = jnp.broadcast_to(power, (places, LANES))


def order_kernel(column, xi, xt, own_i, own_t, away, turned):
    places = RING // 2
    depth, size = turned.shape[0], own_i.shape[0]
    five = 5
    nine = 2 * five - 1
    planes = size // (2 * five * places)
    block = depth // (2 * planes)
    for side, x in enumerate((xi, xt)):
        turned[...] = x[...].astype(F32).T
        for beside in range(2):
            first = (column[0] + beside) % 2 * block
            for p in range(planes):
                for q in range(2):
                    for r in range(five):
                        start = first + 2 * p * block + (five - 1) * q + r
                        rows = turned[pl.ds(start, places, stride=nine)].astype(BF16)
                        at = ((2 * p + q) * five + r) * places
                        if beside:
                            away[side * size + at : side * size + at + places] = rows
                        else:
                            (own_t if side else own_i)[at : at + places] = rows


def shares(total, width, share):
    count = width // LANES
    rest = width - count * LANES
    five = 5
    fold = total[2 * count * five : 2 * count * five + five // 2 + 1]
    half = lax.axis_index("dp") % 2
    out = []
    for side in range(2):
        pieces = [total[(side * count + j) * five : (side * count + j + 1) * five] for j in range(count)]
        top = fold[:, side * rest : (side + 1) * rest]
        low = fold[1:, (2 + side) * rest : (3 + side) * rest]
        pieces.append(jnp.concatenate((top, low), axis=0))
        flat = jnp.concatenate(pieces, axis=1).reshape(1, -1)
        out.append(jnp.where(half == 0, flat[:, :share], flat[:, flat.shape[1] - share :]))
    return out


def shards(image_feats, text_feats, image_proj, text_proj, logit_scale, logit_bias):
    rows, depth = image_feats.shape
    width = image_proj.shape[1]
    dp, tower = lax.axis_size("dp"), lax.axis_size("tower")
    planes = dp // RING
    to_core = [(t, t ^ 1) for t in range(tower)]
    to_chip = [(t, t ^ 2) for t in range(tower)]
    first = lax.axis_index("tower") % 2 == 0
    core0 = first.astype(F32)
    numbers = jnp.concatenate((logit_scale, logit_bias, core0[None]))
    scalars = pl.BlockSpec(memory_space=pltpu.SMEM)
    array = pl.BlockSpec(memory_space=pltpu.VMEM)

    here = [pltpu.VMEM((rows, depth), BF16), pltpu.VMEM((width, depth), BF16)] * 2
    z, own = pl.pallas_call(
        project_kernel,
        out_shape=(
            jax.ShapeDtypeStruct((2 * width, rows), F32),
            jax.ShapeDtypeStruct((2 * width, rows), BF16),
        ),
        in_specs=[pl.BlockSpec(memory_space=pl.ANY)] * 4,
        out_specs=(array, array),
        scratch_shapes=here + [pltpu.SemaphoreType.DMA((4,))],
        compiler_params=pltpu.CompilerParams(vmem_limit_bytes=60 * 1024 * 1024),
        name="project",
    )(image_feats, image_proj.T, text_feats, text_proj.T)
    other = lax.ppermute(own, "tower", to_core)
    i0 = jnp.concatenate((own[:width], other[:width]), axis=0)
    t0 = jnp.concatenate((own[width:], other[width:]), axis=0)
    mine, o0 = jnp.where(first, i0, t0), jnp.where(first, t0, i0)
    o2 = shifted(o0, (2, -2))
    o1 = shifted(o0, (1, -1))
    o4 = shifted(o2, (2, -2))
    o3 = shifted(o1, (2, -2))
    column = (lax.axis_index("dp") // RING % 2).astype(jnp.int32)[None]
    beside = [(i, i ^ RING) for i in range(dp)]
    image_feats, text_feats, column = lax.optimization_barrier((image_feats, text_feats, column, o0))[:3]
    size = planes * 5 * (RING // 2)
    xi, xt, away = pl.pallas_call(
        order_kernel,
        out_shape=tuple(jax.ShapeDtypeStruct((n, rows), BF16) for n in (size, size, 2 * size)),
        in_specs=[scalars, array, array],
        out_specs=(array,) * 3,
        scratch_shapes=[pltpu.VMEM((depth, rows), F32)],
        compiler_params=VMEM,
        name="order",
    )(column, image_feats, text_feats)
    x_beside = lax.ppermute(away, "dp", beside)

    scores = pl.pallas_call(
        score_kernel,
        out_shape=jax.ShapeDtypeStruct((5 * rows + 16, rows), BF16),
        in_specs=[array] * 6,
        out_specs=array,
        compiler_params=VMEM,
        name="scores",
    )(mine, o0, o1, o2, o3, o4)
    peer = lax.ppermute(scores, "tower", to_chip)
    sums = jax.ShapeDtypeStruct((width + 8, rows), F32)
    send, keep = pl.pallas_call(
        weight_kernel,
        out_shape=(sums, sums),
        in_specs=[scalars] + [array] * 7,
        out_specs=(array, array),
        compiler_params=VMEM,
        name="weights",
    )(numbers, scores, lax.optimization_barrier((peer, x_beside))[0], o0, o1, o2, o3, o4)
    got = lax.ppermute(send, "tower", to_core)
    slopes, send, loss = pl.pallas_call(
        slope_kernel,
        out_shape=(
            jax.ShapeDtypeStruct((2 * width, 2 * rows), BF16),
            jax.ShapeDtypeStruct((2 * width, rows), BF16),
            jax.ShapeDtypeStruct((8, rows), F32),
        ),
        in_specs=[scalars] + [array] * 3,
        out_specs=(array,) * 3,
        compiler_params=VMEM,
        name="slopes",
    )(numbers, keep, got, z)
    theirs = lax.ppermute(send, "dp", beside)
    parts = planes
    block = xi.shape[0] // parts
    payload = 2 * (width // LANES) * block + -(-block // 32) * 16
    grads = pl.pallas_call(
        functools.partial(gradient_kernel, parts),
        out_shape=jax.ShapeDtypeStruct((parts, payload, LANES), BF16),
        in_specs=[array] * 5,
        out_specs=array,
        compiler_params=VMEM,
        name="gradients",
    )(slopes, theirs, xi, xt, x_beside)

    places = RING // 2
    groups = [
        [(2 * y + x) * RING + 2 * m + q for y in range(planes // 2) for q in range(2)]
        for x in range(2)
        for m in range(places)
    ]
    grads = lax.all_to_all(grads, "dp", 0, 0, axis_index_groups=groups, tiled=True)
    sent = pl.pallas_call(
        ring_kernel,
        out_shape=jax.ShapeDtypeStruct((places, payload // places + 1, LANES), F32),
        in_specs=[array],
        out_specs=array,
        compiler_params=VMEM,
        name="ring",
    )(grads)
    groups = [
        [g * RING + (2 * m + places) % RING + q for m in range(places)]
        for g in range(planes)
        for q in range(2)
    ]
    sent = sent.astype(jnp.float16)
    back = lax.all_to_all(sent, "dp", 0, 0, axis_index_groups=groups, tiled=True).astype(F32)
    total = jnp.sum(back * jnp.exp2(back[:, -1:]), axis=0)
    image_grad, text_grad = shares(total, width, depth * width // dp)
    return (loss[0], image_grad, text_grad)


def solution(mesh):
    in_specs = (P("dp", None), P("dp", None), P(None, "tower"), P(None, "tower"), P(), P())
    out_specs = (P("dp"), P("tower", "dp"), P("tower", "dp"))
    return jax.shard_map(shards, mesh=mesh, in_specs=in_specs, out_specs=out_specs, check_vma=False)
```

```python
import functools

import jax
import jax.numpy as jnp
from jax import lax
from jax.experimental import pallas as pl
from jax.experimental.pallas import tpu as pltpu
from jax.sharding import PartitionSpec as P

RING = 32
LANES = 128
BF16, F32 = jnp.bfloat16, jnp.float32
VMEM = pltpu.CompilerParams(vmem_limit_bytes=32 * 1024 * 1024)


def dot(left, right, over_left, over_right):
    return lax.dot_general(
        left, right, (((over_left,), (over_right,)), ((), ())), preferred_element_type=F32
    )


def two_terms(x):
    high = x.astype(BF16)
    return jnp.concatenate((high, (x - high.astype(F32)).astype(BF16)), axis=1)


def fine(block, weights):
    both = dot(block, two_terms(weights), 1, 0)
    return both[:, :LANES] + both[:, LANES:]


def shifted(block, distances):
    dp, tower = lax.axis_size("dp"), lax.axis_size("tower")
    route = [
        (i * tower + t, ((i + distances[t % 2]) % dp) * tower + t)
        for i in range(dp)
        for t in range(tower)
    ]
    return lax.ppermute(block, ("dp", "tower"), route)


def project_kernel(xi, wi, xt, wt, z, own, xi_here, wi_here, xt_here, wt_here, arrived):
    moves = [
        pltpu.make_async_copy(there, here, arrived.at[j])
        for j, (there, here) in enumerate(
            ((xi, xi_here), (wi, wi_here), (xt, xt_here), (wt, wt_here))
        )
    ]
    for move in moves:
        move.start()
    width = wi_here.shape[0]
    for side, (x, w) in enumerate(((xi_here, wi_here), (xt_here, wt_here))):
        moves[2 * side].wait()
        moves[2 * side + 1].wait()
        part = dot(w[...], x[...], 1, 1)
        z[side * width : (side + 1) * width] = part
        own[side * width : (side + 1) * width] = part.astype(BF16)


def score_kernel(count, own, *refs):
    blocks, out = [b[...] for b in (own,) + refs[:count]], refs[count]
    for j, other in enumerate(blocks[1:]):
        out[j * LANES : (j + 1) * LANES] = dot(other, blocks[0], 0, 0).astype(BF16)
    squares = [jnp.sum(jnp.square(b.astype(F32)), axis=0, keepdims=True) for b in blocks]
    squares = jnp.concatenate(squares + [jnp.zeros((7 - count, LANES), F32)], axis=0)
    high = squares.astype(BF16).astype(F32)
    low = (squares - high).astype(BF16).astype(F32)
    out[count * LANES :] = jnp.concatenate((high, low), axis=0).astype(BF16)


def weigh(numbers, mine, peer, others, paired, d, along, loss):
    scale, bias = numbers[0], numbers[1]

    def total(start, rows):
        a = mine[start : start + rows].astype(F32)
        return a + peer[start : start + rows].astype(F32)

    squares = total(len(others) * LANES, 16)
    inv = lax.rsqrt(squares[:8] + squares[8:] + 1e-06)
    down = inv.T
    n = inv[0:1]
    for j, other in enumerate(others):
        col = down[:, j + 1 : j + 2]
        c = scale * (total(j * LANES, LANES) * n * col)
        s = c + bias
        e = jnp.exp(-jnp.abs(s))
        g = jnp.where(s >= 0, 1.0, e) / (1.0 + e)
        signed = s
        if paired and j == 0:
            eye = (
                lax.broadcasted_iota(jnp.int32, (LANES, LANES), 0)
                == lax.broadcasted_iota(jnp.int32, (LANES, LANES), 1)
            ).astype(F32)
            signed, g = (1.0 - 2.0 * eye) * s, g - eye
        terms = (
            fine(other[...], g * col),
            jnp.sum(g * c, axis=0, keepdims=True),
            jnp.sum(jnp.maximum(signed, 0.0) + jnp.log1p(e), axis=0, keepdims=True),
        )
        if d is None:
            d, along, loss = terms
        else:
            d, along, loss = d + terms[0], along + terms[1], loss + terms[2]
    return d, along, loss, n


def near_kernel(numbers, mine, peer, o0, o1, o2, d_out, lines):
    d, along, loss, n = weigh(numbers, mine, peer, (o0, o1, o2), True, None, None, None)
    d_out[...] = d
    lines[...] = jnp.concatenate((along, loss, n, jnp.zeros((5, LANES), F32)), axis=0)


def far_kernel(numbers, mine, peer, d_in, near, o3, o4, send, keep):
    width = d_in.shape[0] // 2
    d, along, loss, _ = weigh(
        numbers, mine, peer, (o3, o4), False, d_in[...], near[0:1], near[1:2]
    )
    lines = jnp.concatenate((along, loss, near[2:8]), axis=0)
    keep[:width], send[:width] = d[:width], d[width:]
    keep[width:], send[width:] = lines, lines


def slope_kernel(numbers, keep, got, z, slopes, send, loss):
    scale, first = numbers[0], numbers[2] > 0
    width = z.shape[0] // 2
    for side in range(2):
        own, other = (keep, got) if side == 0 else (got, keep)
        lines = jnp.where(first, own[width:], other[width:])
        along, n = lines[0:1], lines[2:3]
        if side == 0:
            loss[...] = jnp.broadcast_to(lines[1:2], loss.shape)
        d = scale * jnp.where(first, own[:width], other[:width])
        part = slice(side * width, (side + 1) * width)
        terms = two_terms((d - z[part] * (n * along)) * n)
        slopes[part] = terms
        send[part] = terms[:, :LANES]


def gradient_kernel(parts, slopes, theirs, xi, xt, beside, out):
    width, count = slopes.shape[0] // 2, xi.shape[0]
    block = xi.shape[0] // parts
    whole = width // LANES * LANES
    rest = width - whole
    fold = -(-block // 32) * 16
    tail = None
    for side, x in enumerate((xi, xt)):
        there = slice(side * count, (side + 1) * count)
        feats = jnp.concatenate((x[...], x[...], beside[there]), axis=1)
        part = slice(side * width, (side + 1) * width)
        grads = jnp.concatenate((slopes[part], theirs[part]), axis=1)
        main = dot(feats, grads[:whole], 1, 1).astype(BF16)
        for j in range(whole // LANES):
            at = (side * (whole // LANES) + j) * block
            for p in range(parts):
                out[p, at : at + block] = main[p * block : (p + 1) * block, j * LANES : (j + 1) * LANES]
        piece = grads[whole:]
        gap = jnp.zeros_like(piece)
        pieces = [gap] * (2 * LANES // rest)
        pieces[side] = pieces[LANES // rest + LANES // rest // 2 + side] = piece
        term = dot(feats, jnp.concatenate(pieces, axis=0), 1, 1)
        tail = term if tail is None else tail + term
    for p in range(parts):
        upper = tail[p * block : p * block + fold, :LANES]
        lower = tail[(p + 1) * block - fold : (p + 1) * block, LANES:]
        out[p, 2 * whole // LANES * block :] = (upper + lower).astype(BF16)


def ring_kernel(got, out):
    total = jnp.sum(got[...].astype(F32), axis=0)
    top = jnp.max(jnp.max(jnp.abs(total), axis=0, keepdims=True), axis=1, keepdims=True)
    power = jnp.floor(jnp.log2(jnp.where(top > 0, top, 1.0))) - 13.0
    power = jnp.broadcast_to(jnp.maximum(power, -120.0), (1, LANES))
    total = total * jnp.exp2(-power)
    places = out.shape[0]
    count = total.shape[0] // places
    for j in range(count):
        middle = j * places + places // 2
        out[: places // 2, j] = total[middle : (j + 1) * places]
        out[places // 2 :, j] = total[j * places : middle]
    out[:, count] = jnp.broadcast_to(power, (places, LANES))


def order_kernel(column, xi, xt, own_i, own_t, away, turned):
    places = RING // 2
    depth, size = turned.shape[0], own_i.shape[0]
    five = 5
    nine = 2 * five - 1
    planes = size // (2 * five * places)
    block = depth // (2 * planes)
    for side, x in enumerate((xi, xt)):
        turned[...] = x[...].astype(F32).T
        for beside in range(2):
            first = (column[0] + beside) % 2 * block
            for p in range(planes):
                for q in range(2):
                    for r in range(five):
                        start = first + 2 * p * block + (five - 1) * q + r
                        rows = turned[pl.ds(start, places, stride=nine)].astype(BF16)
                        at = ((2 * p + q) * five + r) * places
                        if beside:
                            away[side * size + at : side * size + at + places] = rows
                        else:
                            (own_t if side else own_i)[at : at + places] = rows


def shares(total, width, share):
    count = width // LANES
    rest = width - count * LANES
    five = 5
    fold = total[2 * count * five : 2 * count * five + five // 2 + 1]
    half = lax.axis_index("dp") % 2
    out = []
    for side in range(2):
        pieces = [total[(side * count + j) * five : (side * count + j + 1) * five] for j in range(count)]
        top = fold[:, side * rest : (side + 1) * rest]
        low = fold[1:, (2 + side) * rest : (3 + side) * rest]
        pieces.append(jnp.concatenate((top, low), axis=0))
        flat = jnp.concatenate(pieces, axis=1).reshape(1, -1)
        out.append(jnp.where(half == 0, flat[:, :share], flat[:, flat.shape[1] - share :]))
    return out


def shards(image_feats, text_feats, image_proj, text_proj, logit_scale, logit_bias):
    rows, depth = image_feats.shape
    width = image_proj.shape[1]
    dp, tower = lax.axis_size("dp"), lax.axis_size("tower")
    planes = dp // RING
    to_core = [(t, t ^ 1) for t in range(tower)]
    to_chip = [(t, t ^ 2) for t in range(tower)]
    first = lax.axis_index("tower") % 2 == 0
    core0 = first.astype(F32)
    numbers = jnp.concatenate((logit_scale, logit_bias, core0[None]))
    scalars = pl.BlockSpec(memory_space=pltpu.SMEM)
    array = pl.BlockSpec(memory_space=pltpu.VMEM)

    here = [pltpu.VMEM((rows, depth), BF16), pltpu.VMEM((width, depth), BF16)] * 2
    z, own = pl.pallas_call(
        project_kernel,
        out_shape=(
            jax.ShapeDtypeStruct((2 * width, rows), F32),
            jax.ShapeDtypeStruct((2 * width, rows), BF16),
        ),
        in_specs=[pl.BlockSpec(memory_space=pl.ANY)] * 4,
        out_specs=(array, array),
        scratch_shapes=here + [pltpu.SemaphoreType.DMA((4,))],
        compiler_params=pltpu.CompilerParams(vmem_limit_bytes=60 * 1024 * 1024),
        name="project",
    )(image_feats, image_proj.T, text_feats, text_proj.T)
    other = lax.ppermute(own, "tower", to_core)
    i0 = jnp.concatenate((own[:width], other[:width]), axis=0)
    t0 = jnp.concatenate((own[width:], other[width:]), axis=0)
    mine, o0 = jnp.where(first, i0, t0), jnp.where(first, t0, i0)
    o2 = shifted(o0, (2, -2))
    o1 = shifted(o0, (1, -1))
    o4 = shifted(o2, (2, -2))
    o3 = shifted(o1, (2, -2))
    column = (lax.axis_index("dp") // RING % 2).astype(jnp.int32)[None]
    beside = [(i, i ^ RING) for i in range(dp)]
    image_feats, text_feats, column = lax.optimization_barrier((image_feats, text_feats, column, o0))[:3]
    size = planes * 5 * (RING // 2)
    xi, xt, away = pl.pallas_call(
        order_kernel,
        out_shape=tuple(jax.ShapeDtypeStruct((n, rows), BF16) for n in (size, size, 2 * size)),
        in_specs=[scalars, array, array],
        out_specs=(array,) * 3,
        scratch_shapes=[pltpu.VMEM((depth, rows), F32)],
        compiler_params=VMEM,
        name="order",
    )(column, image_feats, text_feats)
    x_beside = lax.ppermute(away, "dp", beside)

    def scores(*blocks):
        count = len(blocks) - 1
        return pl.pallas_call(
            functools.partial(score_kernel, count),
            out_shape=jax.ShapeDtypeStruct((count * rows + 16, rows), BF16),
            in_specs=[array] * (count + 1),
            out_specs=array,
            compiler_params=VMEM,
            name="scores",
        )(*blocks)

    near = scores(mine, o0, o1, o2)
    near_peer = lax.ppermute(near, "tower", to_chip)
    far = scores(mine, o3, o4)
    far_peer = lax.ppermute(far, "tower", to_chip)
    d, lines = pl.pallas_call(
        near_kernel,
        out_shape=(
            jax.ShapeDtypeStruct((2 * width, rows), F32),
            jax.ShapeDtypeStruct((8, rows), F32),
        ),
        in_specs=[scalars] + [array] * 5,
        out_specs=(array, array),
        compiler_params=VMEM,
        name="near",
    )(numbers, near, near_peer, o0, o1, o2)
    far_peer, x_beside = lax.optimization_barrier((far_peer, x_beside))
    sums = jax.ShapeDtypeStruct((width + 8, rows), F32)
    send, keep = pl.pallas_call(
        far_kernel,
        out_shape=(sums, sums),
        in_specs=[scalars] + [array] * 6,
        out_specs=(array, array),
        compiler_params=VMEM,
        name="far",
    )(numbers, far, far_peer, d, lines, o3, o4)
    got = lax.ppermute(send, "tower", to_core)
    slopes, send, loss = pl.pallas_call(
        slope_kernel,
        out_shape=(
            jax.ShapeDtypeStruct((2 * width, 2 * rows), BF16),
            jax.ShapeDtypeStruct((2 * width, rows), BF16),
            jax.ShapeDtypeStruct((8, rows), F32),
        ),
        in_specs=[scalars] + [array] * 3,
        out_specs=(array,) * 3,
        compiler_params=VMEM,
        name="slopes",
    )(numbers, keep, got, z)
    theirs = lax.ppermute(send, "dp", beside)
    parts = planes
    block = xi.shape[0] // parts
    payload = 2 * (width // LANES) * block + -(-block // 32) * 16
    grads = pl.pallas_call(
        functools.partial(gradient_kernel, parts),
        out_shape=jax.ShapeDtypeStruct((parts, payload, LANES), BF16),
        in_specs=[array] * 5,
        out_specs=array,
        compiler_params=VMEM,
        name="gradients",
    )(slopes, theirs, xi, xt, x_beside)

    places = RING // 2
    groups = [
        [(2 * y + x) * RING + 2 * m + q for y in range(planes // 2) for q in range(2)]
        for x in range(2)
        for m in range(places)
    ]
    grads = lax.all_to_all(grads, "dp", 0, 0, axis_index_groups=groups, tiled=True)
    sent = pl.pallas_call(
        ring_kernel,
        out_shape=jax.ShapeDtypeStruct((places, payload // places + 1, LANES), F32),
        in_specs=[array],
        out_specs=array,
        compiler_params=VMEM,
        name="ring",
    )(grads)
    groups = [
        [g * RING + (2 * m + places) % RING + q for m in range(places)]
        for g in range(planes)
        for q in range(2)
    ]
    sent = sent.astype(jnp.float16)
    back = lax.all_to_all(sent, "dp", 0, 0, axis_index_groups=groups, tiled=True).astype(F32)
    total = jnp.sum(back * jnp.exp2(back[:, -1:]), axis=0)
    image_grad, text_grad = shares(total, width, depth * width // dp)
    return (loss[0], image_grad, text_grad)


def solution(mesh):
    in_specs = (P("dp", None), P("dp", None), P(None, "tower"), P(None, "tower"), P(), P())
    out_specs = (P("dp"), P("tower", "dp"), P("tower", "dp"))
    return jax.shard_map(shards, mesh=mesh, in_specs=in_specs, out_specs=out_specs, check_vma=False)
```

```python
import functools

import jax
import jax.numpy as jnp
from jax import lax
from jax.experimental import pallas as pl
from jax.experimental.pallas import tpu as pltpu
from jax.sharding import PartitionSpec as P

RING = 32
LANES = 128
BF16, F32 = jnp.bfloat16, jnp.float32
VMEM = pltpu.CompilerParams(vmem_limit_bytes=32 * 1024 * 1024)


def dot(left, right, over_left, over_right):
    return lax.dot_general(
        left, right, (((over_left,), (over_right,)), ((), ())), preferred_element_type=F32
    )


def two_terms(x):
    high = x.astype(BF16)
    return jnp.concatenate((high, (x - high.astype(F32)).astype(BF16)), axis=1)


def fine(block, weights):
    both = dot(block, two_terms(weights), 1, 0)
    return both[:, :LANES] + both[:, LANES:]


def shifted(block, distances):
    dp, tower = lax.axis_size("dp"), lax.axis_size("tower")
    route = [
        (i * tower + t, ((i + distances[t % 2]) % dp) * tower + t)
        for i in range(dp)
        for t in range(tower)
    ]
    return lax.ppermute(block, ("dp", "tower"), route)


def project_kernel(xi, wi, xt, wt, z, own, xi_here, wi_here, xt_here, wt_here, arrived):
    moves = [
        pltpu.make_async_copy(there, here, arrived.at[j])
        for j, (there, here) in enumerate(
            ((xi, xi_here), (wi, wi_here), (xt, xt_here), (wt, wt_here))
        )
    ]
    for move in moves:
        move.start()
    width = wi_here.shape[0]
    for side, (x, w) in enumerate(((xi_here, wi_here), (xt_here, wt_here))):
        moves[2 * side].wait()
        moves[2 * side + 1].wait()
        part = dot(w[...], x[...], 1, 1)
        z[side * width : (side + 1) * width] = part
        own[side * width : (side + 1) * width] = part.astype(BF16)


def score_kernel(count, own, *refs):
    blocks, out = [b[...] for b in (own,) + refs[:count]], refs[count]
    for j, other in enumerate(blocks[1:]):
        out[j * LANES : (j + 1) * LANES] = dot(other, blocks[0], 0, 0).astype(BF16)
    squares = [jnp.sum(jnp.square(b.astype(F32)), axis=0, keepdims=True) for b in blocks]
    squares = jnp.concatenate(squares + [jnp.zeros((7 - count, LANES), F32)], axis=0)
    high = squares.astype(BF16).astype(F32)
    low = (squares - high).astype(BF16).astype(F32)
    out[count * LANES :] = jnp.concatenate((high, low), axis=0).astype(BF16)


def weigh(numbers, mine, peer, others, paired, d, along, loss):
    scale, bias = numbers[0], numbers[1]

    def total(start, rows):
        a = mine[start : start + rows].astype(F32)
        return a + peer[start : start + rows].astype(F32)

    squares = total(len(others) * LANES, 16)
    inv = lax.rsqrt(squares[:8] + squares[8:] + 1e-06)
    down = inv.T
    n = inv[0:1]
    for j, other in enumerate(others):
        col = down[:, j + 1 : j + 2]
        c = scale * (total(j * LANES, LANES) * n * col)
        s = c + bias
        e = jnp.exp(-jnp.abs(s))
        g = jnp.where(s >= 0, 1.0, e) / (1.0 + e)
        signed = s
        if paired and j == 0:
            eye = (
                lax.broadcasted_iota(jnp.int32, (LANES, LANES), 0)
                == lax.broadcasted_iota(jnp.int32, (LANES, LANES), 1)
            ).astype(F32)
            signed, g = (1.0 - 2.0 * eye) * s, g - eye
        terms = (
            fine(other[...], g * col),
            jnp.sum(g * c, axis=0, keepdims=True),
            jnp.sum(jnp.maximum(signed, 0.0) + jnp.log1p(e), axis=0, keepdims=True),
        )
        if d is None:
            d, along, loss = terms
        else:
            d, along, loss = d + terms[0], along + terms[1], loss + terms[2]
    return d, along, loss, n


def near_kernel(numbers, mine, peer, o0, o1, o2, d_out, lines):
    d, along, loss, n = weigh(numbers, mine, peer, (o0, o1, o2), True, None, None, None)
    d_out[...] = d
    lines[...] = jnp.concatenate((along, loss, n, jnp.zeros((5, LANES), F32)), axis=0)


def far_kernel(numbers, mine, peer, d_in, near, o3, o4, send, keep):
    width = d_in.shape[0] // 2
    d, along, loss, _ = weigh(
        numbers, mine, peer, (o3, o4), False, d_in[...], near[0:1], near[1:2]
    )
    lines = jnp.concatenate((along, loss, near[2:8]), axis=0)
    keep[:width], send[:width] = d[:width], d[width:]
    keep[width:], send[width:] = lines, lines


def slope_kernel(numbers, keep, got, z, slopes, send, loss):
    scale, first = numbers[0], numbers[2] > 0
    width = z.shape[0] // 2
    for side in range(2):
        own, other = (keep, got) if side == 0 else (got, keep)
        lines = jnp.where(first, own[width:], other[width:])
        along, n = lines[0:1], lines[2:3]
        if side == 0:
            loss[...] = jnp.broadcast_to(lines[1:2], loss.shape)
        d = scale * jnp.where(first, own[:width], other[:width])
        part = slice(side * width, (side + 1) * width)
        terms = two_terms((d - z[part] * (n * along)) * n)
        slopes[part] = terms
        send[part] = terms[:, :LANES]


def gradient_kernel(parts, slopes, theirs, xi, xt, beside, out):
    width, count = slopes.shape[0] // 2, xi.shape[0]
    block = xi.shape[0] // parts
    whole = width // LANES * LANES
    rest = width - whole
    fold = -(-block // 32) * 16
    tail = None
    for side, x in enumerate((xi, xt)):
        there = slice(side * count, (side + 1) * count)
        feats = jnp.concatenate((x[...], x[...], beside[there]), axis=1)
        part = slice(side * width, (side + 1) * width)
        grads = jnp.concatenate((slopes[part], theirs[part]), axis=1)
        main = dot(feats, grads[:whole], 1, 1).astype(BF16)
        for j in range(whole // LANES):
            at = (side * (whole // LANES) + j) * block
            for p in range(parts):
                out[p, at : at + block] = main[p * block : (p + 1) * block, j * LANES : (j + 1) * LANES]
        piece = grads[whole:]
        gap = jnp.zeros_like(piece)
        pieces = [gap] * (2 * LANES // rest)
        pieces[side] = pieces[LANES // rest + LANES // rest // 2 + side] = piece
        term = dot(feats, jnp.concatenate(pieces, axis=0), 1, 1)
        tail = term if tail is None else tail + term
    for p in range(parts):
        upper = tail[p * block : p * block + fold, :LANES]
        lower = tail[(p + 1) * block - fold : (p + 1) * block, LANES:]
        out[p, 2 * whole // LANES * block :] = (upper + lower).astype(BF16)


def ring_kernel(got, out):
    total = jnp.sum(got[...].astype(F32), axis=0)
    top = jnp.max(jnp.max(jnp.abs(total), axis=0, keepdims=True), axis=1, keepdims=True)
    power = jnp.floor(jnp.log2(jnp.where(top > 0, top, 1.0))) - 13.0
    power = jnp.broadcast_to(jnp.maximum(power, -120.0), (1, LANES))
    total = total * jnp.exp2(-power)
    places = out.shape[0]
    count = total.shape[0] // places
    for j in range(count):
        middle = j * places + places // 2
        out[: places // 2, j] = total[middle : (j + 1) * places]
        out[places // 2 :, j] = total[j * places : middle]
    out[:, count] = jnp.broadcast_to(power, (places, LANES))


def order_kernel(column, xi, xt, own_i, own_t, away, turned):
    places = RING // 2
    depth, size = turned.shape[0], own_i.shape[0]
    five = 5
    nine = 2 * five - 1
    planes = size // (2 * five * places)
    block = depth // (2 * planes)
    for side, x in enumerate((xi, xt)):
        turned[...] = x[...].astype(F32).T
        for beside in range(2):
            first = (column[0] + beside) % 2 * block
            for p in range(planes):
                for q in range(2):
                    for r in range(five):
                        start = first + 2 * p * block + (five - 1) * q + r
                        rows = turned[pl.ds(start, places, stride=nine)].astype(BF16)
                        at = ((2 * p + q) * five + r) * places
                        if beside:
                            away[side * size + at : side * size + at + places] = rows
                        else:
                            (own_t if side else own_i)[at : at + places] = rows


def shares(total, width, share):
    count = width // LANES
    rest = width - count * LANES
    five = 5
    fold = total[2 * count * five : 2 * count * five + five // 2 + 1]
    half = lax.axis_index("dp") % 2
    out = []
    for side in range(2):
        pieces = [total[(side * count + j) * five : (side * count + j + 1) * five] for j in range(count)]
        top = fold[:, side * rest : (side + 1) * rest]
        low = fold[1:, (2 + side) * rest : (3 + side) * rest]
        pieces.append(jnp.concatenate((top, low), axis=0))
        flat = jnp.concatenate(pieces, axis=1).reshape(1, -1)
        out.append(jnp.where(half == 0, flat[:, :share], flat[:, flat.shape[1] - share :]))
    return out


def shards(image_feats, text_feats, image_proj, text_proj, logit_scale, logit_bias):
    rows, depth = image_feats.shape
    width = image_proj.shape[1]
    dp, tower = lax.axis_size("dp"), lax.axis_size("tower")
    planes = dp // RING
    to_core = [(t, t ^ 1) for t in range(tower)]
    to_chip = [(t, t ^ 2) for t in range(tower)]
    first = lax.axis_index("tower") % 2 == 0
    core0 = first.astype(F32)
    numbers = jnp.concatenate((logit_scale, logit_bias, core0[None]))
    scalars = pl.BlockSpec(memory_space=pltpu.SMEM)
    array = pl.BlockSpec(memory_space=pltpu.VMEM)

    here = [pltpu.VMEM((rows, depth), BF16), pltpu.VMEM((width, depth), BF16)] * 2
    z, own = pl.pallas_call(
        project_kernel,
        out_shape=(
            jax.ShapeDtypeStruct((2 * width, rows), F32),
            jax.ShapeDtypeStruct((2 * width, rows), BF16),
        ),
        in_specs=[pl.BlockSpec(memory_space=pl.ANY)] * 4,
        out_specs=(array, array),
        scratch_shapes=here + [pltpu.SemaphoreType.DMA((4,))],
        compiler_params=pltpu.CompilerParams(vmem_limit_bytes=60 * 1024 * 1024),
        name="project",
    )(image_feats, image_proj.T, text_feats, text_proj.T)
    other = lax.ppermute(own, "tower", to_core)
    i0 = jnp.concatenate((own[:width], other[:width]), axis=0)
    t0 = jnp.concatenate((own[width:], other[width:]), axis=0)
    mine, o0 = jnp.where(first, i0, t0), jnp.where(first, t0, i0)
    o2 = shifted(o0, (2, -2))
    o1 = shifted(o0, (1, -1))
    o4 = shifted(o2, (2, -2))
    o3 = shifted(o1, (2, -2))
    column = (lax.axis_index("dp") // RING % 2).astype(jnp.int32)[None]
    beside = [(i, i ^ RING) for i in range(dp)]
    image_feats, text_feats, column = lax.optimization_barrier((image_feats, text_feats, column, o0))[:3]
    size = planes * 5 * (RING // 2)
    xi, xt, away = pl.pallas_call(
        order_kernel,
        out_shape=tuple(jax.ShapeDtypeStruct((n, rows), BF16) for n in (size, size, 2 * size)),
        in_specs=[scalars, array, array],
        out_specs=(array,) * 3,
        scratch_shapes=[pltpu.VMEM((depth, rows), F32)],
        compiler_params=VMEM,
        name="order",
    )(column, image_feats, text_feats)
    x_beside = lax.ppermute(away, "dp", beside)

    def scores(*blocks):
        count = len(blocks) - 1
        return pl.pallas_call(
            functools.partial(score_kernel, count),
            out_shape=jax.ShapeDtypeStruct((count * rows + 16, rows), BF16),
            in_specs=[array] * (count + 1),
            out_specs=array,
            compiler_params=VMEM,
            name="scores",
        )(*blocks)

    near = scores(mine, o0, o1, o2)
    near_peer = lax.ppermute(near, "tower", to_chip)
    near_peer, x_beside = lax.optimization_barrier((near_peer, x_beside))
    far = scores(mine, o3, o4)
    far_peer = lax.ppermute(far, "tower", to_chip)
    d, lines = pl.pallas_call(
        near_kernel,
        out_shape=(
            jax.ShapeDtypeStruct((2 * width, rows), F32),
            jax.ShapeDtypeStruct((8, rows), F32),
        ),
        in_specs=[scalars] + [array] * 5,
        out_specs=(array, array),
        compiler_params=VMEM,
        name="near",
    )(numbers, near, near_peer, o0, o1, o2)
    sums = jax.ShapeDtypeStruct((width + 8, rows), F32)
    send, keep = pl.pallas_call(
        far_kernel,
        out_shape=(sums, sums),
        in_specs=[scalars] + [array] * 6,
        out_specs=(array, array),
        compiler_params=VMEM,
        name="far",
    )(numbers, far, far_peer, d, lines, o3, o4)
    got = lax.ppermute(send, "tower", to_core)
    slopes, send, loss = pl.pallas_call(
        slope_kernel,
        out_shape=(
            jax.ShapeDtypeStruct((2 * width, 2 * rows), BF16),
            jax.ShapeDtypeStruct((2 * width, rows), BF16),
            jax.ShapeDtypeStruct((8, rows), F32),
        ),
        in_specs=[scalars] + [array] * 3,
        out_specs=(array,) * 3,
        compiler_params=VMEM,
        name="slopes",
    )(numbers, keep, got, z)
    theirs = lax.ppermute(send, "dp", beside)
    parts = planes
    block = xi.shape[0] // parts
    payload = 2 * (width // LANES) * block + -(-block // 32) * 16
    grads = pl.pallas_call(
        functools.partial(gradient_kernel, parts),
        out_shape=jax.ShapeDtypeStruct((parts, payload, LANES), BF16),
        in_specs=[array] * 5,
        out_specs=array,
        compiler_params=VMEM,
        name="gradients",
    )(slopes, theirs, xi, xt, x_beside)

    places = RING // 2
    groups = [
        [(2 * y + x) * RING + 2 * m + q for y in range(planes // 2) for q in range(2)]
        for x in range(2)
        for m in range(places)
    ]
    grads = lax.all_to_all(grads, "dp", 0, 0, axis_index_groups=groups, tiled=True)
    sent = pl.pallas_call(
        ring_kernel,
        out_shape=jax.ShapeDtypeStruct((places, payload // places + 1, LANES), F32),
        in_specs=[array],
        out_specs=array,
        compiler_params=VMEM,
        name="ring",
    )(grads)
    groups = [
        [g * RING + (2 * m + places) % RING + q for m in range(places)]
        for g in range(planes)
        for q in range(2)
    ]
    sent = sent.astype(jnp.float16)
    back = lax.all_to_all(sent, "dp", 0, 0, axis_index_groups=groups, tiled=True).astype(F32)
    total = jnp.sum(back * jnp.exp2(back[:, -1:]), axis=0)
    image_grad, text_grad = shares(total, width, depth * width // dp)
    return (loss[0], image_grad, text_grad)


def solution(mesh):
    in_specs = (P("dp", None), P("dp", None), P(None, "tower"), P(None, "tower"), P(), P())
    out_specs = (P("dp"), P("tower", "dp"), P("tower", "dp"))
    return jax.shard_map(shards, mesh=mesh, in_specs=in_specs, out_specs=out_specs, check_vma=False)
```

```python
import functools

import jax
import jax.numpy as jnp
from jax import lax
from jax.experimental import pallas as pl
from jax.experimental.pallas import tpu as pltpu
from jax.sharding import PartitionSpec as P

RING = 32
LANES = 128
BF16, F32 = jnp.bfloat16, jnp.float32
VMEM = pltpu.CompilerParams(vmem_limit_bytes=32 * 1024 * 1024)


def dot(left, right, over_left, over_right):
    return lax.dot_general(
        left, right, (((over_left,), (over_right,)), ((), ())), preferred_element_type=F32
    )


def two_terms(x):
    high = x.astype(BF16)
    return jnp.concatenate((high, (x - high.astype(F32)).astype(BF16)), axis=1)


def fine(block, weights):
    both = dot(block, two_terms(weights), 1, 0)
    return both[:, :LANES] + both[:, LANES:]


def shifted(block, distances):
    dp, tower = lax.axis_size("dp"), lax.axis_size("tower")
    route = [
        (i * tower + t, ((i + distances[t % 2]) % dp) * tower + t)
        for i in range(dp)
        for t in range(tower)
    ]
    return lax.ppermute(block, ("dp", "tower"), route)


def project_kernel(xi, wi, xt, wt, z, own, xi_here, wi_here, xt_here, wt_here, arrived):
    moves = [
        pltpu.make_async_copy(there, here, arrived.at[j])
        for j, (there, here) in enumerate(
            ((xi, xi_here), (wi, wi_here), (xt, xt_here), (wt, wt_here))
        )
    ]
    for move in moves:
        move.start()
    width = wi_here.shape[0]
    for side, (x, w) in enumerate(((xi_here, wi_here), (xt_here, wt_here))):
        moves[2 * side].wait()
        moves[2 * side + 1].wait()
        part = dot(w[...], x[...], 1, 1)
        z[side * width : (side + 1) * width] = part
        own[side * width : (side + 1) * width] = part.astype(BF16)


def score_kernel(count, own, *refs):
    blocks, out = [b[...] for b in (own,) + refs[:count]], refs[count]
    for j, other in enumerate(blocks[1:]):
        out[j * LANES : (j + 1) * LANES] = dot(other, blocks[0], 0, 0).astype(BF16)
    squares = [jnp.sum(jnp.square(b.astype(F32)), axis=0, keepdims=True) for b in blocks]
    squares = jnp.concatenate(squares + [jnp.zeros((7 - count, LANES), F32)], axis=0)
    high = squares.astype(BF16).astype(F32)
    low = (squares - high).astype(BF16).astype(F32)
    out[count * LANES :] = jnp.concatenate((high, low), axis=0).astype(BF16)


def weigh(numbers, mine, peer, others, paired, d, along, loss):
    scale, bias = numbers[0], numbers[1]

    def total(start, rows):
        a = mine[start : start + rows].astype(F32)
        return a + peer[start : start + rows].astype(F32)

    squares = total(len(others) * LANES, 16)
    inv = lax.rsqrt(squares[:8] + squares[8:] + 1e-06)
    down = inv.T
    n = inv[0:1]
    for j, other in enumerate(others):
        col = down[:, j + 1 : j + 2]
        c = scale * (total(j * LANES, LANES) * n * col)
        s = c + bias
        e = jnp.exp(-jnp.abs(s))
        g = jnp.where(s >= 0, 1.0, e) / (1.0 + e)
        signed = s
        if paired and j == 0:
            eye = (
                lax.broadcasted_iota(jnp.int32, (LANES, LANES), 0)
                == lax.broadcasted_iota(jnp.int32, (LANES, LANES), 1)
            ).astype(F32)
            signed, g = (1.0 - 2.0 * eye) * s, g - eye
        terms = (
            fine(other[...], g * col),
            jnp.sum(g * c, axis=0, keepdims=True),
            jnp.sum(jnp.maximum(signed, 0.0) + jnp.log1p(e), axis=0, keepdims=True),
        )
        if d is None:
            d, along, loss = terms
        else:
            d, along, loss = d + terms[0], along + terms[1], loss + terms[2]
    return d, along, loss, n


def near_kernel(numbers, mine, peer, o0, o1, o2, d_out, lines):
    d, along, loss, n = weigh(numbers, mine, peer, (o0, o1, o2), True, None, None, None)
    d_out[...] = d
    lines[...] = jnp.concatenate((along, loss, n, jnp.zeros((5, LANES), F32)), axis=0)


def far_kernel(numbers, mine, peer, d_in, near, o3, o4, send, keep):
    width = d_in.shape[0] // 2
    d, along, loss, _ = weigh(
        numbers, mine, peer, (o3, o4), False, d_in[...], near[0:1], near[1:2]
    )
    lines = jnp.concatenate((along, loss, near[2:8]), axis=0)
    keep[:width], send[:width] = d[:width], d[width:]
    keep[width:], send[width:] = lines, lines


def slope_kernel(numbers, keep, got, z, slopes, send, loss):
    scale, first = numbers[0], numbers[2] > 0
    width = z.shape[0] // 2
    for side in range(2):
        own, other = (keep, got) if side == 0 else (got, keep)
        lines = jnp.where(first, own[width:], other[width:])
        along, n = lines[0:1], lines[2:3]
        if side == 0:
            loss[...] = jnp.broadcast_to(lines[1:2], loss.shape)
        d = scale * jnp.where(first, own[:width], other[:width])
        part = slice(side * width, (side + 1) * width)
        terms = two_terms((d - z[part] * (n * along)) * n)
        slopes[part] = terms
        send[part] = terms[:, :LANES]


def gradient_kernel(parts, slopes, theirs, xi, xt, beside, out):
    width, count = slopes.shape[0] // 2, xi.shape[0]
    block = xi.shape[0] // parts
    whole = width // LANES * LANES
    rest = width - whole
    fold = -(-block // 32) * 16
    tail = None
    for side, x in enumerate((xi, xt)):
        there = slice(side * count, (side + 1) * count)
        feats = jnp.concatenate((x[...], x[...], beside[there]), axis=1)
        part = slice(side * width, (side + 1) * width)
        grads = jnp.concatenate((slopes[part], theirs[part]), axis=1)
        main = dot(feats, grads[:whole], 1, 1).astype(BF16)
        for j in range(whole // LANES):
            at = (side * (whole // LANES) + j) * block
            for p in range(parts):
                out[p, at : at + block] = main[p * block : (p + 1) * block, j * LANES : (j + 1) * LANES]
        piece = grads[whole:]
        gap = jnp.zeros_like(piece)
        pieces = [gap] * (2 * LANES // rest)
        pieces[side] = pieces[LANES // rest + LANES // rest // 2 + side] = piece
        term = dot(feats, jnp.concatenate(pieces, axis=0), 1, 1)
        tail = term if tail is None else tail + term
    for p in range(parts):
        upper = tail[p * block : p * block + fold, :LANES]
        lower = tail[(p + 1) * block - fold : (p + 1) * block, LANES:]
        out[p, 2 * whole // LANES * block :] = (upper + lower).astype(BF16)


def ring_order(places):
    near = [m // 2 if m % 2 == 0 else places - 1 - m // 2 for m in range(places)]
    return [places // 2] + [m for m in near if m != places // 2]


def ring_kernel(got, out, laid):
    total = jnp.sum(got[...].astype(F32), axis=0)
    top = jnp.max(jnp.max(jnp.abs(total), axis=0, keepdims=True), axis=1, keepdims=True)
    power = jnp.floor(jnp.log2(jnp.where(top > 0, top, 1.0))) - 13.0
    power = jnp.broadcast_to(jnp.maximum(power, -120.0), (1, LANES))
    total = total * jnp.exp2(-power)
    places = out.shape[0]
    count = total.shape[0] // places
    for j in range(count):
        laid[:, j] = total[j * places : (j + 1) * places]
    laid[:, count] = jnp.broadcast_to(power, (places, LANES))
    for at, place in enumerate(ring_order(places)):
        out[at] = laid[place]


def order_kernel(column, xi, xt, own_i, own_t, away, turned):
    places = RING // 2
    depth, size = turned.shape[0], own_i.shape[0]
    five = 5
    nine = 2 * five - 1
    planes = size // (2 * five * places)
    block = depth // (2 * planes)
    for side, x in enumerate((xi, xt)):
        turned[...] = x[...].astype(F32).T
        for beside in range(2):
            first = (column[0] + beside) % 2 * block
            for p in range(planes):
                for q in range(2):
                    for r in range(five):
                        start = first + 2 * p * block + (five - 1) * q + r
                        rows = turned[pl.ds(start, places, stride=nine)].astype(BF16)
                        at = ((2 * p + q) * five + r) * places
                        if beside:
                            away[side * size + at : side * size + at + places] = rows
                        else:
                            (own_t if side else own_i)[at : at + places] = rows


def shares(total, width, share):
    count = width // LANES
    rest = width - count * LANES
    five = 5
    fold = total[2 * count * five : 2 * count * five + five // 2 + 1]
    half = lax.axis_index("dp") % 2
    out = []
    for side in range(2):
        pieces = [total[(side * count + j) * five : (side * count + j + 1) * five] for j in range(count)]
        top = fold[:, side * rest : (side + 1) * rest]
        low = fold[1:, (2 + side) * rest : (3 + side) * rest]
        pieces.append(jnp.concatenate((top, low), axis=0))
        flat = jnp.concatenate(pieces, axis=1).reshape(1, -1)
        out.append(jnp.where(half == 0, flat[:, :share], flat[:, flat.shape[1] - share :]))
    return out


def shards(image_feats, text_feats, image_proj, text_proj, logit_scale, logit_bias):
    rows, depth = image_feats.shape
    width = image_proj.shape[1]
    dp, tower = lax.axis_size("dp"), lax.axis_size("tower")
    planes = dp // RING
    to_core = [(t, t ^ 1) for t in range(tower)]
    to_chip = [(t, t ^ 2) for t in range(tower)]
    first = lax.axis_index("tower") % 2 == 0
    core0 = first.astype(F32)
    numbers = jnp.concatenate((logit_scale, logit_bias, core0[None]))
    scalars = pl.BlockSpec(memory_space=pltpu.SMEM)
    array = pl.BlockSpec(memory_space=pltpu.VMEM)

    here = [pltpu.VMEM((rows, depth), BF16), pltpu.VMEM((width, depth), BF16)] * 2
    z, own = pl.pallas_call(
        project_kernel,
        out_shape=(
            jax.ShapeDtypeStruct((2 * width, rows), F32),
            jax.ShapeDtypeStruct((2 * width, rows), BF16),
        ),
        in_specs=[pl.BlockSpec(memory_space=pl.ANY)] * 4,
        out_specs=(array, array),
        scratch_shapes=here + [pltpu.SemaphoreType.DMA((4,))],
        compiler_params=pltpu.CompilerParams(vmem_limit_bytes=60 * 1024 * 1024),
        name="project",
    )(image_feats, image_proj.T, text_feats, text_proj.T)
    other = lax.ppermute(own, "tower", to_core)
    i0 = jnp.concatenate((own[:width], other[:width]), axis=0)
    t0 = jnp.concatenate((own[width:], other[width:]), axis=0)
    mine, o0 = jnp.where(first, i0, t0), jnp.where(first, t0, i0)
    o2 = shifted(o0, (2, -2))
    o1 = shifted(o0, (1, -1))
    o4 = shifted(o2, (2, -2))
    o3 = shifted(o1, (2, -2))
    column = (lax.axis_index("dp") // RING % 2).astype(jnp.int32)[None]
    beside = [(i, i ^ RING) for i in range(dp)]
    image_feats, text_feats, column = lax.optimization_barrier((image_feats, text_feats, column, o0))[:3]
    size = planes * 5 * (RING // 2)
    xi, xt, away = pl.pallas_call(
        order_kernel,
        out_shape=tuple(jax.ShapeDtypeStruct((n, rows), BF16) for n in (size, size, 2 * size)),
        in_specs=[scalars, array, array],
        out_specs=(array,) * 3,
        scratch_shapes=[pltpu.VMEM((depth, rows), F32)],
        compiler_params=VMEM,
        name="order",
    )(column, image_feats, text_feats)
    x_beside = lax.ppermute(away, "dp", beside)

    def scores(*blocks):
        count = len(blocks) - 1
        return pl.pallas_call(
            functools.partial(score_kernel, count),
            out_shape=jax.ShapeDtypeStruct((count * rows + 16, rows), BF16),
            in_specs=[array] * (count + 1),
            out_specs=array,
            compiler_params=VMEM,
            name="scores",
        )(*blocks)

    near = scores(mine, o0, o1, o2)
    near_peer = lax.ppermute(near, "tower", to_chip)
    near_peer, x_beside = lax.optimization_barrier((near_peer, x_beside))
    far = scores(mine, o3, o4)
    far_peer = lax.ppermute(far, "tower", to_chip)
    d, lines = pl.pallas_call(
        near_kernel,
        out_shape=(
            jax.ShapeDtypeStruct((2 * width, rows), F32),
            jax.ShapeDtypeStruct((8, rows), F32),
        ),
        in_specs=[scalars] + [array] * 5,
        out_specs=(array, array),
        compiler_params=VMEM,
        name="near",
    )(numbers, near, near_peer, o0, o1, o2)
    sums = jax.ShapeDtypeStruct((width + 8, rows), F32)
    send, keep = pl.pallas_call(
        far_kernel,
        out_shape=(sums, sums),
        in_specs=[scalars] + [array] * 6,
        out_specs=(array, array),
        compiler_params=VMEM,
        name="far",
    )(numbers, far, far_peer, d, lines, o3, o4)
    got = lax.ppermute(send, "tower", to_core)
    slopes, send, loss = pl.pallas_call(
        slope_kernel,
        out_shape=(
            jax.ShapeDtypeStruct((2 * width, 2 * rows), BF16),
            jax.ShapeDtypeStruct((2 * width, rows), BF16),
            jax.ShapeDtypeStruct((8, rows), F32),
        ),
        in_specs=[scalars] + [array] * 3,
        out_specs=(array,) * 3,
        compiler_params=VMEM,
        name="slopes",
    )(numbers, keep, got, z)
    theirs = lax.ppermute(send, "dp", beside)
    parts = planes
    block = xi.shape[0] // parts
    payload = 2 * (width // LANES) * block + -(-block // 32) * 16
    grads = pl.pallas_call(
        functools.partial(gradient_kernel, parts),
        out_shape=jax.ShapeDtypeStruct((parts, payload, LANES), BF16),
        in_specs=[array] * 5,
        out_specs=array,
        compiler_params=VMEM,
        name="gradients",
    )(slopes, theirs, xi, xt, x_beside)

    places = RING // 2
    groups = [
        [(2 * y + x) * RING + 2 * m + q for y in range(planes // 2) for q in range(2)]
        for x in range(2)
        for m in range(places)
    ]
    grads = lax.all_to_all(grads, "dp", 0, 0, axis_index_groups=groups, tiled=True)
    sent = pl.pallas_call(
        ring_kernel,
        out_shape=jax.ShapeDtypeStruct((places, payload // places + 1, LANES), F32),
        in_specs=[array],
        out_specs=array,
        scratch_shapes=[pltpu.VMEM((places, payload // places + 1, LANES), F32)],
        compiler_params=VMEM,
        name="ring",
    )(grads)
    groups = [
        [g * RING + 2 * m + q for m in ring_order(places)] for g in range(planes) for q in range(2)
    ]
    sent = sent.astype(jnp.float16)
    back = lax.all_to_all(sent, "dp", 0, 0, axis_index_groups=groups, tiled=True).astype(F32)
    total = jnp.sum(back * jnp.exp2(back[:, -1:]), axis=0)
    image_grad, text_grad = shares(total, width, depth * width // dp)
    return (loss[0], image_grad, text_grad)


def solution(mesh):
    in_specs = (P("dp", None), P("dp", None), P(None, "tower"), P(None, "tower"), P(), P())
    out_specs = (P("dp"), P("tower", "dp"), P("tower", "dp"))
    return jax.shard_map(shards, mesh=mesh, in_specs=in_specs, out_specs=out_specs, check_vma=False)
```

```python
import functools

import jax
import jax.numpy as jnp
from jax import lax
from jax.experimental import pallas as pl
from jax.experimental.pallas import tpu as pltpu
from jax.sharding import PartitionSpec as P

RING = 32
LANES = 128
BF16, F32 = jnp.bfloat16, jnp.float32
VMEM = pltpu.CompilerParams(vmem_limit_bytes=32 * 1024 * 1024)


def dot(left, right, over_left, over_right):
    return lax.dot_general(
        left, right, (((over_left,), (over_right,)), ((), ())), preferred_element_type=F32
    )


def two_terms(x):
    high = x.astype(BF16)
    return jnp.concatenate((high, (x - high.astype(F32)).astype(BF16)), axis=1)


def fine(block, weights):
    both = dot(block, two_terms(weights), 1, 0)
    return both[:, :LANES] + both[:, LANES:]


def shifted(block, distances):
    dp, tower = lax.axis_size("dp"), lax.axis_size("tower")
    route = [
        (i * tower + t, ((i + distances[t % 2]) % dp) * tower + t)
        for i in range(dp)
        for t in range(tower)
    ]
    return lax.ppermute(block, ("dp", "tower"), route)


def project_kernel(xi, wi, xt, wt, z, own, xi_here, wi_here, xt_here, wt_here, arrived):
    moves = [
        pltpu.make_async_copy(there, here, arrived.at[j])
        for j, (there, here) in enumerate(
            ((xi, xi_here), (wi, wi_here), (xt, xt_here), (wt, wt_here))
        )
    ]
    for move in moves:
        move.start()
    width = wi_here.shape[0]
    for side, (x, w) in enumerate(((xi_here, wi_here), (xt_here, wt_here))):
        moves[2 * side].wait()
        moves[2 * side + 1].wait()
        part = dot(w[...], x[...], 1, 1)
        z[side * width : (side + 1) * width] = part
        own[side * width : (side + 1) * width] = part.astype(BF16)


def score_kernel(count, own, *refs):
    blocks, out = [b[...] for b in (own,) + refs[:count]], refs[count]
    for j, other in enumerate(blocks[1:]):
        out[j * LANES : (j + 1) * LANES] = dot(other, blocks[0], 0, 0).astype(BF16)
    squares = [jnp.sum(jnp.square(b.astype(F32)), axis=0, keepdims=True) for b in blocks]
    squares = jnp.concatenate(squares + [jnp.zeros((7 - count, LANES), F32)], axis=0)
    high = squares.astype(BF16).astype(F32)
    low = (squares - high).astype(BF16).astype(F32)
    out[count * LANES :] = jnp.concatenate((high, low), axis=0).astype(BF16)


def weigh(numbers, mine, peer, others, paired, d, along, loss):
    scale, bias = numbers[0], numbers[1]

    def total(start, rows):
        a = mine[start : start + rows].astype(F32)
        return a + peer[start : start + rows].astype(F32)

    squares = total(len(others) * LANES, 16)
    inv = lax.rsqrt(squares[:8] + squares[8:] + 1e-06)
    down = inv.T
    n = inv[0:1]
    for j, other in enumerate(others):
        col = down[:, j + 1 : j + 2]
        c = scale * (total(j * LANES, LANES) * n * col)
        s = c + bias
        e = jnp.exp(-jnp.abs(s))
        g = jnp.where(s >= 0, 1.0, e) / (1.0 + e)
        signed = s
        if paired and j == 0:
            eye = (
                lax.broadcasted_iota(jnp.int32, (LANES, LANES), 0)
                == lax.broadcasted_iota(jnp.int32, (LANES, LANES), 1)
            ).astype(F32)
            signed, g = (1.0 - 2.0 * eye) * s, g - eye
        terms = (
            fine(other[...], g * col),
            jnp.sum(g * c, axis=0, keepdims=True),
            jnp.sum(jnp.maximum(signed, 0.0) + jnp.log1p(e), axis=0, keepdims=True),
        )
        if d is None:
            d, along, loss = terms
        else:
            d, along, loss = d + terms[0], along + terms[1], loss + terms[2]
    return d, along, loss, n


def near_kernel(numbers, mine, peer, o0, o1, o2, d_out, lines):
    d, along, loss, n = weigh(numbers, mine, peer, (o0, o1, o2), True, None, None, None)
    d_out[...] = d
    lines[...] = jnp.concatenate((along, loss, n, jnp.zeros((5, LANES), F32)), axis=0)


def far_kernel(numbers, mine, peer, d_in, near, o3, o4, send, keep):
    width = d_in.shape[0] // 2
    d, along, loss, _ = weigh(
        numbers, mine, peer, (o3, o4), False, d_in[...], near[0:1], near[1:2]
    )
    lines = jnp.concatenate((along, loss, near[2:8]), axis=0)
    keep[:width], send[:width] = d[:width], d[width:]
    keep[width:], send[width:] = lines, lines


def slope_kernel(numbers, keep, got, z, slopes, send, loss):
    scale, first = numbers[0], numbers[2] > 0
    width = z.shape[0] // 2
    for side in range(2):
        own, other = (keep, got) if side == 0 else (got, keep)
        lines = jnp.where(first, own[width:], other[width:])
        along, n = lines[0:1], lines[2:3]
        if side == 0:
            loss[...] = jnp.broadcast_to(lines[1:2], loss.shape)
        d = scale * jnp.where(first, own[:width], other[:width])
        part = slice(side * width, (side + 1) * width)
        terms = two_terms((d - z[part] * (n * along)) * n)
        slopes[part] = terms
        send[part] = terms[:, :LANES]


def gradient_kernel(parts, slopes, theirs, xi, xt, beside, out):
    width, count = slopes.shape[0] // 2, xi.shape[0]
    block = xi.shape[0] // parts
    whole = width // LANES * LANES
    rest = width - whole
    fold = -(-block // 32) * 16
    tail = None
    for side, x in enumerate((xi, xt)):
        there = slice(side * count, (side + 1) * count)
        feats = jnp.concatenate((x[...], x[...], beside[there]), axis=1)
        part = slice(side * width, (side + 1) * width)
        grads = jnp.concatenate((slopes[part], theirs[part]), axis=1)
        main = dot(feats, grads[:whole], 1, 1).astype(BF16)
        for j in range(whole // LANES):
            at = (side * (whole // LANES) + j) * block
            for p in range(parts):
                out[p, at : at + block] = main[p * block : (p + 1) * block, j * LANES : (j + 1) * LANES]
        piece = grads[whole:]
        gap = jnp.zeros_like(piece)
        pieces = [gap] * (2 * LANES // rest)
        pieces[side] = pieces[LANES // rest + LANES // rest // 2 + side] = piece
        term = dot(feats, jnp.concatenate(pieces, axis=0), 1, 1)
        tail = term if tail is None else tail + term
    for p in range(parts):
        upper = tail[p * block : p * block + fold, :LANES]
        lower = tail[(p + 1) * block - fold : (p + 1) * block, LANES:]
        out[p, 2 * whole // LANES * block :] = (upper + lower).astype(BF16)


def ring_order(places):
    first = 3 * places // 8
    near = [m // 2 if m % 2 == 0 else places - 1 - m // 2 for m in range(places)]
    return [first] + [m for m in near if m != first]


def ring_kernel(got, out, laid):
    total = jnp.sum(got[...].astype(F32), axis=0)
    top = jnp.max(jnp.max(jnp.abs(total), axis=0, keepdims=True), axis=1, keepdims=True)
    power = jnp.floor(jnp.log2(jnp.where(top > 0, top, 1.0))) - 13.0
    power = jnp.broadcast_to(jnp.maximum(power, -120.0), (1, LANES))
    total = total * jnp.exp2(-power)
    places = out.shape[0]
    count = total.shape[0] // places
    for j in range(count):
        laid[:, j] = total[j * places : (j + 1) * places]
    laid[:, count] = jnp.broadcast_to(power, (places, LANES))
    for at, place in enumerate(ring_order(places)):
        out[at] = laid[place]


def order_kernel(column, xi, xt, own_i, own_t, away, turned):
    places = RING // 2
    depth, size = turned.shape[0], own_i.shape[0]
    five = 5
    nine = 2 * five - 1
    planes = size // (2 * five * places)
    block = depth // (2 * planes)
    for side, x in enumerate((xi, xt)):
        turned[...] = x[...].astype(F32).T
        for beside in range(2):
            first = (column[0] + beside) % 2 * block
            for p in range(planes):
                for q in range(2):
                    for r in range(five):
                        start = first + 2 * p * block + (five - 1) * q + r
                        rows = turned[pl.ds(start, places, stride=nine)].astype(BF16)
                        at = ((2 * p + q) * five + r) * places
                        if beside:
                            away[side * size + at : side * size + at + places] = rows
                        else:
                            (own_t if side else own_i)[at : at + places] = rows


def shares(total, width, share):
    count = width // LANES
    rest = width - count * LANES
    five = 5
    fold = total[2 * count * five : 2 * count * five + five // 2 + 1]
    half = lax.axis_index("dp") % 2
    out = []
    for side in range(2):
        pieces = [total[(side * count + j) * five : (side * count + j + 1) * five] for j in range(count)]
        top = fold[:, side * rest : (side + 1) * rest]
        low = fold[1:, (2 + side) * rest : (3 + side) * rest]
        pieces.append(jnp.concatenate((top, low), axis=0))
        flat = jnp.concatenate(pieces, axis=1).reshape(1, -1)
        out.append(jnp.where(half == 0, flat[:, :share], flat[:, flat.shape[1] - share :]))
    return out


def shards(image_feats, text_feats, image_proj, text_proj, logit_scale, logit_bias):
    rows, depth = image_feats.shape
    width = image_proj.shape[1]
    dp, tower = lax.axis_size("dp"), lax.axis_size("tower")
    planes = dp // RING
    to_core = [(t, t ^ 1) for t in range(tower)]
    to_chip = [(t, t ^ 2) for t in range(tower)]
    first = lax.axis_index("tower") % 2 == 0
    core0 = first.astype(F32)
    numbers = jnp.concatenate((logit_scale, logit_bias, core0[None]))
    scalars = pl.BlockSpec(memory_space=pltpu.SMEM)
    array = pl.BlockSpec(memory_space=pltpu.VMEM)

    here = [pltpu.VMEM((rows, depth), BF16), pltpu.VMEM((width, depth), BF16)] * 2
    z, own = pl.pallas_call(
        project_kernel,
        out_shape=(
            jax.ShapeDtypeStruct((2 * width, rows), F32),
            jax.ShapeDtypeStruct((2 * width, rows), BF16),
        ),
        in_specs=[pl.BlockSpec(memory_space=pl.ANY)] * 4,
        out_specs=(array, array),
        scratch_shapes=here + [pltpu.SemaphoreType.DMA((4,))],
        compiler_params=pltpu.CompilerParams(vmem_limit_bytes=60 * 1024 * 1024),
        name="project",
    )(image_feats, image_proj.T, text_feats, text_proj.T)
    other = lax.ppermute(own, "tower", to_core)
    i0 = jnp.concatenate((own[:width], other[:width]), axis=0)
    t0 = jnp.concatenate((own[width:], other[width:]), axis=0)
    mine, o0 = jnp.where(first, i0, t0), jnp.where(first, t0, i0)
    o2 = shifted(o0, (2, -2))
    o1 = shifted(o0, (1, -1))
    o4 = shifted(o2, (2, -2))
    o3 = shifted(o1, (2, -2))
    column = (lax.axis_index("dp") // RING % 2).astype(jnp.int32)[None]
    beside = [(i, i ^ RING) for i in range(dp)]
    image_feats, text_feats, column = lax.optimization_barrier((image_feats, text_feats, column, o0))[:3]
    size = planes * 5 * (RING // 2)
    xi, xt, away = pl.pallas_call(
        order_kernel,
        out_shape=tuple(jax.ShapeDtypeStruct((n, rows), BF16) for n in (size, size, 2 * size)),
        in_specs=[scalars, array, array],
        out_specs=(array,) * 3,
        scratch_shapes=[pltpu.VMEM((depth, rows), F32)],
        compiler_params=VMEM,
        name="order",
    )(column, image_feats, text_feats)
    x_beside = lax.ppermute(away, "dp", beside)

    def scores(*blocks):
        count = len(blocks) - 1
        return pl.pallas_call(
            functools.partial(score_kernel, count),
            out_shape=jax.ShapeDtypeStruct((count * rows + 16, rows), BF16),
            in_specs=[array] * (count + 1),
            out_specs=array,
            compiler_params=VMEM,
            name="scores",
        )(*blocks)

    near = scores(mine, o0, o1, o2)
    near_peer = lax.ppermute(near, "tower", to_chip)
    near_peer, x_beside = lax.optimization_barrier((near_peer, x_beside))
    far = scores(mine, o3, o4)
    far_peer = lax.ppermute(far, "tower", to_chip)
    d, lines = pl.pallas_call(
        near_kernel,
        out_shape=(
            jax.ShapeDtypeStruct((2 * width, rows), F32),
            jax.ShapeDtypeStruct((8, rows), F32),
        ),
        in_specs=[scalars] + [array] * 5,
        out_specs=(array, array),
        compiler_params=VMEM,
        name="near",
    )(numbers, near, near_peer, o0, o1, o2)
    sums = jax.ShapeDtypeStruct((width + 8, rows), F32)
    send, keep = pl.pallas_call(
        far_kernel,
        out_shape=(sums, sums),
        in_specs=[scalars] + [array] * 6,
        out_specs=(array, array),
        compiler_params=VMEM,
        name="far",
    )(numbers, far, far_peer, d, lines, o3, o4)
    got = lax.ppermute(send, "tower", to_core)
    slopes, send, loss = pl.pallas_call(
        slope_kernel,
        out_shape=(
            jax.ShapeDtypeStruct((2 * width, 2 * rows), BF16),
            jax.ShapeDtypeStruct((2 * width, rows), BF16),
            jax.ShapeDtypeStruct((8, rows), F32),
        ),
        in_specs=[scalars] + [array] * 3,
        out_specs=(array,) * 3,
        compiler_params=VMEM,
        name="slopes",
    )(numbers, keep, got, z)
    theirs = lax.ppermute(send, "dp", beside)
    parts = planes
    block = xi.shape[0] // parts
    payload = 2 * (width // LANES) * block + -(-block // 32) * 16
    grads = pl.pallas_call(
        functools.partial(gradient_kernel, parts),
        out_shape=jax.ShapeDtypeStruct((parts, payload, LANES), BF16),
        in_specs=[array] * 5,
        out_specs=array,
        compiler_params=VMEM,
        name="gradients",
    )(slopes, theirs, xi, xt, x_beside)

    places = RING // 2
    groups = [
        [(2 * y + x) * RING + 2 * m + q for y in range(planes // 2) for q in range(2)]
        for x in range(2)
        for m in range(places)
    ]
    grads = lax.all_to_all(grads, "dp", 0, 0, axis_index_groups=groups, tiled=True)
    sent = pl.pallas_call(
        ring_kernel,
        out_shape=jax.ShapeDtypeStruct((places, payload // places + 1, LANES), F32),
        in_specs=[array],
        out_specs=array,
        scratch_shapes=[pltpu.VMEM((places, payload // places + 1, LANES), F32)],
        compiler_params=VMEM,
        name="ring",
    )(grads)
    groups = [
        [g * RING + 2 * m + q for m in ring_order(places)] for g in range(planes) for q in range(2)
    ]
    sent = sent.astype(jnp.float16)
    back = lax.all_to_all(sent, "dp", 0, 0, axis_index_groups=groups, tiled=True).astype(F32)
    total = jnp.sum(back * jnp.exp2(back[:, -1:]), axis=0)
    image_grad, text_grad = shares(total, width, depth * width // dp)
    return (loss[0], image_grad, text_grad)


def solution(mesh):
    in_specs = (P("dp", None), P("dp", None), P(None, "tower"), P(None, "tower"), P(), P())
    out_specs = (P("dp"), P("tower", "dp"), P("tower", "dp"))
    return jax.shard_map(shards, mesh=mesh, in_specs=in_specs, out_specs=out_specs, check_vma=False)
```

```python
import functools

import jax
import jax.numpy as jnp
from jax import lax
from jax.experimental import pallas as pl
from jax.experimental.pallas import tpu as pltpu
from jax.sharding import PartitionSpec as P

RING = 32
LANES = 128
BF16, F32 = jnp.bfloat16, jnp.float32
VMEM = pltpu.CompilerParams(vmem_limit_bytes=32 * 1024 * 1024)


def dot(left, right, over_left, over_right):
    return lax.dot_general(
        left, right, (((over_left,), (over_right,)), ((), ())), preferred_element_type=F32
    )


def two_terms(x):
    high = x.astype(BF16)
    return jnp.concatenate((high, (x - high.astype(F32)).astype(BF16)), axis=1)


def fine(block, weights):
    both = dot(block, two_terms(weights), 1, 0)
    return both[:, :LANES] + both[:, LANES:]


def shifted(block, distances):
    dp, tower = lax.axis_size("dp"), lax.axis_size("tower")
    route = [
        (i * tower + t, ((i + distances[t % 2]) % dp) * tower + t)
        for i in range(dp)
        for t in range(tower)
    ]
    return lax.ppermute(block, ("dp", "tower"), route)


def project_kernel(xi, wi, xt, wt, z, own, xi_here, wi_here, xt_here, wt_here, arrived):
    moves = [
        pltpu.make_async_copy(there, here, arrived.at[j])
        for j, (there, here) in enumerate(
            ((xi, xi_here), (wi, wi_here), (xt, xt_here), (wt, wt_here))
        )
    ]
    for move in moves:
        move.start()
    width = wi_here.shape[0]
    for side, (x, w) in enumerate(((xi_here, wi_here), (xt_here, wt_here))):
        moves[2 * side].wait()
        moves[2 * side + 1].wait()
        part = dot(w[...], x[...], 1, 1)
        z[side * width : (side + 1) * width] = part
        own[side * width : (side + 1) * width] = part.astype(BF16)


def score_kernel(count, own, *refs):
    blocks, out = [b[...] for b in (own,) + refs[:count]], refs[count]
    for j, other in enumerate(blocks[1:]):
        out[j * LANES : (j + 1) * LANES] = dot(other, blocks[0], 0, 0).astype(BF16)
    squares = [jnp.sum(jnp.square(b.astype(F32)), axis=0, keepdims=True) for b in blocks]
    squares = jnp.concatenate(squares + [jnp.zeros((7 - count, LANES), F32)], axis=0)
    high = squares.astype(BF16).astype(F32)
    low = (squares - high).astype(BF16).astype(F32)
    out[count * LANES :] = jnp.concatenate((high, low), axis=0).astype(BF16)


def weigh(numbers, mine, peer, others, paired, d, along, loss):
    scale, bias = numbers[0], numbers[1]

    def total(start, rows):
        a = mine[start : start + rows].astype(F32)
        return a + peer[start : start + rows].astype(F32)

    squares = total(len(others) * LANES, 16)
    inv = lax.rsqrt(squares[:8] + squares[8:] + 1e-06)
    down = inv.T
    n = inv[0:1]
    for j, other in enumerate(others):
        col = down[:, j + 1 : j + 2]
        c = scale * (total(j * LANES, LANES) * n * col)
        s = c + bias
        e = jnp.exp(-jnp.abs(s))
        g = jnp.where(s >= 0, 1.0, e) / (1.0 + e)
        signed = s
        if paired and j == 0:
            eye = (
                lax.broadcasted_iota(jnp.int32, (LANES, LANES), 0)
                == lax.broadcasted_iota(jnp.int32, (LANES, LANES), 1)
            ).astype(F32)
            signed, g = (1.0 - 2.0 * eye) * s, g - eye
        terms = (
            fine(other[...], g * col),
            jnp.sum(g * c, axis=0, keepdims=True),
            jnp.sum(jnp.maximum(signed, 0.0) + jnp.log1p(e), axis=0, keepdims=True),
        )
        if d is None:
            d, along, loss = terms
        else:
            d, along, loss = d + terms[0], along + terms[1], loss + terms[2]
    return d, along, loss, n


def near_kernel(numbers, mine, peer, o0, o1, o2, d_out, lines):
    d, along, loss, n = weigh(numbers, mine, peer, (o0, o1, o2), True, None, None, None)
    d_out[...] = d
    lines[...] = jnp.concatenate((along, loss, n, jnp.zeros((5, LANES), F32)), axis=0)


def far_kernel(numbers, mine, peer, d_in, near, o3, o4, send, keep):
    width = d_in.shape[0] // 2
    d, along, loss, _ = weigh(
        numbers, mine, peer, (o3, o4), False, d_in[...], near[0:1], near[1:2]
    )
    lines = jnp.concatenate((along, loss, near[2:8]), axis=0)
    keep[:width], send[:width] = d[:width], d[width:]
    keep[width:], send[width:] = lines, lines


def slope_kernel(numbers, keep, got, z, slopes, send, loss):
    scale, first = numbers[0], numbers[2] > 0
    width = z.shape[0] // 2
    for side in range(2):
        own, other = (keep, got) if side == 0 else (got, keep)
        lines = jnp.where(first, own[width:], other[width:])
        along, n = lines[0:1], lines[2:3]
        if side == 0:
            loss[...] = jnp.broadcast_to(lines[1:2], loss.shape)
        d = scale * jnp.where(first, own[:width], other[:width])
        part = slice(side * width, (side + 1) * width)
        terms = two_terms((d - z[part] * (n * along)) * n)
        slopes[part] = terms
        send[part] = terms[:, :LANES]


def gradient_kernel(parts, slopes, theirs, xi, xt, beside, out):
    width, count = slopes.shape[0] // 2, xi.shape[0]
    block = xi.shape[0] // parts
    whole = width // LANES * LANES
    rest = width - whole
    fold = -(-block // 32) * 16
    tail = None
    for side, x in enumerate((xi, xt)):
        there = slice(side * count, (side + 1) * count)
        feats = jnp.concatenate((x[...], x[...], beside[there]), axis=1)
        part = slice(side * width, (side + 1) * width)
        grads = jnp.concatenate((slopes[part], theirs[part]), axis=1)
        main = dot(feats, grads[:whole], 1, 1).astype(BF16)
        for j in range(whole // LANES):
            at = (side * (whole // LANES) + j) * block
            for p in range(parts):
                out[p, at : at + block] = main[p * block : (p + 1) * block, j * LANES : (j + 1) * LANES]
        piece = grads[whole:]
        gap = jnp.zeros_like(piece)
        pieces = [gap] * (2 * LANES // rest)
        pieces[side] = pieces[LANES // rest + LANES // rest // 2 + side] = piece
        term = dot(feats, jnp.concatenate(pieces, axis=0), 1, 1)
        tail = term if tail is None else tail + term
    for p in range(parts):
        upper = tail[p * block : p * block + fold, :LANES]
        lower = tail[(p + 1) * block - fold : (p + 1) * block, LANES:]
        out[p, 2 * whole // LANES * block :] = (upper + lower).astype(BF16)


def ring_order(places):
    first = 5 * places // 8
    near = [m // 2 if m % 2 == 0 else places - 1 - m // 2 for m in range(places)]
    return [first] + [m for m in near if m != first]


def ring_kernel(got, out, laid):
    total = jnp.sum(got[...].astype(F32), axis=0)
    top = jnp.max(jnp.max(jnp.abs(total), axis=0, keepdims=True), axis=1, keepdims=True)
    power = jnp.floor(jnp.log2(jnp.where(top > 0, top, 1.0))) - 13.0
    power = jnp.broadcast_to(jnp.maximum(power, -120.0), (1, LANES))
    total = total * jnp.exp2(-power)
    places = out.shape[0]
    count = total.shape[0] // places
    for j in range(count):
        laid[:, j] = total[j * places : (j + 1) * places]
    laid[:, count] = jnp.broadcast_to(power, (places, LANES))
    for at, place in enumerate(ring_order(places)):
        out[at] = laid[place]


def order_kernel(column, xi, xt, own_i, own_t, away, turned):
    places = RING // 2
    depth, size = turned.shape[0], own_i.shape[0]
    five = 5
    nine = 2 * five - 1
    planes = size // (2 * five * places)
    block = depth // (2 * planes)
    for side, x in enumerate((xi, xt)):
        turned[...] = x[...].astype(F32).T
        for beside in range(2):
            first = (column[0] + beside) % 2 * block
            for p in range(planes):
                for q in range(2):
                    for r in range(five):
                        start = first + 2 * p * block + (five - 1) * q + r
                        rows = turned[pl.ds(start, places, stride=nine)].astype(BF16)
                        at = ((2 * p + q) * five + r) * places
                        if beside:
                            away[side * size + at : side * size + at + places] = rows
                        else:
                            (own_t if side else own_i)[at : at + places] = rows


def shares(total, width, share):
    count = width // LANES
    rest = width - count * LANES
    five = 5
    fold = total[2 * count * five : 2 * count * five + five // 2 + 1]
    half = lax.axis_index("dp") % 2
    out = []
    for side in range(2):
        pieces = [total[(side * count + j) * five : (side * count + j + 1) * five] for j in range(count)]
        top = fold[:, side * rest : (side + 1) * rest]
        low = fold[1:, (2 + side) * rest : (3 + side) * rest]
        pieces.append(jnp.concatenate((top, low), axis=0))
        flat = jnp.concatenate(pieces, axis=1).reshape(1, -1)
        out.append(jnp.where(half == 0, flat[:, :share], flat[:, flat.shape[1] - share :]))
    return out


def shards(image_feats, text_feats, image_proj, text_proj, logit_scale, logit_bias):
    rows, depth = image_feats.shape
    width = image_proj.shape[1]
    dp, tower = lax.axis_size("dp"), lax.axis_size("tower")
    planes = dp // RING
    to_core = [(t, t ^ 1) for t in range(tower)]
    to_chip = [(t, t ^ 2) for t in range(tower)]
    first = lax.axis_index("tower") % 2 == 0
    core0 = first.astype(F32)
    numbers = jnp.concatenate((logit_scale, logit_bias, core0[None]))
    scalars = pl.BlockSpec(memory_space=pltpu.SMEM)
    array = pl.BlockSpec(memory_space=pltpu.VMEM)

    here = [pltpu.VMEM((rows, depth), BF16), pltpu.VMEM((width, depth), BF16)] * 2
    z, own = pl.pallas_call(
        project_kernel,
        out_shape=(
            jax.ShapeDtypeStruct((2 * width, rows), F32),
            jax.ShapeDtypeStruct((2 * width, rows), BF16),
        ),
        in_specs=[pl.BlockSpec(memory_space=pl.ANY)] * 4,
        out_specs=(array, array),
        scratch_shapes=here + [pltpu.SemaphoreType.DMA((4,))],
        compiler_params=pltpu.CompilerParams(vmem_limit_bytes=60 * 1024 * 1024),
        name="project",
    )(image_feats, image_proj.T, text_feats, text_proj.T)
    other = lax.ppermute(own, "tower", to_core)
    i0 = jnp.concatenate((own[:width], other[:width]), axis=0)
    t0 = jnp.concatenate((own[width:], other[width:]), axis=0)
    mine, o0 = jnp.where(first, i0, t0), jnp.where(first, t0, i0)
    o2 = shifted(o0, (2, -2))
    o1 = shifted(o0, (1, -1))
    o4 = shifted(o2, (2, -2))
    o3 = shifted(o1, (2, -2))
    column = (lax.axis_index("dp") // RING % 2).astype(jnp.int32)[None]
    beside = [(i, i ^ RING) for i in range(dp)]
    image_feats, text_feats, column = lax.optimization_barrier((image_feats, text_feats, column, o0))[:3]
    size = planes * 5 * (RING // 2)
    xi, xt, away = pl.pallas_call(
        order_kernel,
        out_shape=tuple(jax.ShapeDtypeStruct((n, rows), BF16) for n in (size, size, 2 * size)),
        in_specs=[scalars, array, array],
        out_specs=(array,) * 3,
        scratch_shapes=[pltpu.VMEM((depth, rows), F32)],
        compiler_params=VMEM,
        name="order",
    )(column, image_feats, text_feats)
    x_beside = lax.ppermute(away, "dp", beside)

    def scores(*blocks):
        count = len(blocks) - 1
        return pl.pallas_call(
            functools.partial(score_kernel, count),
            out_shape=jax.ShapeDtypeStruct((count * rows + 16, rows), BF16),
            in_specs=[array] * (count + 1),
            out_specs=array,
            compiler_params=VMEM,
            name="scores",
        )(*blocks)

    near = scores(mine, o0, o1, o2)
    near_peer = lax.ppermute(near, "tower", to_chip)
    near_peer, x_beside = lax.optimization_barrier((near_peer, x_beside))
    far = scores(mine, o3, o4)
    far_peer = lax.ppermute(far, "tower", to_chip)
    d, lines = pl.pallas_call(
        near_kernel,
        out_shape=(
            jax.ShapeDtypeStruct((2 * width, rows), F32),
            jax.ShapeDtypeStruct((8, rows), F32),
        ),
        in_specs=[scalars] + [array] * 5,
        out_specs=(array, array),
        compiler_params=VMEM,
        name="near",
    )(numbers, near, near_peer, o0, o1, o2)
    sums = jax.ShapeDtypeStruct((width + 8, rows), F32)
    send, keep = pl.pallas_call(
        far_kernel,
        out_shape=(sums, sums),
        in_specs=[scalars] + [array] * 6,
        out_specs=(array, array),
        compiler_params=VMEM,
        name="far",
    )(numbers, far, far_peer, d, lines, o3, o4)
    got = lax.ppermute(send, "tower", to_core)
    slopes, send, loss = pl.pallas_call(
        slope_kernel,
        out_shape=(
            jax.ShapeDtypeStruct((2 * width, 2 * rows), BF16),
            jax.ShapeDtypeStruct((2 * width, rows), BF16),
            jax.ShapeDtypeStruct((8, rows), F32),
        ),
        in_specs=[scalars] + [array] * 3,
        out_specs=(array,) * 3,
        compiler_params=VMEM,
        name="slopes",
    )(numbers, keep, got, z)
    theirs = lax.ppermute(send, "dp", beside)
    parts = planes
    block = xi.shape[0] // parts
    payload = 2 * (width // LANES) * block + -(-block // 32) * 16
    grads = pl.pallas_call(
        functools.partial(gradient_kernel, parts),
        out_shape=jax.ShapeDtypeStruct((parts, payload, LANES), BF16),
        in_specs=[array] * 5,
        out_specs=array,
        compiler_params=VMEM,
        name="gradients",
    )(slopes, theirs, xi, xt, x_beside)

    places = RING // 2
    groups = [
        [(2 * y + x) * RING + 2 * m + q for y in range(planes // 2) for q in range(2)]
        for x in range(2)
        for m in range(places)
    ]
    grads = lax.all_to_all(grads, "dp", 0, 0, axis_index_groups=groups, tiled=True)
    sent = pl.pallas_call(
        ring_kernel,
        out_shape=jax.ShapeDtypeStruct((places, payload // places + 1, LANES), F32),
        in_specs=[array],
        out_specs=array,
        scratch_shapes=[pltpu.VMEM((places, payload // places + 1, LANES), F32)],
        compiler_params=VMEM,
        name="ring",
    )(grads)
    groups = [
        [g * RING + 2 * m + q for m in ring_order(places)] for g in range(planes) for q in range(2)
    ]
    sent = sent.astype(jnp.float16)
    back = lax.all_to_all(sent, "dp", 0, 0, axis_index_groups=groups, tiled=True).astype(F32)
    total = jnp.sum(back * jnp.exp2(back[:, -1:]), axis=0)
    image_grad, text_grad = shares(total, width, depth * width // dp)
    return (loss[0], image_grad, text_grad)


def solution(mesh):
    in_specs = (P("dp", None), P("dp", None), P(None, "tower"), P(None, "tower"), P(), P())
    out_specs = (P("dp"), P("tower", "dp"), P("tower", "dp"))
    return jax.shard_map(shards, mesh=mesh, in_specs=in_specs, out_specs=out_specs, check_vma=False)
```
